32 devices in a mesh: wide: 8 (over y, x, core), narrow: 4 (over z).
Axes of the slice: x: 2, y: 2, z: 4, core: 2. Of those that a mesh axis runs over, the one named last changes fastest.
Arguments:
- vectors: float32 [32000, 8192], P('wide', 'narrow'), may hold values from -0.44860464 to 0.44860464
- reflectors: float32 [32000, 256], P('wide'), may hold values from -6 to 6
- triangle: float32 [256, 256], replicated, may hold values from -3.125e-05 to 7.8125e-05, as said below
- energies: float32 [32000], P('wide'), may hold values from -1 to 1
Outputs:
- updated: float32 [32000, 8192], P('wide', 'narrow')
- fock_block: float32 [8192, 512], P(('narrow', 'wide'))
The draws below stay inside these ranges and needn't reach their ends.
Inputs may be any that keep to these rules, and one draw needn't show every extreme that they name: `triangle`: upper triangular, with diagonal entries between 1.5 / 32000 and 2.5 / 32000 and entries above the diagonal of magnitude at most 1 / 32000.
All inputs are finite; a program needn't handle non-finite values.
Results may differ from the reference program's by a relative error of at most 0.00007.
Values sent between devices are 32-bit elements; how exact they have to be, the bound alone decides.
No kernel may reach another device: no remote copies, remote signals or barrier semaphores. Data moves between devices by JAX's collectives and lax.ppermute only.
A program may use at most 128 MiB of HBM per device.

```python
import math
import jax
import jax.numpy as jnp
from jax import lax

NV = 32000
NK = 8192
NB = 256
FB = 512
OFF = 256
N_NARROW = 4


def draw_triangle(key, part):
    key_one, key_two = jax.random.split(key, 2)
    diagonal_part = jax.random.uniform(key_one, (NB,), jnp.float32, 1.5, 2.5)
    upper_part = jnp.clip(jax.random.normal(key_two, (NB, NB), jnp.float32), -4.0, 4.0) * (0.5 / math.sqrt(NB))
    matrix = jnp.triu(upper_part, 1) + jnp.diag(diagonal_part)
    return matrix * (1.0 / NV)


def levels(key, dims, pieces, smallest, top_value):
    level, own = 1.0, jax.random.fold_in(key, 6)
    for position, blocks in pieces:
        heights = jnp.exp(jax.random.uniform(jax.random.fold_in(own, position), (blocks,), jnp.float32, smallest / len(pieces), top_value / len(pieces)))
        level = level * jnp.repeat(heights, dims[position] // blocks).reshape([-1 if axis == position else 1 for axis in range(len(dims))])
    return level


def centred(key, dims, spread, bound, cuts=(), held_as=jnp.bfloat16):
    entries = spread * jax.random.normal(key, dims, jnp.float32)
    if cuts:
        entries = entries * levels(key, dims, cuts, -0.22, 0.18)
    return jnp.clip(entries, -bound, bound).astype(held_as)


def setup_inputs(seed: int = 0) -> dict:
    keys = jax.random.split(jax.random.key(seed), 5)
    return {
        "vectors": centred(keys[0], (NV, NK), (NV ** -0.25), 0.44860464, ((0, 8), (1, 4)), jnp.float32),
        "reflectors": centred(keys[1], (NV, NB), 1.0, 6.0, ((0, 8),), jnp.float32),
        "triangle": draw_triangle(jax.random.fold_in(keys[4], 71), 0),
        "energies": jnp.clip(jax.random.uniform(keys[3], (NV,), jnp.float32, -1.0, 1.0) * levels(keys[3], (NV,), ((0, 8),), -0.4, 0.0), -1.0, 1.0),
    }


def reference(vectors, reflectors, triangle, energies):
    highest = lax.Precision.HIGHEST
    projected = jnp.dot(reflectors.T, vectors, precision=highest, preferred_element_type=jnp.float32)
    coefficients = jnp.dot(triangle, projected, precision=highest, preferred_element_type=jnp.float32)
    updated = vectors - jnp.dot(reflectors, coefficients, precision=highest, preferred_element_type=jnp.float32)
    columns = NK // N_NARROW
    block_width = FB // N_NARROW
    fock_input = updated.reshape(NV, N_NARROW, columns)[:, :, OFF:OFF + block_width].reshape(NV, FB)
    fock_block = jnp.dot(updated.T, energies[:, None] * fock_input, precision=highest, preferred_element_type=jnp.float32)
    return updated, fock_block
```

```python
import jax
import jax.numpy as jnp
from jax import lax
from jax.sharding import PartitionSpec as P

FB = 512
OFF = 256
CHUNKS = 2

ROWS = (((0,), (0,)), ((), ()))
LAST = (((1,), (1,)), ((), ()))


def dot(left, right, dims):
    return lax.dot_general(
        left, right, dims, precision=lax.Precision.HIGH, preferred_element_type=jnp.float32
    )


def arrivals(n):
    order = []
    for z in range(n):
        found = [(hops, 0) for hops in range(1, n) if z + hops < n]
        found += [(hops, 1) for hops in range(1, n) if z - hops >= 0]
        order.append(sorted(found))
    return [[order[z][slot] for z in range(n)] for slot in range(n - 1)]


def exchange(block, n):
    came = {}
    for direction in (0, 1):
        held = block
        for hops in range(1, n):
            if direction == 0:
                pairs = [(z, z - 1) for z in range(1, n - hops + 1)]
            else:
                pairs = [(z, z + 1) for z in range(hops - 1, n - 1)]
            held = lax.ppermute(held, "narrow", pairs)
            came[(hops, direction)] = held
    return came


def pick(came, places, z):
    choices = sorted(set(places))
    value = came[choices[0]]
    for choice in choices[1:]:
        here = [p for p, place in enumerate(places) if place == choice]
        mine = z == here[0]
        for p in here[1:]:
            mine = mine | (z == p)
        value = jnp.where(mine, came[choice], value)
    return value


def source(places, z):
    value = jnp.int32(0)
    for p, (hops, direction) in enumerate(places):
        value = jnp.where(z == p, p - hops if direction else p + hops, value)
    return value


def on_device(vectors, reflectors, triangle, energies):
    n = lax.axis_size("narrow")
    wide = lax.axis_size("wide")
    z = lax.axis_index("narrow")
    block_width = FB // n
    rows = vectors.shape[0]
    step = rows // CHUNKS
    scaled_rows = energies[:, None]

    raw = vectors[:, OFF : OFF + block_width]
    scaled = scaled_rows * raw
    chunks = [scaled[c * step : (c + 1) * step] for c in range(CHUNKS)]
    came = [exchange(chunk, n) for chunk in chunks]

    own = lax.psum_scatter(dot(raw, reflectors, ROWS), "wide", scatter_dimension=0, tiled=True)
    coef_block = lax.all_gather(
        dot(own, triangle, LAST), ("narrow", "wide"), axis=0, tiled=True
    )

    projected = lax.psum_scatter(
        dot(vectors, reflectors, ROWS), "wide", scatter_dimension=0, tiled=True
    )
    coefficients = lax.all_gather(dot(projected, triangle, LAST), "wide", axis=0, tiled=True)
    updated = vectors - dot(reflectors, coefficients, LAST)

    def fixed(block, start, first, count):
        coef = lax.dynamic_slice_in_dim(coef_block, start * block_width, block_width, 0)
        part = slice(first, first + count)
        return block - scaled_rows[part] * dot(reflectors[part], coef, LAST)

    table = arrivals(n)
    sources = [z] + [source(places, z) for places in table]

    def scatter(part):
        return lax.psum_scatter(part, "wide", scatter_dimension=0, tiled=True)

    pieces = []
    for slot in range(n):
        if slot == 0:
            total = dot(updated, fixed(scaled, z, 0, rows), ROWS)
        elif slot < n - 1:
            block = jnp.concatenate([pick(c, table[slot - 1], z) for c in came], axis=0)
            total = dot(updated, fixed(block, sources[slot], 0, rows), ROWS)
        else:
            total = None
            for c in range(CHUNKS):
                block = fixed(pick(came[c], table[slot - 1], z), sources[slot], c * step, step)
                term = dot(updated[c * step : (c + 1) * step], block, ROWS)
                total = term if total is None else total + term
        pieces.append(scatter(total))
    fock_block = jnp.zeros((pieces[0].shape[0], FB), jnp.float32)
    for start, piece in zip(sources, pieces):
        fock_block = lax.dynamic_update_slice_in_dim(fock_block, piece, start * block_width, 1)
    return (updated, fock_block)


def solution(mesh):
    return jax.shard_map(
        on_device,
        mesh=mesh,
        in_specs=(P("wide", "narrow"), P("wide", None), P(), P("wide")),
        out_specs=(P("wide", "narrow"), P(("narrow", "wide"), None)),
        check_vma=False,
    )
```

```python
import functools

import jax
import jax.numpy as jnp
from jax import lax
from jax.experimental import pallas as pl
from jax.experimental.pallas import tpu as pltpu
from jax.sharding import PartitionSpec as P

FB = 512
OFF = 256
CHUNKS = 1
VMEM = 56 * 1024 * 1024

F32 = jnp.float32
BF16 = jnp.bfloat16
LONG = pl.CostEstimate(flops=10**11, bytes_accessed=1024, transcendentals=0)
SHORT = pl.CostEstimate(flops=1024, bytes_accessed=1024, transcendentals=0)


def split(x):
    high = x.astype(BF16)
    return high, (x - high.astype(F32)).astype(BF16)


def mul(left, right):
    return jnp.dot(left, right, preferred_element_type=F32)


def three(left, right):
    (lh, ll), (rh, rl) = left, right
    return mul(lh, rh) + mul(ll, rh) + mul(lh, rl)


def stacked(both, high, right):
    rh, rl = right
    m = high.shape[0]
    top = mul(both, rh)
    return top[:m] + top[m:] + mul(high, rl)


def params():
    return pltpu.CompilerParams(
        dimension_semantics=("arbitrary",), vmem_limit_bytes=VMEM
    )


def width(columns, wide):
    return 256 if columns % 256 == 0 and 256 % (columns // wide) == 0 else columns // wide


def whole(shape):
    return pl.BlockSpec(shape, lambda j, *_: (0,) * len(shape), pipeline_mode=pl.Buffered(1))


ANY = pl.BlockSpec(memory_space=pl.ANY)


def gate_kernel(*refs):
    del refs


def gate(held, *others, cost=SHORT):
    count = len(held)
    return pl.pallas_call(
        gate_kernel,
        in_specs=[ANY] * (count + len(others)),
        out_specs=[ANY] * count,
        out_shape=[jax.ShapeDtypeStruct(x.shape, x.dtype) for x in held],
        input_output_aliases={k: k for k in range(count)},
        cost_estimate=cost,
        name="gate",
    )(*held, *others)


def place(value, index, even_ref, odd_ref):
    half = index // 2

    @pl.when(index % 2 == 0)
    def _():
        even_ref[half] = value

    @pl.when(index % 2 == 1)
    def _():
        odd_ref[half] = value


def take(index, even_ref, odd_ref):
    half = index // 2
    return jnp.where(index % 2 == 0, even_ref[half], odd_ref[half])


def own_kernel(block_width, v_ref, r_ref, out_ref):
    out_ref[...] = three(split(v_ref[:, :block_width].T), split(r_ref[...]))


def own_columns(vectors, reflectors, block_width):
    rows, nb = reflectors.shape
    taken = max(block_width, 128)
    return pl.pallas_call(
        functools.partial(own_kernel, block_width),
        grid=(1,),
        in_specs=[pl.BlockSpec((rows, taken), lambda j: (0, OFF // taken)), whole((rows, nb))],
        out_specs=whole((block_width, nb)),
        out_shape=jax.ShapeDtypeStruct((block_width, nb), F32),
        compiler_params=params(),
        cost_estimate=SHORT,
        name="own",
    )(vectors, reflectors)


def project_kernel(per, me_ref, v_ref, r_ref, after_ref, even_ref, odd_ref, token_ref, both_ref):
    j = pl.program_id(0)
    nb = r_ref.shape[1]

    @pl.when(j == 0)
    def _():
        high, low = split(r_ref[...].T)
        both_ref[:nb] = high
        both_ref[nb:] = low
        token_ref[...] = jnp.zeros_like(token_ref)

    value = stacked(both_ref[...], both_ref[:nb], split(v_ref[...]))
    step = v_ref.shape[1]
    for g in range(step // per):
        w = j * (step // per) + g
        place(value[:, g * per : (g + 1) * per], w ^ me_ref[0], even_ref, odd_ref)


def project(me, vectors, reflectors, after, wide):
    rows, columns = vectors.shape
    nb = reflectors.shape[1]
    per = columns // wide
    step = width(columns, wide)
    half = jax.ShapeDtypeStruct((wide // 2, nb, per), F32)
    return pl.pallas_call(
        functools.partial(project_kernel, per),
        grid_spec=pltpu.PrefetchScalarGridSpec(
            num_scalar_prefetch=1,
            grid=(columns // step,),
            in_specs=[pl.BlockSpec((rows, step), lambda j, *_: (0, j)), whole((rows, nb)), ANY],
            out_specs=[whole(half.shape), whole(half.shape), whole((8, 128))],
            scratch_shapes=[pltpu.VMEM((2 * nb, rows), BF16)],
        ),
        out_shape=[half, half, jax.ShapeDtypeStruct((8, 128), F32)],
        compiler_params=params(),
        cost_estimate=SHORT,
        name="project",
    )(me, vectors, reflectors, after)


def gather(choice, groups, block_ref):
    first = 0
    for group in groups:
        rows = group[0].shape[0]
        for k, ref in enumerate(group):

            @pl.when(choice == k)
            def _(ref=ref, first=first, rows=rows):
                pltpu.sync_copy(ref, block_ref.at[pl.ds(first, rows)])

        first += rows


def early_kernel(per, groups, me_ref, v_ref, r_ref, e_ref, after_ref, *refs):
    out_ref, small_ref, both_ref, *block = refs[-3 - bool(groups) :]
    j = pl.program_id(0)
    m = both_ref.shape[0] // 2

    @pl.when(j == 0)
    def _():
        if groups:
            gather(me_ref[1], regroup(refs, groups), block[0])
            x = block[0][...].T
        else:
            x = r_ref[...].T * e_ref[...]
        high, low = split(x)
        both_ref[:m] = high
        both_ref[m:] = low
        small_ref[...] = stacked(both_ref[...], both_ref[:m], split(r_ref[...]))

    value = stacked(both_ref[...], both_ref[:m], split(v_ref[...]))
    for g in range(v_ref.shape[1] // per):
        out_ref[g] = value[:, g * per : (g + 1) * per]


def regroup(refs, groups):
    refs = list(refs)
    return [[refs.pop(0) for _ in range(count)] for count in groups]


def early(me, vectors, reflectors, e_row, chosen, wide, after):
    rows, columns = vectors.shape
    nb = reflectors.shape[1]
    per = columns // wide
    step = width(columns, wide)
    flat = [x for group in chosen for x in group]
    m = flat[0].shape[1] if flat else nb
    scratch = [pltpu.VMEM((2 * m, rows), BF16)]
    if flat:
        scratch.append(pltpu.VMEM((rows, m), F32))
    return pl.pallas_call(
        functools.partial(early_kernel, per, [len(group) for group in chosen]),
        grid_spec=pltpu.PrefetchScalarGridSpec(
            num_scalar_prefetch=1,
            grid=(columns // step,),
            in_specs=[
                pl.BlockSpec((rows, step), lambda j, *_: (0, j)),
                whole((rows, nb)),
                whole((1, rows)),
                ANY,
            ]
            + [ANY] * len(flat),
            out_specs=[
                pl.BlockSpec((step // per, m, per), lambda j, *_: (j, 0, 0)),
                whole((m, nb)),
            ],
            scratch_shapes=scratch,
        ),
        out_shape=[
            jax.ShapeDtypeStruct((wide, m, per), F32),
            jax.ShapeDtypeStruct((m, nb), F32),
        ],
        compiler_params=params(),
        cost_estimate=SHORT,
        name="early",
    )(me, vectors, reflectors, e_row, after, *flat)


def finish_kernel(me_ref, even_ref, odd_ref, *refs):
    *refs, out_ref = refs
    w = pl.program_id(0)
    c = split(take(w ^ me_ref[0], even_ref, odd_ref))
    first = 0
    for a_ref, d_ref in zip(refs[::2], refs[1::2]):
        m = a_ref.shape[1]
        out_ref[0, first : first + m] = a_ref[0] - three(split(d_ref[...]), c)
        first += m


def finish(me, even, odd, *parts):
    wide, _, per = parts[0].shape
    m = sum(part.shape[1] for part in parts[::2])
    specs = []
    for a, d in zip(parts[::2], parts[1::2]):
        specs += [pl.BlockSpec((1, *a.shape[1:]), lambda w, *_: (w, 0, 0)), whole(d.shape)]
    return pl.pallas_call(
        finish_kernel,
        grid_spec=pltpu.PrefetchScalarGridSpec(
            num_scalar_prefetch=1,
            grid=(wide,),
            in_specs=[whole(even.shape), whole(odd.shape)] + specs,
            out_specs=pl.BlockSpec((1, m, per), lambda w, *_: (w, 0, 0)),
        ),
        out_shape=jax.ShapeDtypeStruct((wide, m, per), F32),
        compiler_params=params(),
        cost_estimate=SHORT,
        name="finish",
    )(me, even, odd, *parts)


def update_kernel(per, me_ref, v_ref, r_ref, even_ref, odd_ref, after_ref, out_ref, rh_ref, rl_ref):
    j = pl.program_id(0)

    @pl.when(j == 0)
    def _():
        rh_ref[...], rl_ref[...] = split(r_ref[...])

    count = v_ref.shape[1] // per
    blocks = [take((j * count + g) ^ me_ref[0], even_ref, odd_ref) for g in range(count)]
    c = blocks[0] if count == 1 else jnp.concatenate(blocks, axis=1)
    out_ref[...] = v_ref[...] - three((rh_ref[...], rl_ref[...]), split(c))


def update(me, vectors, reflectors, even, odd, after, wide):
    rows, columns = vectors.shape
    nb = reflectors.shape[1]
    per = columns // wide
    step = width(columns, wide)
    return pl.pallas_call(
        functools.partial(update_kernel, per),
        grid_spec=pltpu.PrefetchScalarGridSpec(
            num_scalar_prefetch=1,
            grid=(columns // step,),
            in_specs=[
                pl.BlockSpec((rows, step), lambda j, *_: (0, j)),
                whole((rows, nb)),
                whole(even.shape),
                whole(odd.shape),
                ANY,
            ],
            out_specs=pl.BlockSpec((rows, step), lambda j, *_: (0, j)),
            scratch_shapes=[pltpu.VMEM((rows, nb), BF16), pltpu.VMEM((rows, nb), BF16)],
        ),
        out_shape=jax.ShapeDtypeStruct(vectors.shape, F32),
        compiler_params=params(),
        cost_estimate=SHORT,
        name="update",
    )(me, vectors, reflectors, even, odd, after)


def late_kernel(per, relative, groups, *refs):
    me_ref, v_ref, r_ref, even_ref, odd_ref, before_ref, dbefore_ref, _, *refs = refs
    *outs, both_ref, small_ref, block_ref = refs[sum(groups) :]
    j = pl.program_id(0)
    m = block_ref.shape[1]

    @pl.when(j == 0)
    def _():
        gather(me_ref[1], regroup(refs, groups), block_ref)
        high, low = split(block_ref[...].T)
        both_ref[:m] = high
        both_ref[m:] = low
        small_ref[...] = dbefore_ref[...] + stacked(
            both_ref[...], both_ref[:m], split(r_ref[...])
        )

    value = stacked(both_ref[...], both_ref[:m], split(v_ref[...]))
    small = split(small_ref[...])
    count = v_ref.shape[1] // per
    for g in range(count):
        index = (j * count + g) ^ me_ref[0]
        c = split(take(index, even_ref, odd_ref))
        part = before_ref[g] + value[:, g * per : (g + 1) * per] - three(small, c)
        if relative:
            place(part, index, *outs)
        else:
            outs[0][g] = part


def late(me, vectors, reflectors, chosen, even, odd, before, dbefore, after, chunk, wide, relative):
    columns = vectors.shape[1]
    rows = sum(group[0].shape[0] for group in chosen)
    m = chosen[0][0].shape[1]
    flat = [x for group in chosen for x in group]
    nb = reflectors.shape[1]
    per = columns // wide
    step = width(columns, wide)
    count = step // per
    if relative:
        half = jax.ShapeDtypeStruct((wide // 2, m, per), F32)
        out_shape, out_specs = [half, half], [whole(half.shape)] * 2
    else:
        out_shape = [jax.ShapeDtypeStruct((wide, m, per), F32)]
        out_specs = [pl.BlockSpec((count, m, per), lambda j, *_: (j, 0, 0))]
    return pl.pallas_call(
        functools.partial(late_kernel, per, relative, [len(group) for group in chosen]),
        grid_spec=pltpu.PrefetchScalarGridSpec(
            num_scalar_prefetch=1,
            grid=(columns // step,),
            in_specs=[
                pl.BlockSpec((rows, step), lambda j, *_: (chunk, j)),
                pl.BlockSpec((rows, nb), lambda j, *_: (chunk, 0)),
                whole(even.shape),
                whole(odd.shape),
                pl.BlockSpec((count, m, per), lambda j, *_: (j, 0, 0)),
                whole((m, nb)),
                ANY,
            ]
            + [ANY] * len(flat),
            out_specs=out_specs,
            scratch_shapes=[
                pltpu.VMEM((2 * m, rows), BF16),
                pltpu.VMEM((m, nb), F32),
                pltpu.VMEM((rows, m), F32),
            ],
        ),
        out_shape=out_shape,
        compiler_params=params(),
        cost_estimate=SHORT,
        name="late",
    )(me, vectors, reflectors, even, odd, before, dbefore, after, *flat)


def last_kernel(block_width, n_early, groups, source_ref, y_ref, coef_ref, *refs):
    *refs, out_ref, scratch_ref = refs
    nb = coef_ref.shape[1]
    pieces = [y_ref[nb + s * block_width : nb + (s + 1) * block_width] for s in range(n_early)]
    pieces += [
        functools.reduce(jnp.add, [ref[...] for ref in group]) for group in regroup(refs, groups)
    ]
    for slot, piece in enumerate(pieces):
        first = pl.multiple_of(source_ref[slot] * block_width, block_width)
        scratch_ref[pl.ds(first, block_width), :] = piece
    taken = three(split(coef_ref[...]), split(y_ref[:nb]))
    out_ref[...] = (scratch_ref[...] - taken).T


def last(sources, ready, coef_block, terms, block_width, n_early):
    per = ready.shape[1]
    operands = [ready, coef_block] + [x for group in terms for x in group]
    return pl.pallas_call(
        functools.partial(last_kernel, block_width, n_early, [len(group) for group in terms]),
        grid_spec=pltpu.PrefetchScalarGridSpec(
            num_scalar_prefetch=1,
            grid=(1,),
            in_specs=[whole(x.shape) for x in operands],
            out_specs=whole((per, FB)),
            scratch_shapes=[pltpu.VMEM((FB, per), F32)],
        ),
        out_shape=jax.ShapeDtypeStruct((per, FB), F32),
        compiler_params=params(),
        cost_estimate=SHORT,
        name="last",
    )(sources, *operands)


def arrivals(n):
    order = []
    for z in range(n):
        found = [(hops, 0) for hops in range(1, n) if z + hops < n]
        found += [(hops, 1) for hops in range(1, n) if z - hops >= 0]
        order.append(sorted(found))
    return [[order[z][slot] for z in range(n)] for slot in range(n - 1)]


def exchange(blocks, n):
    came = {}
    held = [list(blocks), list(blocks)]
    for hops in range(1, n):
        pairs = [
            [(z, z - 1) for z in range(1, n - hops + 1)],
            [(z, z + 1) for z in range(hops - 1, n - 1)],
        ]
        held = [[lax.ppermute(x, "narrow", pairs[d]) for x in held[d]] for d in (0, 1)]
        if hops < n - 1:
            count = len(blocks)
            both = gate(held[0] + held[1], cost=LONG)
            held = [both[:count], both[count:]]
        for d in (0, 1):
            came[(hops, d)] = held[d]
    return came


def options(came, places, z):
    choices = sorted(set(places))
    which = jnp.int32(0)
    for p, place in enumerate(places):
        which = jnp.where(z == p, choices.index(place), which)
    return [[came[choice][c] for choice in choices] for c in range(CHUNKS)], which


def source(places, z):
    value = jnp.int32(0)
    for p, (hops, direction) in enumerate(places):
        value = jnp.where(z == p, p - hops if direction else p + hops, value)
    return value


def swap(x, wide, distance):
    return lax.ppermute(x, "wide", [(i, i ^ distance) for i in range(wide)])


def scatter_terms(even, odd, wide):
    other = swap(odd, wide, 1)
    sums = [even[h] + other[h] for h in range(wide // 2)]
    return [sums[0]] + [swap(sums[h], wide, 2 * h) for h in range(1, wide // 2)]


def on_device(vectors, reflectors, triangle, energies):
    n = lax.axis_size("narrow")
    wide = lax.axis_size("wide")
    z = lax.axis_index("narrow")
    me = lax.axis_index("wide").astype(jnp.int32).reshape(1)
    block_width = FB // n
    rows, columns = vectors.shape
    nb = reflectors.shape[1]
    step = rows // CHUNKS
    e_row = energies.reshape(1, rows)

    chunks = [
        energies[c * step : (c + 1) * step, None]
        * vectors[c * step : (c + 1) * step, OFF : OFF + block_width]
        for c in range(CHUNKS)
    ]
    came = exchange(chunks, n)
    table = arrivals(n)
    sources = jnp.stack([z.astype(jnp.int32)] + [source(places, z) for places in table])

    own = own_columns(vectors, reflectors, block_width)
    even, odd, token = project(me, vectors, reflectors, own, wide)

    part = lax.psum_scatter(own, "wide", scatter_dimension=0, tiled=True)
    share = lax.dot_general(
        part, triangle, (((1,), (1,)), ((), ())), precision=lax.Precision.HIGHEST
    )
    shares = lax.all_gather(share, "narrow", axis=0)
    coef_block = lax.all_gather(shares, "wide", axis=1).reshape(FB, nb)

    def with_choice(which):
        return jnp.stack([me[0], which.astype(jnp.int32)])

    none = with_choice(jnp.int32(0))
    y, dy = early(none, vectors, reflectors, e_row, [], wide, token)
    a, da = early(none, vectors, reflectors, e_row, [[chunk] for chunk in chunks], wide, dy)

    (odd,) = gate([odd], da, part, *came[(1, 0)], *came[(1, 1)])
    terms = scatter_terms(even, odd, wide)
    chosen, which = options(came, table[0], z)
    b, db = early(with_choice(which), vectors, reflectors, e_row, chosen, wide, da)
    terms[0] = gate(terms[:1], db)[0]
    projected = functools.reduce(jnp.add, terms)
    coefficients = jnp.dot(triangle, projected, precision=lax.Precision.HIGHEST)
    c_even = jnp.stack(
        [coefficients] + [swap(coefficients, wide, 2 * h) for h in range(1, wide // 2)]
    )
    c_odd = swap(c_even, wide, 1)

    (db,) = gate([db], cost=LONG)
    (db,) = gate([db], shares)
    first = finish(me, c_even, c_odd, y, dy, a, da, b, db)
    ready = lax.psum_scatter(first, "wide", scatter_dimension=0)

    zero = jnp.zeros((wide, block_width, columns // wide), F32)
    small_zero = jnp.zeros((block_width, nb), F32)
    mids, done = [], first
    for slot in range(1, n - 2):
        chosen, which = options(came, table[slot], z)
        halves = late(
            with_choice(which), vectors, reflectors, chosen, c_even, c_odd, zero, small_zero,
            done, 0, wide, True,
        )
        mids.append(scatter_terms(*halves, wide))
        done = halves[0]
    updated = update(me, vectors, reflectors, c_even, c_odd, done, wide)

    total = zero
    chosen, which = options(came, table[n - 2], z)
    for c in range(CHUNKS):
        out = late(
            with_choice(which), vectors, reflectors, chosen[c : c + 1], c_even, c_odd, total,
            small_zero, updated, c, wide, c == CHUNKS - 1,
        )
        total = out[0]
    tail = scatter_terms(*out, wide)
    fock_block = last(sources, ready, coef_block, mids + [tail], block_width, 2)
    return (updated, fock_block)


def solution(mesh):
    return jax.shard_map(
        on_device,
        mesh=mesh,
        in_specs=(P("wide", "narrow"), P("wide", None), P(), P("wide")),
        out_specs=(P("wide", "narrow"), P(("narrow", "wide"), None)),
        check_vma=False,
    )
```

```python
import functools

import jax
import jax.numpy as jnp
from jax import lax
from jax.experimental import pallas as pl
from jax.experimental.pallas import tpu as pltpu
from jax.sharding import PartitionSpec as P

FB = 512
OFF = 256
CHUNKS = 1
VMEM = 56 * 1024 * 1024

F32 = jnp.float32
BF16 = jnp.bfloat16
LONG = pl.CostEstimate(flops=10**11, bytes_accessed=1024, transcendentals=0)
SHORT = pl.CostEstimate(flops=1024, bytes_accessed=1024, transcendentals=0)


def split(x):
    high = x.astype(BF16)
    return high, (x - high.astype(F32)).astype(BF16)


def mul(left, right):
    return jnp.dot(left, right, preferred_element_type=F32)


def three(left, right):
    (lh, ll), (rh, rl) = left, right
    return mul(lh, rh) + mul(ll, rh) + mul(lh, rl)


def stacked(both, high, right):
    rh, rl = right
    m = high.shape[0]
    top = mul(both, rh)
    return top[:m] + top[m:] + mul(high, rl)


def params():
    return pltpu.CompilerParams(
        dimension_semantics=("arbitrary",), vmem_limit_bytes=VMEM
    )


def width(columns, wide):
    return 256 if columns % 256 == 0 and 256 % (columns // wide) == 0 else columns // wide


def whole(shape):
    return pl.BlockSpec(shape, lambda j, *_: (0,) * len(shape), pipeline_mode=pl.Buffered(1))


ANY = pl.BlockSpec(memory_space=pl.ANY)


def gate_kernel(*refs):
    del refs


def gate(held, *others, cost=SHORT):
    count = len(held)
    return pl.pallas_call(
        gate_kernel,
        in_specs=[ANY] * (count + len(others)),
        out_specs=[ANY] * count,
        out_shape=[jax.ShapeDtypeStruct(x.shape, x.dtype) for x in held],
        input_output_aliases={k: k for k in range(count)},
        cost_estimate=cost,
        name="gate",
    )(*held, *others)


def place(value, index, even_ref, odd_ref):
    half = index // 2

    @pl.when(index % 2 == 0)
    def _():
        even_ref[half] = value

    @pl.when(index % 2 == 1)
    def _():
        odd_ref[half] = value


def take(index, even_ref, odd_ref):
    half = index // 2
    return jnp.where(index % 2 == 0, even_ref[half], odd_ref[half])


def first_kernel(per, me_ref, v_ref, r_ref, e_ref, x_ref, even_ref, odd_ref, out_ref, small_ref, both_ref):
    j = pl.program_id(0)
    nb = r_ref.shape[1]
    m = both_ref.shape[0] // 2

    @pl.when(j == 0)
    def _():
        turned = r_ref[...].T
        parts = [turned, turned * e_ref[...], x_ref[...].T]
        first = 0
        for part in parts:
            size = part.shape[0]
            both_ref[first : first + size], both_ref[m + first : m + first + size] = split(part)
            first += size
        small_ref[...] = three((both_ref[nb:m], both_ref[m + nb :]), split(r_ref[...]))

    value = stacked(both_ref[...], both_ref[:m], split(v_ref[...]))
    step = v_ref.shape[1]
    for g in range(step // per):
        w = j * (step // per) + g
        part = value[:, g * per : (g + 1) * per]
        place(part[:nb], w ^ me_ref[0], even_ref, odd_ref)
        out_ref[g] = part[nb:]


def first_pass(me, vectors, reflectors, e_row, block, wide):
    rows, columns = vectors.shape
    nb = reflectors.shape[1]
    per = columns // wide
    step = width(columns, wide)
    k = nb + block.shape[1]
    half = jax.ShapeDtypeStruct((wide // 2, nb, per), F32)
    return pl.pallas_call(
        functools.partial(first_kernel, per),
        grid_spec=pltpu.PrefetchScalarGridSpec(
            num_scalar_prefetch=1,
            grid=(columns // step,),
            in_specs=[
                pl.BlockSpec((rows, step), lambda j, *_: (0, j)),
                whole((rows, nb)),
                whole((1, rows)),
                whole(block.shape),
            ],
            out_specs=[
                whole(half.shape),
                whole(half.shape),
                pl.BlockSpec((step // per, k, per), lambda j, *_: (j, 0, 0)),
                whole((k, nb)),
            ],
            scratch_shapes=[pltpu.VMEM((2 * (nb + k), rows), BF16)],
        ),
        out_shape=[
            half,
            half,
            jax.ShapeDtypeStruct((wide, k, per), F32),
            jax.ShapeDtypeStruct((k, nb), F32),
        ],
        compiler_params=params(),
        cost_estimate=SHORT,
        name="first_pass",
    )(me, vectors, reflectors, e_row, block)


def update_kernel(per, offset, me_ref, v_ref, r_ref, even_ref, odd_ref, *refs):
    out_ref, token_ref, left_ref = refs[-3:]
    j = pl.program_id(0)
    nb = r_ref.shape[1]

    @pl.when(j == 0)
    def _():
        token_ref[...] = jnp.zeros_like(token_ref)
        high, low = split(r_ref[...])
        left_ref[:, :nb] = high
        left_ref[:, nb : 2 * nb] = low
        left_ref[:, 2 * nb :] = high

    count = v_ref.shape[1] // per
    blocks = [take(((j + offset) * count + g) ^ me_ref[0], even_ref, odd_ref) for g in range(count)]
    high, low = split(blocks[0] if count == 1 else jnp.concatenate(blocks, axis=1))
    right = jnp.concatenate([high, high, low], axis=0)
    out_ref[...] = v_ref[...] - mul(left_ref[...], right)


def update(me, vectors, reflectors, even, odd, wide, offset, blocks, after, before):
    rows, columns = vectors.shape
    nb = reflectors.shape[1]
    per = columns // wide
    step = width(columns, wide)
    operands = [me, vectors, reflectors, even, odd, *after]
    aliases = {}
    if before is not None:
        aliases = {len(operands): 0}
        operands.append(before)
    columns_of = pl.BlockSpec((rows, step), lambda j, *_: (0, j + offset))
    return pl.pallas_call(
        functools.partial(update_kernel, per, offset),
        grid_spec=pltpu.PrefetchScalarGridSpec(
            num_scalar_prefetch=1,
            grid=(blocks,),
            in_specs=[columns_of, whole((rows, nb)), whole(even.shape), whole(odd.shape)]
            + [ANY] * (len(operands) - 5),
            out_specs=[columns_of, whole((8, 128))],
            scratch_shapes=[pltpu.VMEM((rows, 3 * nb), BF16)],
        ),
        out_shape=[
            jax.ShapeDtypeStruct(vectors.shape, F32),
            jax.ShapeDtypeStruct((8, 128), F32),
        ],
        input_output_aliases=aliases,
        compiler_params=params(),
        cost_estimate=SHORT,
        name="update",
    )(*operands)


def gather(choice, groups, block_ref):
    first = 0
    for group in groups:
        rows = group[0].shape[0]
        for k, ref in enumerate(group):

            @pl.when(choice == k)
            def _(ref=ref, first=first, rows=rows):
                pltpu.sync_copy(ref, block_ref.at[pl.ds(first, rows)])

        first += rows


def regroup(refs, groups):
    refs = list(refs)
    return [[refs.pop(0) for _ in range(count)] for count in groups]


def late_kernel(per, slots, me_ref, v_ref, r_ref, even_ref, odd_ref, after_ref, *refs):
    *refs, even_out, odd_out, both_ref, small_ref, block_ref = refs
    j = pl.program_id(0)
    m = both_ref.shape[0] // 2
    each = block_ref.shape[1]

    @pl.when(j == 0)
    def _():
        left = list(refs)
        for s, groups in enumerate(slots):
            used = sum(groups)
            gather(me_ref[1 + s], regroup(left[:used], groups), block_ref)
            left = left[used:]
            high, low = split(block_ref[...].T)
            both_ref[s * each : (s + 1) * each] = high
            both_ref[m + s * each : m + (s + 1) * each] = low
        small_ref[...] = stacked(both_ref[...], both_ref[:m], split(r_ref[...]))

    value = stacked(both_ref[...], both_ref[:m], split(v_ref[...]))
    small = split(small_ref[...])
    count = v_ref.shape[1] // per
    for g in range(count):
        index = (j * count + g) ^ me_ref[0]
        c = split(take(index, even_ref, odd_ref))
        place(value[:, g * per : (g + 1) * per] - three(small, c), index, even_out, odd_out)


def late(me, vectors, reflectors, slots, even, odd, after, wide):
    rows, columns = vectors.shape
    nb = reflectors.shape[1]
    per = columns // wide
    step = width(columns, wide)
    flat = [x for groups, _ in slots for group in groups for x in group]
    counts = [[len(group) for group in groups] for groups, _ in slots]
    each = flat[0].shape[1]
    m = each * len(slots)
    which = jnp.stack([me[0]] + [choice.astype(jnp.int32) for _, choice in slots])
    half = jax.ShapeDtypeStruct((wide // 2, m, per), F32)
    return pl.pallas_call(
        functools.partial(late_kernel, per, counts),
        grid_spec=pltpu.PrefetchScalarGridSpec(
            num_scalar_prefetch=1,
            grid=(columns // step,),
            in_specs=[
                pl.BlockSpec((rows, step), lambda j, *_: (0, j)),
                whole((rows, nb)),
                whole(even.shape),
                whole(odd.shape),
                ANY,
            ]
            + [ANY] * len(flat),
            out_specs=[whole(half.shape)] * 2,
            scratch_shapes=[
                pltpu.VMEM((2 * m, rows), BF16),
                pltpu.VMEM((m, nb), F32),
                pltpu.VMEM((rows, each), F32),
            ],
        ),
        out_shape=[half, half],
        compiler_params=params(),
        cost_estimate=SHORT,
        name="late",
    )(which, vectors, reflectors, even, odd, after, *flat)


def share_kernel(rows, me_ref, even_ref, odd_ref, out_ref, all_ref):
    per = even_ref.shape[2]
    block = take((OFF // per) ^ me_ref[0], even_ref, odd_ref)
    first = OFF % per
    all_ref[...] = block[:, first : first + all_ref.shape[0]].T
    start = pl.multiple_of((me_ref[0] % (all_ref.shape[0] // rows)) * rows, rows)
    out_ref[...] = all_ref[pl.ds(start, rows), :]


def share(me, even, odd, block_width, rows):
    nb = even.shape[1]
    return pl.pallas_call(
        functools.partial(share_kernel, rows),
        grid_spec=pltpu.PrefetchScalarGridSpec(
            num_scalar_prefetch=1,
            grid=(1,),
            in_specs=[whole(even.shape), whole(odd.shape)],
            out_specs=whole((rows, nb)),
            scratch_shapes=[pltpu.VMEM((block_width, nb), F32)],
        ),
        out_shape=jax.ShapeDtypeStruct((rows, nb), F32),
        compiler_params=params(),
        cost_estimate=SHORT,
        name="share",
    )(me, even, odd)


def base_kernel(n, each, terms, at_ref, ready_ref, small_ref, c_ref, ce_ref, co_ref, *refs):
    *refs, out_ref, coef_ref = refs
    me, z = at_ref[0], at_ref[1]
    nb = c_ref.shape[0]
    half, _, rows, _ = ce_ref.shape
    for h in range(half):
        for p, ref in enumerate((ce_ref, co_ref)):
            owner = (me ^ (2 * h + p)) % (2 * half)
            for s in range(n):
                home = (z + n - s) % n
                first = pl.multiple_of(home * each + owner * rows, rows)
                coef_ref[pl.ds(first, rows), :] = ref[h, s]
    corrected = ready_ref[...] - three(split(small_ref[...]), split(c_ref[...]))
    out_ref[...] = -three(split(coef_ref[...]), split(corrected[:nb]))
    pieces = [corrected[nb:]]
    if terms:
        total = functools.reduce(jnp.add, [ref[...] for ref in refs])
        pieces += [total[k * each : (k + 1) * each] for k in range(total.shape[0] // each)]
    for slot, piece in enumerate(pieces):
        first = pl.multiple_of(at_ref[2 + slot] * each, each)
        out_ref[pl.ds(first, each), :] += piece


def base(at, ready, small, c, ce, co, terms, n, each):
    operands = [ready, small, c, ce, co, *terms]
    per = ready.shape[1]
    return pl.pallas_call(
        functools.partial(base_kernel, n, each, len(terms)),
        grid_spec=pltpu.PrefetchScalarGridSpec(
            num_scalar_prefetch=1,
            grid=(1,),
            in_specs=[whole(x.shape) for x in operands],
            out_specs=whole((FB, per)),
            scratch_shapes=[pltpu.VMEM((FB, c.shape[0]), F32)],
        ),
        out_shape=jax.ShapeDtypeStruct((FB, per), F32),
        compiler_params=params(),
        cost_estimate=SHORT,
        name="base",
    )(at, *operands)


def last_kernel(n, at_ref, base_ref, *refs):
    *refs, out_ref, total_ref = refs
    total = functools.reduce(jnp.add, [ref[...] for ref in refs])
    each = total.shape[0]
    first = pl.multiple_of(at_ref[1 + n] * each, each)
    total_ref[...] = base_ref[...]
    total_ref[pl.ds(first, each), :] += total
    out_ref[...] = total_ref[...].T


def last(at, held, terms, n):
    per = held.shape[1]
    operands = [held, *terms]
    return pl.pallas_call(
        functools.partial(last_kernel, n),
        grid_spec=pltpu.PrefetchScalarGridSpec(
            num_scalar_prefetch=1,
            grid=(1,),
            in_specs=[whole(x.shape) for x in operands],
            out_specs=whole((per, FB)),
            scratch_shapes=[pltpu.VMEM((FB, per), F32)],
        ),
        out_shape=jax.ShapeDtypeStruct((per, FB), F32),
        compiler_params=params(),
        cost_estimate=SHORT,
        name="last",
    )(at, *operands)


def arrivals(n):
    order = []
    for z in range(n):
        found = [(hops, 0) for hops in range(1, n) if z + hops < n]
        found += [(hops, 1) for hops in range(1, n) if z - hops >= 0]
        order.append(sorted(found))
    return [[order[z][slot] for z in range(n)] for slot in range(n - 1)]


def hop(held, n, hops, after):
    if after:
        count = len(held[0])
        both = gate(held[0] + held[1], *after, cost=LONG)
        held = [both[:count], both[count:]]
    pairs = [
        [(p, p - 1) for p in range(1, n - hops + 1)],
        [(p, p + 1) for p in range(hops - 1, n - 1)],
    ]
    return held, [[lax.ppermute(x, "narrow", pairs[d]) for x in held[d]] for d in (0, 1)]


def options(came, places, z):
    choices = sorted(set(places))
    which = jnp.int32(0)
    for p, place in enumerate(places):
        which = jnp.where(z == p, choices.index(place), which)
    return [[came[choice][c] for choice in choices] for c in range(CHUNKS)], which


def source(places, z):
    value = jnp.int32(0)
    for p, (hops, direction) in enumerate(places):
        value = jnp.where(z == p, p - hops if direction else p + hops, value)
    return value


def swap(x, wide, distance):
    return lax.ppermute(x, "wide", [(i, i ^ distance) for i in range(wide)])


def scatter_terms(even, odd, wide):
    other = swap(odd, wide, 1)
    sums = [even[h] + other[h] for h in range(wide // 2)]
    return [sums[0]] + [swap(sums[h], wide, 2 * h) for h in range(1, wide // 2)]


def collect(x, count):
    even = jnp.stack([x] + [swap(x, lax.axis_size("wide"), 2 * h) for h in range(1, count // 2)])
    return even, swap(even, lax.axis_size("wide"), 1)


def on_device(vectors, reflectors, triangle, energies):
    n = lax.axis_size("narrow")
    wide = lax.axis_size("wide")
    z = lax.axis_index("narrow").astype(jnp.int32)
    me = lax.axis_index("wide").astype(jnp.int32).reshape(1)
    each = FB // n
    rows, columns = vectors.shape
    step = rows // CHUNKS
    e_row = energies.reshape(1, rows)

    chunks = [
        energies[c * step : (c + 1) * step, None]
        * vectors[c * step : (c + 1) * step, OFF : OFF + each]
        for c in range(CHUNKS)
    ]
    came = {}

    def travel(held, hops, after):
        held, passed = hop(held, n, hops, after)
        for d in (0, 1):
            if hops > 1:
                came[(hops - 1, d)] = held[d]
            came[(hops, d)] = passed[d]
        return passed

    held = travel([chunks, chunks], 1, [])
    table = arrivals(n)
    at = jnp.stack([me[0], z, z] + [source(places, z) for places in table])

    own = chunks[0] if CHUNKS == 1 else jnp.concatenate(chunks, axis=0)
    even, odd, sums, small = first_pass(me, vectors, reflectors, e_row, own, wide)
    if n > 2:
        held = travel(held, 2, [small])
    ready = lax.psum_scatter(sums, "wide", scatter_dimension=0)
    small = lax.psum(small, "wide")

    terms = scatter_terms(even, odd, wide)
    projected = functools.reduce(jnp.add, terms)
    coefficients = jnp.dot(triangle, projected, precision=lax.Precision.HIGHEST)
    c_even, c_odd = collect(coefficients, wide)

    sharers = wide
    while (each // sharers) % 8:
        sharers //= 2
    mine = share(me, c_even, c_odd, each, each // sharers)
    shares = [mine] + [
        lax.ppermute(mine, "narrow", [(p, (p + s) % n) for p in range(n)]) for s in range(1, n)
    ]
    blocks = columns // width(columns, wide)
    updated, token = update(
        me, vectors, reflectors, c_even, c_odd, wide, 0, blocks // 2, [mine], None
    )
    for hops in range(3, n):
        held = travel(held, hops, [token])
    updated, token = update(
        me, vectors, reflectors, c_even, c_odd, wide, blocks // 2, blocks - blocks // 2,
        [x for d in (0, 1) for x in came[(n - 2, d)]] if n > 2 else [mine], updated,
    )
    share_even, share_odd = collect(jnp.stack(shares), sharers)

    middle = []
    if n > 2:
        slots = [options(came, table[slot], z) for slot in range(n - 2)]
        halves = late(me, vectors, reflectors, slots, c_even, c_odd, token, wide)
        middle = scatter_terms(*halves, wide)
    (token,) = gate([token], share_even, share_odd, *middle[:1])
    halves = late(
        me, vectors, reflectors, [options(came, table[n - 2], z)], c_even, c_odd, token, wide
    )
    held = base(at, ready, small, coefficients, share_even, share_odd, middle, n, each)
    fock_block = last(at, held, scatter_terms(*halves, wide), n)
    return (updated, fock_block)


def solution(mesh):
    return jax.shard_map(
        on_device,
        mesh=mesh,
        in_specs=(P("wide", "narrow"), P("wide", None), P(), P("wide")),
        out_specs=(P("wide", "narrow"), P(("narrow", "wide"), None)),
        check_vma=False,
    )
```

```python
import functools

import jax
import jax.numpy as jnp
from jax import lax
from jax.experimental import pallas as pl
from jax.experimental.pallas import tpu as pltpu
from jax.sharding import PartitionSpec as P

FB = 512
OFF = 256
CHUNKS = 1
VMEM = 56 * 1024 * 1024

F32 = jnp.float32
BF16 = jnp.bfloat16
LONG = pl.CostEstimate(flops=10**11, bytes_accessed=1024, transcendentals=0)
SHORT = pl.CostEstimate(flops=1024, bytes_accessed=1024, transcendentals=0)


def split(x):
    high = x.astype(BF16)
    return high, (x - high.astype(F32)).astype(BF16)


def mul(left, right):
    return jnp.dot(left, right, preferred_element_type=F32)


def three(left, right):
    (lh, ll), (rh, rl) = left, right
    return mul(lh, rh) + mul(ll, rh) + mul(lh, rl)


def stacked(both, high, right):
    rh, rl = right
    m = high.shape[0]
    top = mul(both, rh)
    return top[:m] + top[m:] + mul(high, rl)


def params():
    return pltpu.CompilerParams(
        dimension_semantics=("arbitrary",), vmem_limit_bytes=VMEM
    )


def width(columns, wide):
    return 256 if columns % 256 == 0 and 256 % (columns // wide) == 0 else columns // wide


def whole(shape):
    return pl.BlockSpec(shape, lambda j, *_: (0,) * len(shape), pipeline_mode=pl.Buffered(1))


ANY = pl.BlockSpec(memory_space=pl.ANY)


def gate_kernel(*refs):
    del refs


def gate(held, *others, cost=SHORT):
    count = len(held)
    return pl.pallas_call(
        gate_kernel,
        in_specs=[ANY] * (count + len(others)),
        out_specs=[ANY] * count,
        out_shape=[jax.ShapeDtypeStruct(x.shape, x.dtype) for x in held],
        input_output_aliases={k: k for k in range(count)},
        cost_estimate=cost,
        name="gate",
    )(*held, *others)


def place(value, index, even_ref, odd_ref):
    half = index // 2

    @pl.when(index % 2 == 0)
    def _():
        even_ref[half] = value

    @pl.when(index % 2 == 1)
    def _():
        odd_ref[half] = value


def take(index, even_ref, odd_ref):
    half = index // 2
    return jnp.where(index % 2 == 0, even_ref[half], odd_ref[half])


def project_kernel(per, me_ref, v_ref, r_ref, e_ref, even_ref, odd_ref, scaled_ref, both_ref):
    j = pl.program_id(0)
    nb = r_ref.shape[1]

    @pl.when(j == 0)
    def _():
        turned = r_ref[...].T
        both_ref[:nb], both_ref[nb:] = split(turned)
        scaled_ref[:nb], scaled_ref[nb:] = split(turned * e_ref[...])

    value = stacked(both_ref[...], both_ref[:nb], split(v_ref[...]))
    step = v_ref.shape[1]
    for g in range(step // per):
        w = j * (step // per) + g
        place(value[:, g * per : (g + 1) * per], w ^ me_ref[0], even_ref, odd_ref)


def project(me, vectors, reflectors, e_row, wide):
    rows, columns = vectors.shape
    nb = reflectors.shape[1]
    per = columns // wide
    step = width(columns, wide)
    half = jax.ShapeDtypeStruct((wide // 2, nb, per), F32)
    return pl.pallas_call(
        functools.partial(project_kernel, per),
        grid_spec=pltpu.PrefetchScalarGridSpec(
            num_scalar_prefetch=1,
            grid=(columns // step,),
            in_specs=[
                pl.BlockSpec((rows, step), lambda j, *_: (0, j)),
                whole((rows, nb)),
                whole((1, rows)),
            ],
            out_specs=[whole(half.shape), whole(half.shape), whole((2 * nb, rows))],
            scratch_shapes=[pltpu.VMEM((2 * nb, rows), BF16)],
        ),
        out_shape=[half, half, jax.ShapeDtypeStruct((2 * nb, rows), BF16)],
        compiler_params=params(),
        cost_estimate=SHORT,
        name="project",
    )(me, vectors, reflectors, e_row)


def update_kernel(per, me_ref, v_ref, r_ref, even_ref, odd_ref, after_ref, out_ref, token_ref, left_ref):
    j = pl.program_id(0)
    nb = r_ref.shape[1]

    @pl.when(j == 0)
    def _():
        token_ref[...] = jnp.zeros_like(token_ref)
        high, low = split(r_ref[...])
        left_ref[:, :nb] = high
        left_ref[:, nb : 2 * nb] = low
        left_ref[:, 2 * nb :] = high

    count = v_ref.shape[1] // per
    blocks = [take((j * count + g) ^ me_ref[0], even_ref, odd_ref) for g in range(count)]
    high, low = split(blocks[0] if count == 1 else jnp.concatenate(blocks, axis=1))
    right = jnp.concatenate([high, high, low], axis=0)
    out_ref[...] = v_ref[...] - mul(left_ref[...], right)


def update(me, vectors, reflectors, even, odd, wide, after):
    rows, columns = vectors.shape
    nb = reflectors.shape[1]
    per = columns // wide
    step = width(columns, wide)
    columns_of = pl.BlockSpec((rows, step), lambda j, *_: (0, j))
    return pl.pallas_call(
        functools.partial(update_kernel, per),
        grid_spec=pltpu.PrefetchScalarGridSpec(
            num_scalar_prefetch=1,
            grid=(columns // step,),
            in_specs=[columns_of, whole((rows, nb)), whole(even.shape), whole(odd.shape), ANY],
            out_specs=[columns_of, whole((8, 128))],
            scratch_shapes=[pltpu.VMEM((rows, 3 * nb), BF16)],
        ),
        out_shape=[
            jax.ShapeDtypeStruct(vectors.shape, F32),
            jax.ShapeDtypeStruct((8, 128), F32),
        ],
        compiler_params=params(),
        cost_estimate=SHORT,
        name="update",
    )(me, vectors, reflectors, even, odd, after)


def gather(choice, groups, block_ref):
    first = 0
    for group in groups:
        rows = group[0].shape[0]
        for k, ref in enumerate(group):

            @pl.when(choice == k)
            def _(ref=ref, first=first, rows=rows):
                pltpu.sync_copy(ref, block_ref.at[pl.ds(first, rows)])

        first += rows


def regroup(refs, groups):
    refs = list(refs)
    return [[refs.pop(0) for _ in range(count)] for count in groups]


def late_kernel(n, per, slots, at_ref, u_ref, scaled_ref, ce_ref, co_ref, after_ref, *refs):
    *refs, even_out, odd_out, both_ref, coef_ref, block_ref = refs
    j = pl.program_id(0)
    m = both_ref.shape[0] // 2
    each = block_ref.shape[1]
    me, z = at_ref[0], at_ref[1]

    @pl.when(j == 0)
    def _():
        nb = scaled_ref.shape[0] // 2
        half, _, rows, _ = ce_ref.shape
        left = list(refs)
        for s, groups in enumerate(slots):
            used = sum(groups)
            gather(at_ref[2 + 2 * s], regroup(left[:used], groups), block_ref)
            left = left[used:]
            away = (z + n - at_ref[3 + 2 * s]) % n
            for h in range(half):
                for p, ref in enumerate((ce_ref, co_ref)):
                    owner = (me ^ (2 * h + p)) % (2 * half)
                    first = pl.multiple_of(owner * rows, rows)
                    coef_ref[pl.ds(first, rows), :] = ref[h, away]
            scaled = (scaled_ref[:nb], scaled_ref[nb:])
            block = block_ref[...].T - three(split(coef_ref[...]), scaled)
            high, low = split(block)
            both_ref[s * each : (s + 1) * each] = high
            both_ref[m + s * each : m + (s + 1) * each] = low

    value = stacked(both_ref[...], both_ref[:m], split(u_ref[...]))
    count = u_ref.shape[1] // per
    for g in range(count):
        place(value[:, g * per : (g + 1) * per], (j * count + g) ^ me, even_out, odd_out)


def late(me, z, n, updated, scaled, slots, coef, after, wide):
    rows, columns = updated.shape
    per = columns // wide
    step = width(columns, wide)
    flat = [x for groups, _, _ in slots for group in groups for x in group]
    counts = [[len(group) for group in groups] for groups, _, _ in slots]
    each = flat[0].shape[1]
    m = each * len(slots)
    at = [me[0], z]
    for _, choice, home in slots:
        at += [choice, home]
    at = jnp.stack([x.astype(jnp.int32) for x in at])
    half = jax.ShapeDtypeStruct((wide // 2, m, per), F32)
    return pl.pallas_call(
        functools.partial(late_kernel, n, per, counts),
        grid_spec=pltpu.PrefetchScalarGridSpec(
            num_scalar_prefetch=1,
            grid=(columns // step,),
            in_specs=[
                pl.BlockSpec((rows, step), lambda j, *_: (0, j)),
                whole(scaled.shape),
                whole(coef[0].shape),
                whole(coef[1].shape),
                ANY,
            ]
            + [ANY] * len(flat),
            out_specs=[whole(half.shape)] * 2,
            scratch_shapes=[
                pltpu.VMEM((2 * m, rows), BF16),
                pltpu.VMEM((each, scaled.shape[0] // 2), F32),
                pltpu.VMEM((rows, each), F32),
            ],
        ),
        out_shape=[half, half],
        compiler_params=params(),
        cost_estimate=SHORT,
        name="late",
    )(at, updated, scaled, *coef, after, *flat)


def share_kernel(rows, me_ref, even_ref, odd_ref, out_ref, all_ref):
    per = even_ref.shape[2]
    block = take((OFF // per) ^ me_ref[0], even_ref, odd_ref)
    first = OFF % per
    all_ref[...] = block[:, first : first + all_ref.shape[0]].T
    start = pl.multiple_of((me_ref[0] % (all_ref.shape[0] // rows)) * rows, rows)
    out_ref[...] = all_ref[pl.ds(start, rows), :]


def share(me, even, odd, block_width, rows):
    nb = even.shape[1]
    return pl.pallas_call(
        functools.partial(share_kernel, rows),
        grid_spec=pltpu.PrefetchScalarGridSpec(
            num_scalar_prefetch=1,
            grid=(1,),
            in_specs=[whole(even.shape), whole(odd.shape)],
            out_specs=whole((rows, nb)),
            scratch_shapes=[pltpu.VMEM((block_width, nb), F32)],
        ),
        out_shape=jax.ShapeDtypeStruct((rows, nb), F32),
        compiler_params=params(),
        cost_estimate=SHORT,
        name="share",
    )(me, even, odd)


def base_kernel(at_ref, *refs):
    *refs, out_ref = refs
    total = functools.reduce(jnp.add, [ref[...] for ref in refs])
    count = total.shape[0] * at_ref.shape[0] // out_ref.shape[0]
    each = total.shape[0] // count
    for slot in range(count):
        first = pl.multiple_of(at_ref[slot] * each, each)
        out_ref[pl.ds(first, each), :] = total[slot * each : (slot + 1) * each]


def base(at, terms):
    per = terms[0].shape[1]
    return pl.pallas_call(
        base_kernel,
        grid_spec=pltpu.PrefetchScalarGridSpec(
            num_scalar_prefetch=1,
            grid=(1,),
            in_specs=[whole(x.shape) for x in terms],
            out_specs=whole((FB, per)),
        ),
        out_shape=jax.ShapeDtypeStruct((FB, per), F32),
        compiler_params=params(),
        cost_estimate=LONG,
        name="base",
    )(at, *terms)


def last_kernel(at_ref, base_ref, *refs):
    *refs, out_ref, total_ref = refs
    total = functools.reduce(jnp.add, [ref[...] for ref in refs])
    each = total.shape[0]
    first = pl.multiple_of(at_ref[at_ref.shape[0] - 1] * each, each)
    total_ref[...] = base_ref[...]
    total_ref[pl.ds(first, each), :] = total
    out_ref[...] = total_ref[...].T


def last(at, held, terms):
    per = held.shape[1]
    operands = [held, *terms]
    return pl.pallas_call(
        last_kernel,
        grid_spec=pltpu.PrefetchScalarGridSpec(
            num_scalar_prefetch=1,
            grid=(1,),
            in_specs=[whole(x.shape) for x in operands],
            out_specs=whole((per, FB)),
            scratch_shapes=[pltpu.VMEM((FB, per), F32)],
        ),
        out_shape=jax.ShapeDtypeStruct((per, FB), F32),
        compiler_params=params(),
        cost_estimate=SHORT,
        name="last",
    )(at, *operands)


def arrivals(n):
    order = []
    for z in range(n):
        found = [(hops, 0) for hops in range(1, n) if z + hops < n]
        found += [(hops, 1) for hops in range(1, n) if z - hops >= 0]
        order.append(sorted(found))
    return [[order[z][slot] for z in range(n)] for slot in range(n - 1)]


def hop(held, n, hops, after):
    if after:
        count = len(held[0])
        both = gate(held[0] + held[1], *after, cost=LONG)
        held = [both[:count], both[count:]]
    pairs = [
        [(p, p - 1) for p in range(1, n - hops + 1)],
        [(p, p + 1) for p in range(hops - 1, n - 1)],
    ]
    return held, [[lax.ppermute(x, "narrow", pairs[d]) for x in held[d]] for d in (0, 1)]


def options(came, places, z):
    choices = sorted(set(places))
    which = jnp.int32(0)
    for p, place in enumerate(places):
        which = jnp.where(z == p, choices.index(place), which)
    return [[came[choice][c] for choice in choices] for c in range(CHUNKS)], which


def source(places, z):
    value = jnp.int32(0)
    for p, (hops, direction) in enumerate(places):
        value = jnp.where(z == p, p - hops if direction else p + hops, value)
    return value


def swap(x, wide, distance):
    return lax.ppermute(x, "wide", [(i, i ^ distance) for i in range(wide)])


def scatter_terms(even, odd, wide, after=None):
    other = swap(odd, wide, 1)
    if after is not None:
        (other,) = gate([other], after)
    sums = [even[h] + other[h] for h in range(wide // 2)]
    return [sums[0]] + [swap(sums[h], wide, 2 * h) for h in range(1, wide // 2)]


def collect(x, count):
    even = jnp.stack([x] + [swap(x, lax.axis_size("wide"), 2 * h) for h in range(1, count // 2)])
    return even, swap(even, lax.axis_size("wide"), 1)


def on_device(vectors, reflectors, triangle, energies):
    n = lax.axis_size("narrow")
    wide = lax.axis_size("wide")
    z = lax.axis_index("narrow").astype(jnp.int32)
    me = lax.axis_index("wide").astype(jnp.int32).reshape(1)
    each = FB // n
    rows, columns = vectors.shape
    step = rows // CHUNKS
    e_row = energies.reshape(1, rows)

    chunks = [
        energies[c * step : (c + 1) * step, None]
        * vectors[c * step : (c + 1) * step, OFF : OFF + each]
        for c in range(CHUNKS)
    ]
    came = {}

    def travel(held, hops, after):
        held, passed = hop(held, n, hops, after)
        for d in (0, 1):
            if hops > 1:
                came[(hops - 1, d)] = held[d]
            came[(hops, d)] = passed[d]
        return passed

    held = travel([chunks, chunks], 1, [])
    table = arrivals(n)
    at = jnp.stack([z] + [source(places, z) for places in table])

    even, odd, scaled = project(me, vectors, reflectors, e_row, wide)
    if n > 2:
        held = travel(held, 2, [scaled])

    projected = functools.reduce(jnp.add, scatter_terms(even, odd, wide))
    coefficients = jnp.dot(triangle, projected, precision=lax.Precision.HIGHEST)
    c_even, c_odd = collect(coefficients, wide)

    sharers = wide
    while (each // sharers) % 8:
        sharers //= 2
    mine = share(me, c_even, c_odd, each, each // sharers)
    shares = jnp.stack(
        [mine]
        + [lax.ppermute(mine, "narrow", [(p, (p + s) % n) for p in range(n)]) for s in range(1, n)]
    )
    updated, token = update(me, vectors, reflectors, c_even, c_odd, wide, shares)
    for hops in range(3, n):
        held = travel(held, hops, [token])
    coef = collect(shares, sharers)

    slots = [([[chunk] for chunk in chunks], jnp.int32(0), z)]
    for slot in range(n - 1):
        slots.append((*options(came, table[slot], z), at[1 + slot]))
    halves = late(me, z, n, updated, scaled, slots[:-1], coef, token, wide)
    middle = scatter_terms(*halves, wide)
    (token,) = gate([token], middle[0])
    halves = late(me, z, n, updated, scaled, slots[-1:], coef, token, wide)
    held = base(at, middle)
    fock_block = last(at, held, scatter_terms(*halves, wide, held))
    return (updated, fock_block)


def solution(mesh):
    return jax.shard_map(
        on_device,
        mesh=mesh,
        in_specs=(P("wide", "narrow"), P("wide", None), P(), P("wide")),
        out_specs=(P("wide", "narrow"), P(("narrow", "wide"), None)),
        check_vma=False,
    )
```

```python
import functools

import jax
import jax.numpy as jnp
from jax import lax
from jax.experimental import pallas as pl
from jax.experimental.pallas import tpu as pltpu
from jax.sharding import PartitionSpec as P

FB = 512
OFF = 256
VMEM = 60 * 1024 * 1024

F32 = jnp.float32
BF16 = jnp.bfloat16
LONG = pl.CostEstimate(flops=10**11, bytes_accessed=1024, transcendentals=0)
SHORT = pl.CostEstimate(flops=1024, bytes_accessed=1024, transcendentals=0)


def split(x):
    high = x.astype(BF16)
    return high, (x - high.astype(F32)).astype(BF16)


def mul(left, right):
    return jnp.dot(left, right, preferred_element_type=F32)


def three(left, right):
    (lh, ll), (rh, rl) = left, right
    return mul(lh, rh) + mul(ll, rh) + mul(lh, rl)


def stacked(both, high, right):
    rh, rl = right
    m = high.shape[0]
    top = mul(both, rh)
    return top[:m] + top[m:] + mul(high, rl)


def params():
    return pltpu.CompilerParams(
        dimension_semantics=("arbitrary",), vmem_limit_bytes=VMEM
    )


def width(columns, wide):
    return 256 if columns % 256 == 0 and 256 % (columns // wide) == 0 else columns // wide


def whole(shape):
    return pl.BlockSpec(shape, lambda j, *_: (0,) * len(shape), pipeline_mode=pl.Buffered(1))


ANY = pl.BlockSpec(memory_space=pl.ANY)


def gate_kernel(*refs):
    del refs


def gate(held, *others, cost=SHORT):
    count = len(held)
    return pl.pallas_call(
        gate_kernel,
        in_specs=[ANY] * (count + len(others)),
        out_specs=[ANY] * count,
        out_shape=[jax.ShapeDtypeStruct(x.shape, x.dtype) for x in held],
        input_output_aliases={k: k for k in range(count)},
        cost_estimate=cost,
        name="gate",
    )(*held, *others)


def place(value, index, even_ref, odd_ref, first):
    half = index // 2
    rows = value.shape[0]

    @pl.when(index % 2 == 0)
    def _():
        even_ref[half, first : first + rows] = value

    @pl.when(index % 2 == 1)
    def _():
        odd_ref[half, first : first + rows] = value


def take(index, even_ref, odd_ref, rows):
    half = index // 2
    return jnp.where(index % 2 == 0, even_ref[half, rows], odd_ref[half, rows])


def project_kernel(per, each, wide, me_ref, v_ref, r_ref, e_ref, after_ref, even_ref, odd_ref, scaled_ref, own_ref, both_ref):
    j = pl.program_id(0)
    nb = r_ref.shape[1]
    step = v_ref.shape[1]

    @pl.when(j == 0)
    def _():
        turned = r_ref[...].T
        both_ref[:nb], both_ref[nb:] = split(turned)
        scaled_ref[:nb], scaled_ref[nb:] = split(turned * e_ref[...])

    value = stacked(both_ref[...], both_ref[:nb], split(v_ref[...]))
    for g in range(step // per):
        index = (j * (step // per) + g) ^ me_ref[0]
        place(value[:, g * per : (g + 1) * per], index, even_ref, odd_ref, 0)

    @pl.when(j == OFF // step)
    def _():
        own = value[:, OFF % step : OFF % step + each].T
        own_ref[...] = own
        rows = even_ref.shape[1] - nb
        if rows:
            for w in range(wide):
                place(own[w * rows : (w + 1) * rows], w ^ me_ref[0], even_ref, odd_ref, nb)


def project(me, vectors, reflectors, e_row, after, wide, each, rows):
    height, columns = vectors.shape
    nb = reflectors.shape[1]
    per = columns // wide
    step = width(columns, wide)
    half = jax.ShapeDtypeStruct((wide // 2, nb + rows, per), F32)
    return pl.pallas_call(
        functools.partial(project_kernel, per, each, wide),
        grid_spec=pltpu.PrefetchScalarGridSpec(
            num_scalar_prefetch=1,
            grid=(columns // step,),
            in_specs=[
                pl.BlockSpec((height, step), lambda j, *_: (0, j)),
                whole((height, nb)),
                whole((1, height)),
                ANY,
            ],
            out_specs=[
                whole(half.shape),
                whole(half.shape),
                whole((2 * nb, height)),
                whole((each, nb)),
            ],
            scratch_shapes=[pltpu.VMEM((2 * nb, height), BF16)],
        ),
        out_shape=[
            half,
            half,
            jax.ShapeDtypeStruct((2 * nb, height), BF16),
            jax.ShapeDtypeStruct((each, nb), F32),
        ],
        compiler_params=params(),
        cost_estimate=SHORT,
        name="project",
    )(me, vectors, reflectors, e_row, after)


def gather(choice, groups, block_ref):
    first = 0
    for group in groups:
        rows = group[0].shape[0]
        for k, ref in enumerate(group):

            @pl.when(choice == k)
            def _(ref=ref, first=first, rows=rows):
                pltpu.sync_copy(ref, block_ref.at[pl.ds(first, rows)])

        first += rows


def regroup(refs, groups):
    refs = list(refs)
    return [[refs.pop(0) for _ in range(count)] for count in groups]


def load_slots(n, slots, at_ref, scaled, ce_ref, co_ref, coef_in, refs, both_ref, coef_ref, block_ref):
    m = both_ref.shape[0] // 2
    each = block_ref.shape[1]
    nb = coef_ref.shape[1]
    me, z = at_ref[0], at_ref[1]
    left = list(refs)
    for s, groups in enumerate(slots):
        used = sum(groups)
        gather(at_ref[2 + 2 * s], regroup(left[:used], groups), block_ref)
        left = left[used:]
        home = at_ref[3 + 2 * s]
        if coef_in is not None:
            coef_ref[...] = coef_in[home]
        else:
            wide = 2 * ce_ref.shape[0]
            rows = each // wide
            first = pl.multiple_of(nb + (z + n - home) % n * rows, rows)
            for w in range(wide):
                coef_ref[w * rows : (w + 1) * rows] = take(
                    w ^ me, ce_ref, co_ref, pl.ds(first, rows)
                )
        high, low = split(block_ref[...].T - three(split(coef_ref[...]), scaled))
        both_ref[s * each : (s + 1) * each] = high
        both_ref[m + s * each : m + (s + 1) * each] = low


def merged_kernel(n, per, slots, has_coef, at_ref, v_ref, r_ref, scaled_ref, ce_ref, co_ref, after_ref, *refs):
    *refs, out_ref, even_out, odd_out, token_ref, left_ref, both_ref, coef_ref, block_ref = refs
    coef_in, refs = (refs[0], refs[1:]) if has_coef else (None, refs)
    j = pl.program_id(0)
    nb = r_ref.shape[1]
    m = both_ref.shape[0] // 2

    @pl.when(j == 0)
    def _():
        token_ref[...] = jnp.zeros_like(token_ref)
        high, low = split(r_ref[...])
        left_ref[:, :nb] = high
        left_ref[:, nb : 2 * nb] = low
        left_ref[:, 2 * nb :] = high
        scaled = (scaled_ref[:nb], scaled_ref[nb:])
        load_slots(
            n, slots, at_ref, scaled, ce_ref, co_ref, coef_in, refs, both_ref, coef_ref, block_ref
        )

    count = v_ref.shape[1] // per
    indices = [(j * count + g) ^ at_ref[0] for g in range(count)]
    blocks = [take(index, ce_ref, co_ref, slice(0, nb)) for index in indices]
    high, low = split(blocks[0] if count == 1 else jnp.concatenate(blocks, axis=1))
    u = v_ref[...] - mul(left_ref[...], jnp.concatenate([high, high, low], axis=0))
    out_ref[...] = u
    value = stacked(both_ref[...], both_ref[:m], split(u))
    for g, index in enumerate(indices):
        place(value[:, g * per : (g + 1) * per], index, even_out, odd_out, 0)


def late_kernel(n, per, slots, has_coef, has_before, chunk, at_ref, u_ref, scaled_ref, ce_ref, co_ref, after_ref, *refs):
    *refs, even_out, odd_out, both_ref, coef_ref, block_ref = refs
    coef_in, refs = (refs[0], refs[1:]) if has_coef else (None, refs)
    before, refs = (refs[:2], refs[2:]) if has_before else (None, refs)
    j = pl.program_id(0)
    rows = both_ref.shape[1]
    m = both_ref.shape[0] // 2

    @pl.when(j == 0)
    def _():
        nb = coef_ref.shape[1]
        first = chunk * u_ref.shape[0]
        scaled = (scaled_ref[:nb, first : first + rows], scaled_ref[nb:, first : first + rows])
        load_slots(
            n, slots, at_ref, scaled, ce_ref, co_ref, coef_in, refs, both_ref, coef_ref, block_ref
        )

    value = stacked(both_ref[...], both_ref[:m], split(u_ref[:rows]))
    count = u_ref.shape[1] // per
    for g in range(count):
        index = (j * count + g) ^ at_ref[0]
        part = value[:, g * per : (g + 1) * per]
        if before is not None:
            part = part + take(index, *before, slice(0, m))
        place(part, index, even_out, odd_out, 0)


def slot_operands(me, z, slots):
    flat = [x for groups, _, _ in slots for group in groups for x in group]
    counts = [[len(group) for group in groups] for groups, _, _ in slots]
    at = [me[0], z]
    for _, choice, home in slots:
        at += [choice, home]
    return jnp.stack([x.astype(jnp.int32) for x in at]), flat, counts


def merged(me, z, n, vectors, reflectors, scaled, slots, c, coef, after, wide):
    rows, columns = vectors.shape
    nb = reflectors.shape[1]
    per = columns // wide
    step = width(columns, wide)
    at, flat, counts = slot_operands(me, z, slots)
    each = flat[0].shape[1]
    m = each * len(slots)
    half = jax.ShapeDtypeStruct((wide // 2, m, per), F32)
    columns_of = pl.BlockSpec((rows, step), lambda j, *_: (0, j))
    return pl.pallas_call(
        functools.partial(merged_kernel, n, per, counts, bool(coef)),
        grid_spec=pltpu.PrefetchScalarGridSpec(
            num_scalar_prefetch=1,
            grid=(columns // step,),
            in_specs=[columns_of]
            + [whole(x.shape) for x in (reflectors, scaled, *c)]
            + [ANY]
            + [whole(x.shape) for x in coef]
            + [ANY] * len(flat),
            out_specs=[columns_of, whole(half.shape), whole(half.shape), whole((8, 128))],
            scratch_shapes=[
                pltpu.VMEM((rows, 3 * nb), BF16),
                pltpu.VMEM((2 * m, rows), BF16),
                pltpu.VMEM((each, nb), F32),
                pltpu.VMEM((rows, each), F32),
            ],
        ),
        out_shape=[
            jax.ShapeDtypeStruct(vectors.shape, F32),
            half,
            half,
            jax.ShapeDtypeStruct((8, 128), F32),
        ],
        compiler_params=params(),
        cost_estimate=SHORT,
        name="merged",
    )(at, vectors, reflectors, scaled, *c, after, *coef, *flat)


def late(me, z, n, updated, scaled, slots, c, coef, before, after, chunk, wide):
    columns = updated.shape[1]
    per = columns // wide
    step = width(columns, wide)
    at, flat, counts = slot_operands(me, z, slots)
    rows, each = flat[0].shape
    m = each * len(slots)
    half = jax.ShapeDtypeStruct((wide // 2, m, per), F32)
    height = updated.shape[0] - rows if chunk else rows
    return pl.pallas_call(
        functools.partial(late_kernel, n, per, counts, bool(coef), bool(before), chunk),
        grid_spec=pltpu.PrefetchScalarGridSpec(
            num_scalar_prefetch=1,
            grid=(columns // step,),
            in_specs=[pl.BlockSpec((height, step), lambda j, *_: (chunk, j))]
            + [whole(x.shape) for x in (scaled, *c)]
            + [ANY]
            + [whole(x.shape) for x in (*coef, *before)]
            + [ANY] * len(flat),
            out_specs=[whole(half.shape)] * 2,
            scratch_shapes=[
                pltpu.VMEM((2 * m, rows), BF16),
                pltpu.VMEM((each, scaled.shape[0] // 2), F32),
                pltpu.VMEM((rows, each), F32),
            ],
        ),
        out_shape=[half, half],
        compiler_params=params(),
        cost_estimate=SHORT,
        name="late",
    )(at, updated, scaled, *c, after, *coef, *before, *flat)


def fill(at_ref, first_slot, total, each, out_ref):
    for k in range(total.shape[0] // each):
        first = pl.multiple_of(at_ref[first_slot + k] * each, each)
        out_ref[pl.ds(first, each), :] = total[k * each : (k + 1) * each]


def base_kernel(each, at_ref, *refs):
    *refs, out_ref = refs
    out_ref[...] = jnp.zeros_like(out_ref)
    fill(at_ref, 0, functools.reduce(jnp.add, [ref[...] for ref in refs]), each, out_ref)


def base(at, terms, each):
    per = terms[0].shape[1]
    return pl.pallas_call(
        functools.partial(base_kernel, each),
        grid_spec=pltpu.PrefetchScalarGridSpec(
            num_scalar_prefetch=1,
            grid=(1,),
            in_specs=[whole(x.shape) for x in terms],
            out_specs=whole((FB, per)),
        ),
        out_shape=jax.ShapeDtypeStruct((FB, per), F32),
        compiler_params=params(),
        cost_estimate=LONG,
        name="base",
    )(at, *terms)


def last_kernel(each, at_ref, base_ref, *refs):
    *refs, out_ref, total_ref = refs
    total_ref[...] = base_ref[...]
    total = functools.reduce(jnp.add, [ref[...] for ref in refs])
    fill(at_ref, at_ref.shape[0] - total.shape[0] // each, total, each, total_ref)
    out_ref[...] = total_ref[...].T


def last(at, held, terms, each):
    per = held.shape[1]
    operands = [held, *terms]
    return pl.pallas_call(
        functools.partial(last_kernel, each),
        grid_spec=pltpu.PrefetchScalarGridSpec(
            num_scalar_prefetch=1,
            grid=(1,),
            in_specs=[whole(x.shape) for x in operands],
            out_specs=whole((per, FB)),
            scratch_shapes=[pltpu.VMEM((FB, per), F32)],
        ),
        out_shape=jax.ShapeDtypeStruct((per, FB), F32),
        compiler_params=params(),
        cost_estimate=SHORT,
        name="last",
    )(at, *operands)


def arrivals(n):
    order = []
    for z in range(n):
        found = [(hops, 0) for hops in range(1, n) if z + hops < n]
        found += [(hops, 1) for hops in range(1, n) if z - hops >= 0]
        order.append(sorted(found))
    return [[order[z][slot] for z in range(n)] for slot in range(n - 1)]


def hop(held, n, hops, after):
    if hops > 1:
        held = gate(held, *after)
    pairs = [
        [(p, p - 1) for p in range(1, n - hops + 1)],
        [(p, p + 1) for p in range(hops - 1, n - 1)],
    ]
    return held, [lax.ppermute(held[d], "narrow", pairs[d]) for d in (0, 1)]


def options(came, places, z, chunks):
    choices = sorted(set(places))
    which = jnp.int32(0)
    for p, place in enumerate(places):
        which = jnp.where(z == p, choices.index(place), which)
    return [[came[(c, *choice)] for choice in choices] for c in chunks], which


def source(places, z):
    value = jnp.int32(0)
    for p, (hops, direction) in enumerate(places):
        value = jnp.where(z == p, p - hops if direction else p + hops, value)
    return value


def swap(x, wide, distance):
    return lax.ppermute(x, "wide", [(i, i ^ distance) for i in range(wide)])


def scatter_terms(even, odd, wide, after=None):
    other = swap(odd, wide, 1)
    if after is not None:
        (other,) = gate([other], after)
    sums = [even[h] + other[h] for h in range(wide // 2)]
    return [sums[0]] + [swap(sums[h], wide, 2 * h) for h in range(1, wide // 2)]


def collect(x, count):
    even = jnp.stack([x] + [swap(x, lax.axis_size("wide"), 2 * h) for h in range(1, count // 2)])
    return even, swap(even, lax.axis_size("wide"), 1)


def on_device(vectors, reflectors, triangle, energies):
    n = lax.axis_size("narrow")
    wide = lax.axis_size("wide")
    z = lax.axis_index("narrow").astype(jnp.int32)
    me = lax.axis_index("wide").astype(jnp.int32).reshape(1)
    each = FB // n
    height, columns = vectors.shape
    nb = reflectors.shape[1]
    per = columns // wide
    e_row = energies.reshape(1, height)

    cut = -(-height * 4 // 7 // 128) * 128
    bounds = [(0, cut), (cut, height)]
    chunks = [
        energies[first:end, None] * vectors[first:end, OFF : OFF + each] for first, end in bounds
    ]
    came = {}

    def travel(c, held, hops, after):
        held, passed = hop(held, n, hops, after)
        for d in (0, 1):
            if hops > 1:
                came[(c, hops - 1, d)] = held[d]
            came[(c, hops, d)] = passed[d]
        return passed

    held = [travel(c, [chunk, chunk], 1, []) for c, chunk in enumerate(chunks)]
    table = arrivals(n)
    at = jnp.stack([z] + [source(places, z) for places in table])

    rows = each // wide if per == nb and (each // wide) % 8 == 0 else 0
    even, odd, scaled, own = project(me, vectors, reflectors, e_row, chunks[1], wide, each, rows)
    (odd,) = gate([odd], *held[0])
    terms = scatter_terms(even, odd, wide)
    terms[0] = gate(terms[:1], *held[1])[0]
    projected = functools.reduce(jnp.add, terms)
    highest = lax.Precision.HIGHEST
    coefficients = jnp.dot(triangle, projected[:nb], precision=highest)
    turn = (((1,), (1,)), ((), ()))
    if rows:
        mine = lax.dot_general(projected[nb:], triangle, turn, precision=highest)
        shares = [mine] + [
            lax.ppermute(mine, "narrow", [(p, (p + s) % n) for p in range(n)]) for s in range(1, n)
        ]
        coefficients = jnp.concatenate([coefficients, *shares], axis=0)
        ready, coef = shares[1:], []
    else:
        own = lax.dot_general(lax.psum(own, "wide"), triangle, turn, precision=highest)
        coef = [lax.all_gather(own, "narrow")]
        ready = coef
    c = collect(coefficients, wide)

    for hops in range(2, n):
        for k in range(len(chunks)):
            if hops == 2:
                held[k] = travel(k, held[k], hops, ready)
            elif k == 0:
                held[k] = travel(k, held[k], hops, [])
    slots = [([[chunk] for chunk in chunks], jnp.int32(0), z)]
    slots.append((*options(came, table[0], z, (0, 1)), at[1]))
    updated, *halves, token = merged(
        me, z, n, vectors, reflectors, scaled, slots, c, coef, came[(0, min(2, n - 1), 0)], wide
    )
    for hops in range(3, n):
        held[1] = travel(1, held[1], hops, [token])
    even, odd = halves
    (odd,) = gate([odd], *held[0])
    middle = scatter_terms(even, odd, wide)
    (token,) = gate([token], middle[0])
    halves = []
    for k in (0, 1):
        slots = [
            (*options(came, table[slot], z, (k,)), at[1 + slot]) for slot in range(1, n - 1)
        ]
        halves = late(me, z, n, updated, scaled, slots, c, coef, halves, token, k, wide)
    held = base(at, middle, each)
    fock_block = last(at, held, scatter_terms(*halves, wide, held), each)
    return (updated, fock_block)


def solution(mesh):
    return jax.shard_map(
        on_device,
        mesh=mesh,
        in_specs=(P("wide", "narrow"), P("wide", None), P(), P("wide")),
        out_specs=(P("wide", "narrow"), P(("narrow", "wide"), None)),
        check_vma=False,
    )
```

```python
import functools

import jax
import jax.numpy as jnp
from jax import lax
from jax.experimental import pallas as pl
from jax.experimental.pallas import tpu as pltpu
from jax.sharding import PartitionSpec as P

FB = 512
OFF = 256
VMEM = 60 * 1024 * 1024

F32 = jnp.float32
BF16 = jnp.bfloat16
LONG = pl.CostEstimate(flops=10**11, bytes_accessed=1024, transcendentals=0)
SHORT = pl.CostEstimate(flops=1024, bytes_accessed=1024, transcendentals=0)


def split(x):
    high = x.astype(BF16)
    return high, (x - high.astype(F32)).astype(BF16)


def mul(left, right):
    return jnp.dot(left, right, preferred_element_type=F32)


def three(left, right):
    (lh, ll), (rh, rl) = left, right
    return mul(lh, rh) + mul(ll, rh) + mul(lh, rl)


def stacked(both, high, right):
    rh, rl = right
    m = high.shape[0]
    top = mul(both, rh)
    return top[:m] + top[m:] + mul(high, rl)


def params():
    return pltpu.CompilerParams(
        dimension_semantics=("arbitrary",), vmem_limit_bytes=VMEM
    )


def width(columns, wide):
    return 256 if columns % 256 == 0 and 256 % (columns // wide) == 0 else columns // wide


def whole(shape):
    return pl.BlockSpec(shape, lambda j, *_: (0,) * len(shape), pipeline_mode=pl.Buffered(1))


ANY = pl.BlockSpec(memory_space=pl.ANY)


def gate_kernel(*refs):
    del refs


def gate(held, *others, cost=SHORT):
    count = len(held)
    return pl.pallas_call(
        gate_kernel,
        in_specs=[ANY] * (count + len(others)),
        out_specs=[ANY] * count,
        out_shape=[jax.ShapeDtypeStruct(x.shape, x.dtype) for x in held],
        input_output_aliases={k: k for k in range(count)},
        cost_estimate=cost,
        name="gate",
    )(*held, *others)


def place(value, index, even_ref, odd_ref, first):
    half = index // 2
    rows = value.shape[0]

    @pl.when(index % 2 == 0)
    def _():
        even_ref[half, first : first + rows] = value

    @pl.when(index % 2 == 1)
    def _():
        odd_ref[half, first : first + rows] = value


def take(index, even_ref, odd_ref, rows):
    half = index // 2
    return jnp.where(index % 2 == 0, even_ref[half, rows], odd_ref[half, rows])


def project_kernel(per, wide, me_ref, v_ref, r_ref, e_ref, x_ref, even_ref, odd_ref, left_ref, own_ref, small_ref, both_ref):
    j = pl.program_id(0)
    nb = r_ref.shape[1]
    each = x_ref.shape[1]
    step = v_ref.shape[1]
    ride = even_ref.shape[1] - nb

    @pl.when(j == 0)
    def _():
        turned = r_ref[...].T
        both_ref[:nb], both_ref[nb:] = split(turned)
        k = nb + each
        left_ref[:nb], left_ref[k : k + nb] = split(turned * e_ref[...])
        left_ref[nb:k], left_ref[k + nb :] = split(x_ref[...].T)
        small = three((left_ref[:k], left_ref[k:]), split(r_ref[...]))
        small_ref[...] = small
        if ride:
            rows = k // wide
            for w in range(wide):
                place(small[w * rows : (w + 1) * rows], w ^ me_ref[0], even_ref, odd_ref, nb)

    value = stacked(both_ref[...], both_ref[:nb], split(v_ref[...]))
    for g in range(step // per):
        index = (j * (step // per) + g) ^ me_ref[0]
        place(value[:, g * per : (g + 1) * per], index, even_ref, odd_ref, 0)

    @pl.when(j == OFF // step)
    def _():
        own = value[:, OFF % step : OFF % step + each].T
        own_ref[...] = own
        if ride:
            rows = each // wide
            for w in range(wide):
                place(
                    own[w * rows : (w + 1) * rows], w ^ me_ref[0], even_ref, odd_ref,
                    nb + ride - rows,
                )


def project(me, vectors, reflectors, e_row, block, wide, ride):
    rows, columns = vectors.shape
    nb = reflectors.shape[1]
    each = block.shape[1]
    k = nb + each
    per = columns // wide
    step = width(columns, wide)
    shapes = [(wide // 2, nb + ride, per)] * 2 + [(2 * k, rows), (each, nb), (k, nb)]
    kinds = [F32, F32, BF16, F32, F32]
    return pl.pallas_call(
        functools.partial(project_kernel, per, wide),
        grid_spec=pltpu.PrefetchScalarGridSpec(
            num_scalar_prefetch=1,
            grid=(columns // step,),
            in_specs=[pl.BlockSpec((rows, step), lambda j, *_: (0, j))]
            + [whole(x) for x in ((rows, nb), (1, rows), block.shape)],
            out_specs=[whole(x) for x in shapes],
            scratch_shapes=[pltpu.VMEM((2 * nb, rows), BF16)],
        ),
        out_shape=[jax.ShapeDtypeStruct(x, kind) for x, kind in zip(shapes, kinds)],
        compiler_params=params(),
        cost_estimate=SHORT,
        name="project",
    )(me, vectors, reflectors, e_row, block)


def early_kernel(per, v_ref, left_ref, *refs):
    out_ref, token_ref = refs[-2:]
    k = left_ref.shape[0] // 2
    token_ref[...] = jnp.zeros_like(token_ref)
    value = stacked(left_ref[...], left_ref[:k], split(v_ref[...]))
    for g in range(v_ref.shape[1] // per):
        out_ref[g] = value[:, g * per : (g + 1) * per]


def early(vectors, left, offset, blocks, after, before, wide):
    rows, columns = vectors.shape
    per = columns // wide
    step = width(columns, wide)
    count = step // per
    k = left.shape[0] // 2
    operands = [vectors, left, after] + before
    return pl.pallas_call(
        functools.partial(early_kernel, per),
        grid=(blocks,),
        in_specs=[pl.BlockSpec((rows, step), lambda j: (0, j + offset)), whole(left.shape)]
        + [ANY] * (len(operands) - 2),
        out_specs=[
            pl.BlockSpec((count, k, per), lambda j: (j + offset, 0, 0)),
            whole((8, 128)),
        ],
        out_shape=[
            jax.ShapeDtypeStruct((wide, k, per), F32),
            jax.ShapeDtypeStruct((8, 128), F32),
        ],
        input_output_aliases={3: 0} if before else {},
        compiler_params=params(),
        cost_estimate=SHORT,
        name="early",
    )(*operands)


def update_kernel(per, offset, me_ref, v_ref, r_ref, even_ref, odd_ref, *refs):
    out_ref, token_ref, left_ref = refs[-3:]
    j = pl.program_id(0)
    nb = r_ref.shape[1]

    @pl.when(j == 0)
    def _():
        token_ref[...] = jnp.zeros_like(token_ref)
        high, low = split(r_ref[...])
        left_ref[:, :nb] = high
        left_ref[:, nb : 2 * nb] = low
        left_ref[:, 2 * nb :] = high

    count = v_ref.shape[1] // per
    blocks = [
        take(((j + offset) * count + g) ^ me_ref[0], even_ref, odd_ref, slice(0, nb))
        for g in range(count)
    ]
    high, low = split(blocks[0] if count == 1 else jnp.concatenate(blocks, axis=1))
    right = jnp.concatenate([high, high, low], axis=0)
    out_ref[...] = v_ref[...] - mul(left_ref[...], right)


def update(me, vectors, reflectors, c, offset, blocks, after, before, wide):
    rows, columns = vectors.shape
    nb = reflectors.shape[1]
    per = columns // wide
    step = width(columns, wide)
    operands = [me, vectors, reflectors, *c, *after]
    aliases = {len(operands): 0} if before else {}
    operands += before
    columns_of = pl.BlockSpec((rows, step), lambda j, *_: (0, j + offset))
    return pl.pallas_call(
        functools.partial(update_kernel, per, offset),
        grid_spec=pltpu.PrefetchScalarGridSpec(
            num_scalar_prefetch=1,
            grid=(blocks,),
            in_specs=[columns_of]
            + [whole(x.shape) for x in (reflectors, *c)]
            + [ANY] * (len(operands) - 5),
            out_specs=[columns_of, whole((8, 128))],
            scratch_shapes=[pltpu.VMEM((rows, 3 * nb), BF16)],
        ),
        out_shape=[
            jax.ShapeDtypeStruct(vectors.shape, F32),
            jax.ShapeDtypeStruct((8, 128), F32),
        ],
        input_output_aliases=aliases,
        compiler_params=params(),
        cost_estimate=SHORT,
        name="update",
    )(*operands)


def late_kernel(per, counts, at_ref, u_ref, after_ref, *refs):
    *refs, even_out, odd_out, both_ref, block_ref, sem_ref = refs
    j = pl.program_id(0)
    m = both_ref.shape[0] // 2
    each = block_ref.shape[2]

    @pl.when(j == 0)
    def _():
        first = 0
        for s, count in enumerate(counts):
            for k, ref in enumerate(refs[first : first + count]):

                @pl.when(at_ref[1 + s] == k)
                def _(ref=ref, s=s):
                    pltpu.make_async_copy(ref, block_ref.at[s], sem_ref.at[s]).start()

            first += count
        for s in range(len(counts)):
            pltpu.make_async_copy(block_ref.at[s], block_ref.at[s], sem_ref.at[s]).wait()
            high, low = split(block_ref[s].T)
            both_ref[s * each : (s + 1) * each] = high
            both_ref[m + s * each : m + (s + 1) * each] = low

    value = stacked(both_ref[...], both_ref[:m], split(u_ref[...]))
    count = u_ref.shape[1] // per
    for g in range(count):
        index = (j * count + g) ^ at_ref[0]
        place(value[:, g * per : (g + 1) * per], index, even_out, odd_out, 0)


def late(me, updated, slots, after, wide):
    rows, columns = updated.shape
    per = columns // wide
    step = width(columns, wide)
    flat = [x for choices, _ in slots for x in choices]
    counts = [len(choices) for choices, _ in slots]
    each = flat[0].shape[1]
    m = each * len(slots)
    at = jnp.stack([me[0]] + [which.astype(jnp.int32) for _, which in slots])
    half = jax.ShapeDtypeStruct((wide // 2, m, per), F32)
    return pl.pallas_call(
        functools.partial(late_kernel, per, counts),
        grid_spec=pltpu.PrefetchScalarGridSpec(
            num_scalar_prefetch=1,
            grid=(columns // step,),
            in_specs=[pl.BlockSpec((rows, step), lambda j, *_: (0, j))] + [ANY] * (1 + len(flat)),
            out_specs=[whole(half.shape)] * 2,
            scratch_shapes=[
                pltpu.VMEM((2 * m, rows), BF16),
                pltpu.VMEM((len(slots), rows, each), F32),
                pltpu.SemaphoreType.DMA((len(slots),)),
            ],
        ),
        out_shape=[half, half],
        compiler_params=params(),
        cost_estimate=SHORT,
        name="late",
    )(at, updated, after, *flat)


def base_kernel(n, each, ride, at_ref, ready_ref, c_ref, *refs):
    *refs, out_ref, coef_ref, small_ref = refs
    me, z = at_ref[0], at_ref[1]
    nb = c_ref.shape[0]
    k = small_ref.shape[0]
    if ride:
        c_even, c_odd, ce_ref, co_ref, *refs = refs
        half, _, rows, _ = ce_ref.shape
        wide = 2 * half
        for w in range(wide):
            index = w ^ me
            small_ref[w * (k // wide) : (w + 1) * (k // wide)] = take(
                index, c_even, c_odd, slice(nb, nb + k // wide)
            )
            for s in range(n):
                first = pl.multiple_of((z + n - s) % n * each + w * rows, rows)
                coef_ref[pl.ds(first, rows), :] = take(index, ce_ref, co_ref, s)
    else:
        all_small, all_coef, *refs = refs
        small_ref[...] = all_small[...]
        for s in range(n):
            coef_ref[s * each : (s + 1) * each] = all_coef[s]
    corrected = ready_ref[...] - three(split(small_ref[...]), split(c_ref[...]))
    out_ref[...] = -three(split(coef_ref[...]), split(corrected[:nb]))
    total = functools.reduce(jnp.add, [ref[...] for ref in refs])
    for slot in range(1 + total.shape[0] // each):
        piece = corrected[nb:] if slot == 0 else total[(slot - 1) * each : slot * each]
        first = pl.multiple_of(at_ref[1 + slot] * each, each)
        out_ref[pl.ds(first, each), :] += piece


def base(at, ready, c, extra, terms, n, each, ride):
    operands = [ready, c, *extra, *terms]
    k, per = ready.shape
    nb = c.shape[0]
    return pl.pallas_call(
        functools.partial(base_kernel, n, each, ride),
        grid_spec=pltpu.PrefetchScalarGridSpec(
            num_scalar_prefetch=1,
            grid=(1,),
            in_specs=[whole(x.shape) for x in operands],
            out_specs=whole((FB, per)),
            scratch_shapes=[pltpu.VMEM((FB, nb), F32), pltpu.VMEM((k, nb), F32)],
        ),
        out_shape=jax.ShapeDtypeStruct((FB, per), F32),
        compiler_params=params(),
        cost_estimate=LONG,
        name="base",
    )(at, *operands)


def last_kernel(each, at_ref, base_ref, *refs):
    *refs, out_ref, total_ref = refs
    total_ref[...] = base_ref[...]
    total = functools.reduce(jnp.add, [ref[...] for ref in refs])
    first = pl.multiple_of(at_ref[at_ref.shape[0] - 1] * each, each)
    total_ref[pl.ds(first, each), :] += total
    out_ref[...] = total_ref[...].T


def last(at, held, terms, each):
    per = held.shape[1]
    operands = [held, *terms]
    return pl.pallas_call(
        functools.partial(last_kernel, each),
        grid_spec=pltpu.PrefetchScalarGridSpec(
            num_scalar_prefetch=1,
            grid=(1,),
            in_specs=[whole(x.shape) for x in operands],
            out_specs=whole((per, FB)),
            scratch_shapes=[pltpu.VMEM((FB, per), F32)],
        ),
        out_shape=jax.ShapeDtypeStruct((per, FB), F32),
        compiler_params=params(),
        cost_estimate=SHORT,
        name="last",
    )(at, *operands)


def arrivals(n):
    order = []
    for z in range(n):
        found = [(hops, 0) for hops in range(1, n) if z + hops < n]
        found += [(hops, 1) for hops in range(1, n) if z - hops >= 0]
        order.append(sorted(found))
    return [[order[z][slot] for z in range(n)] for slot in range(n - 1)]


def travel(came, held, n, hops, after):
    if hops > 1:
        held = gate(held, *after, cost=LONG)
        came[(hops - 1, 0)], came[(hops - 1, 1)] = held
    pairs = [
        [(p, p - 1) for p in range(1, n - hops + 1)],
        [(p, p + 1) for p in range(hops - 1, n - 1)],
    ]
    held = [lax.ppermute(held[d], "narrow", pairs[d]) for d in (0, 1)]
    came[(hops, 0)], came[(hops, 1)] = held
    return held


def options(came, places, z):
    choices = sorted(set(places))
    which = jnp.int32(0)
    for p, place in enumerate(places):
        which = jnp.where(z == p, choices.index(place), which)
    return [came[choice] for choice in choices], which


def source(places, z):
    value = jnp.int32(0)
    for p, (hops, direction) in enumerate(places):
        value = jnp.where(z == p, p - hops if direction else p + hops, value)
    return value


def swap(x, wide, distance):
    return lax.ppermute(x, "wide", [(i, i ^ distance) for i in range(wide)])


def scatter_terms(even, odd, wide, after=None):
    other = swap(odd, wide, 1)
    if after is not None:
        (other,) = gate([other], after)
    sums = [even[h] + other[h] for h in range(wide // 2)]
    return [sums[0]] + [swap(sums[h], wide, 2 * h) for h in range(1, wide // 2)]


def collect(x, wide, after=()):
    pieces = [swap(x, wide, 2 * h) for h in range(1, wide // 2)]
    if after:
        (x,) = gate([x], *after)
    even = jnp.stack([x, *pieces])
    return even, swap(even, wide, 1)


def on_device(vectors, reflectors, triangle, energies):
    n = lax.axis_size("narrow")
    wide = lax.axis_size("wide")
    z = lax.axis_index("narrow").astype(jnp.int32)
    me = lax.axis_index("wide").astype(jnp.int32).reshape(1)
    each = FB // n
    rows, columns = vectors.shape
    nb = reflectors.shape[1]
    k = nb + each
    per = columns // wide
    blocks = columns // width(columns, wide)
    half = blocks // 2
    e_row = energies.reshape(1, rows)

    own = energies[:, None] * vectors[:, OFF : OFF + each]
    came = {}
    held = travel(came, [own, own], n, 1, [])
    table = arrivals(n)
    at = jnp.stack([me[0], z] + [source(places, z) for places in table])

    fits = per == nb and each % (8 * wide) == 0 and k % (8 * wide) == 0
    ride = (k + each) // wide if fits else 0
    even, odd, left, own_part, small = project(me, vectors, reflectors, e_row, own, wide, ride)
    terms = scatter_terms(even, odd, wide)
    if n > 2:
        held = travel(came, held, n, 2, [left, terms[0]])
    highest = lax.Precision.HIGHEST
    turn = (((1,), (1,)), ((), ()))
    sums, token = early(vectors, left, 0, half, came[(1, 0)], [], wide)
    terms[0] = gate(terms[:1], token)[0]
    projected = functools.reduce(jnp.add, terms)
    coefficients = jnp.dot(triangle, projected[:nb], precision=highest)
    payload = coefficients
    if ride:
        payload = jnp.concatenate([coefficients, projected[nb : nb + k // wide]], axis=0)
    sums, token = early(vectors, left, half, blocks - half, payload, [sums], wide)
    ready = lax.psum_scatter(sums, "wide", scatter_dimension=0)
    c = collect(payload, wide, [token])
    ready_shares = []
    if ride:
        (mine,) = gate([projected[nb + k // wide :]], c[0])
        mine = lax.dot_general(mine, triangle, turn, precision=highest)
        shares = jnp.stack(
            [mine]
            + [
                lax.ppermute(mine, "narrow", [(p, (p + s) % n) for p in range(n)])
                for s in range(1, n)
            ]
        )
        ready_shares = [shares]

    for hops in range(3, n):
        held = travel(came, held, n, hops, [token, *ready_shares])
    after = came[(min(2, n - 1), 0)]
    updated, token = update(me, vectors, reflectors, c, 0, blocks, [after], [], wide)
    if ride:
        share_even, share_odd = collect(shares, wide, [token])
        extra = [*c, share_even, share_odd]
        (token,) = gate([token], share_even)
    else:
        own_part = lax.dot_general(lax.psum(own_part, "wide"), triangle, turn, precision=highest)
        extra = [lax.psum(small, "wide"), lax.all_gather(own_part, "narrow")]
    slots = [options(came, places, z) for places in table]
    even, odd = late(me, updated, slots[:-1], token, wide)
    middle = scatter_terms(even, odd, wide)
    (token,) = gate([token], middle[0], extra[-1])
    even, odd = late(me, updated, slots[-1:], token, wide)
    base_block = base(at, ready, coefficients, extra, middle, n, each, ride)
    tail = scatter_terms(even, odd, wide, base_block)
    return (updated, last(at, base_block, tail, each))


def solution(mesh):
    return jax.shard_map(
        on_device,
        mesh=mesh,
        in_specs=(P("wide", "narrow"), P("wide", None), P(), P("wide")),
        out_specs=(P("wide", "narrow"), P(("narrow", "wide"), None)),
        check_vma=False,
    )
```

```python
import functools

import jax
import jax.numpy as jnp
from jax import lax
from jax.experimental import pallas as pl
from jax.experimental.pallas import tpu as pltpu
from jax.sharding import PartitionSpec as P

FB = 512
OFF = 256
VMEM = 60 * 1024 * 1024

F32 = jnp.float32
BF16 = jnp.bfloat16
LONG = pl.CostEstimate(flops=10**11, bytes_accessed=1024, transcendentals=0)
SHORT = pl.CostEstimate(flops=1024, bytes_accessed=1024, transcendentals=0)


def split(x):
    high = x.astype(BF16)
    return high, (x - high.astype(F32)).astype(BF16)


def mul(left, right):
    return jnp.dot(left, right, preferred_element_type=F32)


def three(left, right):
    (lh, ll), (rh, rl) = left, right
    return mul(lh, rh) + mul(ll, rh) + mul(lh, rl)


def stacked(both, high, right):
    rh, rl = right
    m = high.shape[0]
    top = mul(both, rh)
    return top[:m] + top[m:] + mul(high, rl)


def params():
    return pltpu.CompilerParams(
        dimension_semantics=("arbitrary",), vmem_limit_bytes=VMEM
    )


def width(columns, wide):
    return 256 if columns % 256 == 0 and 256 % (columns // wide) == 0 else columns // wide


def whole(shape):
    return pl.BlockSpec(shape, lambda j, *_: (0,) * len(shape), pipeline_mode=pl.Buffered(1))


ANY = pl.BlockSpec(memory_space=pl.ANY)


def gate_kernel(*refs):
    del refs


def gate(held, *others, cost=SHORT):
    count = len(held)
    return pl.pallas_call(
        gate_kernel,
        in_specs=[ANY] * (count + len(others)),
        out_specs=[ANY] * count,
        out_shape=[jax.ShapeDtypeStruct(x.shape, x.dtype) for x in held],
        input_output_aliases={k: k for k in range(count)},
        cost_estimate=cost,
        name="gate",
    )(*held, *others)


def place(value, index, even_ref, odd_ref, first):
    half = index // 2
    rows = value.shape[0]

    @pl.when(index % 2 == 0)
    def _():
        even_ref[half, first : first + rows] = value

    @pl.when(index % 2 == 1)
    def _():
        odd_ref[half, first : first + rows] = value


def take(index, even_ref, odd_ref, rows):
    half = index // 2
    return jnp.where(index % 2 == 0, even_ref[half, rows], odd_ref[half, rows])


def project_kernel(per, wide, me_ref, v_ref, r_ref, e_ref, x_ref, even_ref, odd_ref, left_ref, own_ref, small_ref, both_ref):
    j = pl.program_id(0)
    nb = r_ref.shape[1]
    each = x_ref.shape[1]
    step = v_ref.shape[1]
    ride = even_ref.shape[1] - nb

    @pl.when(j == 0)
    def _():
        turned = r_ref[...].T
        both_ref[:nb], both_ref[nb:] = split(turned)
        k = nb + each
        left_ref[:nb], left_ref[k : k + nb] = split(turned * e_ref[...])
        left_ref[nb:k], left_ref[k + nb :] = split(x_ref[...].T)
        small = three((left_ref[:k], left_ref[k:]), split(r_ref[...]))
        small_ref[...] = small
        if ride:
            rows = k // wide
            for w in range(wide):
                place(small[w * rows : (w + 1) * rows], w ^ me_ref[0], even_ref, odd_ref, nb)

    value = stacked(both_ref[...], both_ref[:nb], split(v_ref[...]))
    for g in range(step // per):
        index = (j * (step // per) + g) ^ me_ref[0]
        place(value[:, g * per : (g + 1) * per], index, even_ref, odd_ref, 0)

    @pl.when(j == OFF // step)
    def _():
        own = value[:, OFF % step : OFF % step + each].T
        own_ref[...] = own
        if ride:
            rows = each // wide
            for w in range(wide):
                place(
                    own[w * rows : (w + 1) * rows], w ^ me_ref[0], even_ref, odd_ref,
                    nb + ride - rows,
                )


def project(me, vectors, reflectors, e_row, block, wide, ride):
    rows, columns = vectors.shape
    nb = reflectors.shape[1]
    each = block.shape[1]
    k = nb + each
    per = columns // wide
    step = width(columns, wide)
    shapes = [(wide // 2, nb + ride, per)] * 2 + [(2 * k, rows), (each, nb), (k, nb)]
    kinds = [F32, F32, BF16, F32, F32]
    return pl.pallas_call(
        functools.partial(project_kernel, per, wide),
        grid_spec=pltpu.PrefetchScalarGridSpec(
            num_scalar_prefetch=1,
            grid=(columns // step,),
            in_specs=[pl.BlockSpec((rows, step), lambda j, *_: (0, j))]
            + [whole(x) for x in ((rows, nb), (1, rows), block.shape)],
            out_specs=[whole(x) for x in shapes],
            scratch_shapes=[pltpu.VMEM((2 * nb, rows), BF16)],
        ),
        out_shape=[jax.ShapeDtypeStruct(x, kind) for x, kind in zip(shapes, kinds)],
        compiler_params=params(),
        cost_estimate=SHORT,
        name="project",
    )(me, vectors, reflectors, e_row, block)


def early_kernel(per, v_ref, left_ref, *refs):
    out_ref, token_ref = refs[-2:]
    k = left_ref.shape[0] // 2
    token_ref[...] = jnp.zeros_like(token_ref)
    value = stacked(left_ref[...], left_ref[:k], split(v_ref[...]))
    for g in range(v_ref.shape[1] // per):
        out_ref[g] = value[:, g * per : (g + 1) * per]


def early(vectors, left, offset, blocks, after, before, wide):
    rows, columns = vectors.shape
    per = columns // wide
    step = width(columns, wide)
    count = step // per
    k = left.shape[0] // 2
    operands = [vectors, left, after] + before
    return pl.pallas_call(
        functools.partial(early_kernel, per),
        grid=(blocks,),
        in_specs=[pl.BlockSpec((rows, step), lambda j: (0, j + offset)), whole(left.shape)]
        + [ANY] * (len(operands) - 2),
        out_specs=[
            pl.BlockSpec((count, k, per), lambda j: (j + offset, 0, 0)),
            whole((8, 128)),
        ],
        out_shape=[
            jax.ShapeDtypeStruct((wide, k, per), F32),
            jax.ShapeDtypeStruct((8, 128), F32),
        ],
        input_output_aliases={3: 0} if before else {},
        compiler_params=params(),
        cost_estimate=SHORT,
        name="early",
    )(*operands)


def update_kernel(me_ref, v_ref, r_ref, even_ref, odd_ref, after_ref, out_ref, token_ref, right_ref):
    nb = r_ref.shape[1]
    per = even_ref.shape[2]

    @pl.when(pl.program_id(0) == 0)
    def _():
        token_ref[...] = jnp.zeros_like(token_ref)
        for w in range(2 * even_ref.shape[0]):
            high, low = split(take(w ^ me_ref[0], even_ref, odd_ref, slice(0, nb)))
            here = slice(w * per, (w + 1) * per)
            right_ref[:nb, here] = high
            right_ref[nb : 2 * nb, here] = high
            right_ref[2 * nb :, here] = low

    high, low = split(r_ref[...])
    left = jnp.concatenate([high, low, high], axis=1)
    out_ref[...] = v_ref[...] - mul(left, right_ref[...])


def update(me, vectors, reflectors, c, after):
    rows, columns = vectors.shape
    nb = reflectors.shape[1]
    count = next(x for x in range(4, rows) if rows % (16 * x) == 0)
    rows_of = pl.BlockSpec((rows // count, columns), lambda j, *_: (j, 0))
    return pl.pallas_call(
        update_kernel,
        grid_spec=pltpu.PrefetchScalarGridSpec(
            num_scalar_prefetch=1,
            grid=(count,),
            in_specs=[rows_of, pl.BlockSpec((rows // count, nb), lambda j, *_: (j, 0))]
            + [whole(x.shape) for x in c]
            + [ANY],
            out_specs=[rows_of, whole((8, 128))],
            scratch_shapes=[pltpu.VMEM((3 * nb, columns), BF16)],
        ),
        out_shape=[
            jax.ShapeDtypeStruct(vectors.shape, F32),
            jax.ShapeDtypeStruct((8, 128), F32),
        ],
        compiler_params=params(),
        cost_estimate=SHORT,
        name="update",
    )(me, vectors, reflectors, *c, after)


def late_kernel(per, counts, at_ref, u_ref, after_ref, *refs):
    *refs, even_out, odd_out, both_ref, block_ref, sem_ref = refs
    j = pl.program_id(0)
    m = both_ref.shape[0] // 2
    each = block_ref.shape[2]

    @pl.when(j == 0)
    def _():
        first = 0
        for s, count in enumerate(counts):
            for k, ref in enumerate(refs[first : first + count]):

                @pl.when(at_ref[1 + s] == k)
                def _(ref=ref, s=s):
                    pltpu.make_async_copy(ref, block_ref.at[s], sem_ref.at[s]).start()

            first += count
        for s in range(len(counts)):
            pltpu.make_async_copy(block_ref.at[s], block_ref.at[s], sem_ref.at[s]).wait()
            high, low = split(block_ref[s].T)
            both_ref[s * each : (s + 1) * each] = high
            both_ref[m + s * each : m + (s + 1) * each] = low

    value = stacked(both_ref[...], both_ref[:m], split(u_ref[...]))
    count = u_ref.shape[1] // per
    for g in range(count):
        index = (j * count + g) ^ at_ref[0]
        place(value[:, g * per : (g + 1) * per], index, even_out, odd_out, 0)


def late(me, updated, slots, after, wide):
    rows, columns = updated.shape
    per = columns // wide
    step = width(columns, wide)
    flat = [x for choices, _ in slots for x in choices]
    counts = [len(choices) for choices, _ in slots]
    each = flat[0].shape[1]
    m = each * len(slots)
    at = jnp.stack([me[0]] + [which.astype(jnp.int32) for _, which in slots])
    half = jax.ShapeDtypeStruct((wide // 2, m, per), F32)
    return pl.pallas_call(
        functools.partial(late_kernel, per, counts),
        grid_spec=pltpu.PrefetchScalarGridSpec(
            num_scalar_prefetch=1,
            grid=(columns // step,),
            in_specs=[pl.BlockSpec((rows, step), lambda j, *_: (0, j))] + [ANY] * (1 + len(flat)),
            out_specs=[whole(half.shape)] * 2,
            scratch_shapes=[
                pltpu.VMEM((2 * m, rows), BF16),
                pltpu.VMEM((len(slots), rows, each), F32),
                pltpu.SemaphoreType.DMA((len(slots),)),
            ],
        ),
        out_shape=[half, half],
        compiler_params=params(),
        cost_estimate=SHORT,
        name="late",
    )(at, updated, after, *flat)


def total_kernel(*refs):
    refs[-1][...] = functools.reduce(jnp.add, [ref[...] for ref in refs[:-1]])


def total(terms):
    shape = terms[0].shape
    return pl.pallas_call(
        total_kernel,
        grid=(1,),
        in_specs=[pl.BlockSpec(shape, lambda j: (0, 0))] * len(terms),
        out_specs=pl.BlockSpec(shape, lambda j: (0, 0)),
        out_shape=jax.ShapeDtypeStruct(shape, F32),
        compiler_params=params(),
        cost_estimate=LONG,
        name="total",
    )(*terms)


def base_kernel(n, each, ride, at_ref, ready_ref, c_ref, *refs):
    *refs, out_ref, coef_ref, small_ref = refs
    me, z = at_ref[0], at_ref[1]
    nb = c_ref.shape[0]
    k = small_ref.shape[0]
    if ride:
        c_even, c_odd, ce_ref, co_ref = refs[1:]
        half, _, rows, _ = ce_ref.shape
        wide = 2 * half
        for w in range(wide):
            index = w ^ me
            small_ref[w * (k // wide) : (w + 1) * (k // wide)] = take(
                index, c_even, c_odd, slice(nb, nb + k // wide)
            )
            for s in range(n):
                first = pl.multiple_of((z + n - s) % n * each + w * rows, rows)
                coef_ref[pl.ds(first, rows), :] = take(index, ce_ref, co_ref, s)
    else:
        all_small, all_coef = refs[1:]
        small_ref[...] = all_small[...]
        for s in range(n):
            coef_ref[s * each : (s + 1) * each] = all_coef[s]
    corrected = ready_ref[...] - three(split(small_ref[...]), split(c_ref[...]))
    out_ref[...] = -three(split(coef_ref[...]), split(corrected[:nb]))
    total = refs[0]
    for slot in range(1 + total.shape[0] // each):
        piece = corrected[nb:] if slot == 0 else total[(slot - 1) * each : slot * each]
        first = pl.multiple_of(at_ref[1 + slot] * each, each)
        out_ref[pl.ds(first, each), :] += piece


def base(at, ready, c, middle, extra, n, each, ride):
    operands = [ready, c, middle, *extra]
    k, per = ready.shape
    nb = c.shape[0]
    return pl.pallas_call(
        functools.partial(base_kernel, n, each, ride),
        grid_spec=pltpu.PrefetchScalarGridSpec(
            num_scalar_prefetch=1,
            grid=(1,),
            in_specs=[whole(x.shape) for x in operands],
            out_specs=whole((FB, per)),
            scratch_shapes=[pltpu.VMEM((FB, nb), F32), pltpu.VMEM((k, nb), F32)],
        ),
        out_shape=jax.ShapeDtypeStruct((FB, per), F32),
        compiler_params=params(),
        cost_estimate=LONG,
        name="base",
    )(at, *operands)


def last_kernel(each, at_ref, base_ref, *refs):
    *refs, out_ref, total_ref = refs
    total_ref[...] = base_ref[...]
    total = functools.reduce(jnp.add, [ref[...] for ref in refs])
    first = pl.multiple_of(at_ref[at_ref.shape[0] - 1] * each, each)
    total_ref[pl.ds(first, each), :] += total
    out_ref[...] = total_ref[...].T


def last(at, held, terms, each):
    per = held.shape[1]
    operands = [held, *terms]
    return pl.pallas_call(
        functools.partial(last_kernel, each),
        grid_spec=pltpu.PrefetchScalarGridSpec(
            num_scalar_prefetch=1,
            grid=(1,),
            in_specs=[whole(x.shape) for x in operands],
            out_specs=whole((per, FB)),
            scratch_shapes=[pltpu.VMEM((FB, per), F32)],
        ),
        out_shape=jax.ShapeDtypeStruct((per, FB), F32),
        compiler_params=params(),
        cost_estimate=SHORT,
        name="last",
    )(at, *operands)


def arrivals(n):
    order = []
    for z in range(n):
        found = [(hops, 0) for hops in range(1, n) if z + hops < n]
        found += [(hops, 1) for hops in range(1, n) if z - hops >= 0]
        order.append(sorted(found))
    return [[order[z][slot] for z in range(n)] for slot in range(n - 1)]


def travel(came, held, n, hops, after):
    if hops > 1:
        held = gate(held, *after, cost=LONG)
        came[(hops - 1, 0)], came[(hops - 1, 1)] = held
    pairs = [
        [(p, p - 1) for p in range(1, n - hops + 1)],
        [(p, p + 1) for p in range(hops - 1, n - 1)],
    ]
    held = [lax.ppermute(held[d], "narrow", pairs[d]) for d in (0, 1)]
    came[(hops, 0)], came[(hops, 1)] = held
    return held


def options(came, places, z):
    choices = sorted(set(places))
    which = jnp.int32(0)
    for p, place in enumerate(places):
        which = jnp.where(z == p, choices.index(place), which)
    return [came[choice] for choice in choices], which


def source(places, z):
    value = jnp.int32(0)
    for p, (hops, direction) in enumerate(places):
        value = jnp.where(z == p, p - hops if direction else p + hops, value)
    return value


def swap(x, wide, distance):
    return lax.ppermute(x, "wide", [(i, i ^ distance) for i in range(wide)])


def scatter_terms(even, odd, wide, after=None):
    other = swap(odd, wide, 1)
    if after is not None:
        (other,) = gate([other], after)
    sums = [even[h] + other[h] for h in range(wide // 2)]
    return [sums[0]] + [swap(sums[h], wide, 2 * h) for h in range(1, wide // 2)]


def collect(x, wide, after=()):
    pieces = [swap(x, wide, 2 * h) for h in range(1, wide // 2)]
    if after:
        (x,) = gate([x], *after)
    even = jnp.stack([x, *pieces])
    return even, swap(even, wide, 1)


def on_device(vectors, reflectors, triangle, energies):
    n = lax.axis_size("narrow")
    wide = lax.axis_size("wide")
    z = lax.axis_index("narrow").astype(jnp.int32)
    me = lax.axis_index("wide").astype(jnp.int32).reshape(1)
    each = FB // n
    rows, columns = vectors.shape
    nb = reflectors.shape[1]
    k = nb + each
    per = columns // wide
    blocks = columns // width(columns, wide)
    half = blocks // 2
    e_row = energies.reshape(1, rows)

    own = energies[:, None] * vectors[:, OFF : OFF + each]
    came = {}
    held = travel(came, [own, own], n, 1, [])
    table = arrivals(n)
    at = jnp.stack([me[0], z] + [source(places, z) for places in table])

    fits = per == nb and each % (8 * wide) == 0 and k % (8 * wide) == 0
    ride = (k + each) // wide if fits else 0
    even, odd, left, own_part, small = project(me, vectors, reflectors, e_row, own, wide, ride)
    terms = scatter_terms(even, odd, wide)
    highest = lax.Precision.HIGHEST
    turn = (((1,), (1,)), ((), ()))
    if n > 2:
        held = travel(came, held, n, 2, [left, terms[0]])
    sums, token = early(vectors, left, 0, half, came[(1, 0)], [], wide)
    terms[0] = gate(terms[:1], token)[0]
    projected = functools.reduce(jnp.add, terms)
    coefficients = jnp.dot(triangle, projected[:nb], precision=highest)
    payload = coefficients
    if ride:
        payload = jnp.concatenate([coefficients, projected[nb : nb + k // wide]], axis=0)
    sums, token = early(vectors, left, half, blocks - half, payload, [sums], wide)
    ready = lax.psum_scatter(sums, "wide", scatter_dimension=0)
    c = collect(payload, wide, [token])
    for hops in range(3, n):
        held = travel(came, held, n, hops, [token])
    after = came[(min(2, n - 1), 0)]
    updated, token = update(me, vectors, reflectors, c, after)

    if ride:
        (mine,) = gate([projected[nb + k // wide :]], after)
        mine = lax.dot_general(mine, triangle, turn, precision=highest)
        shares = [
            lax.ppermute(mine, "narrow", [(p, (p + s) % n) for p in range(n)]) for s in range(1, n)
        ]
        shares = jnp.stack([*gate([mine], token), *shares])
        token = shares
    slots = [options(came, places, z) for places in table]
    even, odd = late(me, updated, slots[:-1], token, wide)
    if ride:
        extra = [*c, *collect(shares, wide, [even])]
        token = extra[-2]
    else:
        own_part = lax.dot_general(lax.psum(own_part, "wide"), triangle, turn, precision=highest)
        extra = [lax.psum(small, "wide"), lax.all_gather(own_part, "narrow")]
    middle = scatter_terms(even, odd, wide)
    (ready,) = gate([ready], middle[0], token)
    even, odd = late(me, updated, slots[-1:], ready, wide)
    middle = total(middle)
    tail = scatter_terms(even, odd, wide, middle)
    (ready,) = gate([ready], tail[0])
    base_block = base(at, ready, coefficients, middle, extra, n, each, ride)
    return (updated, last(at, base_block, tail, each))


def solution(mesh):
    return jax.shard_map(
        on_device,
        mesh=mesh,
        in_specs=(P("wide", "narrow"), P("wide", None), P(), P("wide")),
        out_specs=(P("wide", "narrow"), P(("narrow", "wide"), None)),
        check_vma=False,
    )
```

```python
import functools

import jax
import jax.numpy as jnp
from jax import lax
from jax.experimental import pallas as pl
from jax.experimental.pallas import tpu as pltpu
from jax.sharding import PartitionSpec as P

FB = 512
OFF = 256
VMEM = 60 * 1024 * 1024

F32 = jnp.float32
BF16 = jnp.bfloat16
LONG = pl.CostEstimate(flops=10**11, bytes_accessed=1024, transcendentals=0)
SHORT = pl.CostEstimate(flops=1024, bytes_accessed=1024, transcendentals=0)


def split(x):
    high = x.astype(BF16)
    return high, (x - high.astype(F32)).astype(BF16)


def mul(left, right):
    return jnp.dot(left, right, preferred_element_type=F32)


def three(left, right):
    (lh, ll), (rh, rl) = left, right
    return mul(lh, rh) + mul(ll, rh) + mul(lh, rl)


def stacked(both, high, right):
    rh, rl = right
    m = high.shape[0]
    top = mul(both, rh)
    return top[:m] + top[m:] + mul(high, rl)


def params():
    return pltpu.CompilerParams(
        dimension_semantics=("arbitrary",), vmem_limit_bytes=VMEM
    )


def width(columns, wide):
    return 256 if columns % 256 == 0 and 256 % (columns // wide) == 0 else columns // wide


def whole(shape):
    return pl.BlockSpec(shape, lambda j, *_: (0,) * len(shape), pipeline_mode=pl.Buffered(1))


ANY = pl.BlockSpec(memory_space=pl.ANY)


def gate_kernel(*refs):
    del refs


def gate(held, *others, cost=SHORT):
    count = len(held)
    return pl.pallas_call(
        gate_kernel,
        in_specs=[ANY] * (count + len(others)),
        out_specs=[ANY] * count,
        out_shape=[jax.ShapeDtypeStruct(x.shape, x.dtype) for x in held],
        input_output_aliases={k: k for k in range(count)},
        cost_estimate=cost,
        name="gate",
    )(*held, *others)


def place(value, index, even_ref, odd_ref, first):
    half = index // 2
    rows = value.shape[0]

    @pl.when(index % 2 == 0)
    def _():
        even_ref[half, first : first + rows] = value

    @pl.when(index % 2 == 1)
    def _():
        odd_ref[half, first : first + rows] = value


def take(index, even_ref, odd_ref, rows):
    half = index // 2
    return jnp.where(index % 2 == 0, even_ref[half, rows], odd_ref[half, rows])


def project_kernel(per, wide, me_ref, v_ref, r_ref, e_ref, x_ref, even_ref, odd_ref, left_ref, small_ref, both_ref):
    j = pl.program_id(0)
    nb = r_ref.shape[1]
    each = x_ref.shape[1]
    step = v_ref.shape[1]
    ride = even_ref.shape[1] - nb

    @pl.when(j == 0)
    def _():
        turned = r_ref[...].T
        both_ref[:nb], both_ref[nb:] = split(turned)
        k = nb + each
        left_ref[:nb], left_ref[k : k + nb] = split(turned * e_ref[...])
        left_ref[nb:k], left_ref[k + nb :] = split(x_ref[...].T)
        small = three((left_ref[:k], left_ref[k:]), split(r_ref[...]))
        small_ref[...] = small
        if ride:
            rows = k // wide
            for w in range(wide):
                place(small[w * rows : (w + 1) * rows], w ^ me_ref[0], even_ref, odd_ref, nb)

    value = stacked(both_ref[...], both_ref[:nb], split(v_ref[...]))
    for g in range(step // per):
        index = (j * (step // per) + g) ^ me_ref[0]
        place(value[:, g * per : (g + 1) * per], index, even_ref, odd_ref, 0)


def project(me, vectors, reflectors, e_row, block, wide, ride):
    rows, columns = vectors.shape
    nb = reflectors.shape[1]
    each = block.shape[1]
    k = nb + each
    per = columns // wide
    step = width(columns, wide)
    shapes = [(wide // 2, nb + ride, per)] * 2 + [(2 * k, rows), (k, nb)]
    kinds = [F32, F32, BF16, F32]
    return pl.pallas_call(
        functools.partial(project_kernel, per, wide),
        grid_spec=pltpu.PrefetchScalarGridSpec(
            num_scalar_prefetch=1,
            grid=(columns // step,),
            in_specs=[pl.BlockSpec((rows, step), lambda j, *_: (0, j))]
            + [whole(x) for x in ((rows, nb), (1, rows), block.shape)],
            out_specs=[whole(x) for x in shapes],
            scratch_shapes=[pltpu.VMEM((2 * nb, rows), BF16)],
        ),
        out_shape=[jax.ShapeDtypeStruct(x, kind) for x, kind in zip(shapes, kinds)],
        compiler_params=params(),
        cost_estimate=SHORT,
        name="project",
    )(me, vectors, reflectors, e_row, block)


def early_kernel(per, v_ref, left_ref, *refs):
    out_ref, token_ref = refs[-2:]
    k = left_ref.shape[0] // 2
    token_ref[...] = jnp.zeros_like(token_ref)
    value = stacked(left_ref[...], left_ref[:k], split(v_ref[...]))
    for g in range(v_ref.shape[1] // per):
        out_ref[g] = value[:, g * per : (g + 1) * per]


def early(vectors, left, offset, blocks, after, before, wide):
    rows, columns = vectors.shape
    per = columns // wide
    step = width(columns, wide)
    count = step // per
    k = left.shape[0] // 2
    operands = [vectors, left, after] + before
    return pl.pallas_call(
        functools.partial(early_kernel, per),
        grid=(blocks,),
        in_specs=[pl.BlockSpec((rows, step), lambda j: (0, j + offset)), whole(left.shape)]
        + [ANY] * (len(operands) - 2),
        out_specs=[
            pl.BlockSpec((count, k, per), lambda j: (j + offset, 0, 0)),
            whole((8, 128)),
        ],
        out_shape=[
            jax.ShapeDtypeStruct((wide, k, per), F32),
            jax.ShapeDtypeStruct((8, 128), F32),
        ],
        input_output_aliases={3: 0} if before else {},
        compiler_params=params(),
        cost_estimate=SHORT,
        name="early",
    )(*operands)


def update_kernel(me_ref, v_ref, r_ref, even_ref, odd_ref, after_ref, out_ref, token_ref, right_ref):
    nb = r_ref.shape[1]
    per = even_ref.shape[2]

    @pl.when(pl.program_id(0) == 0)
    def _():
        token_ref[...] = jnp.zeros_like(token_ref)
        for w in range(2 * even_ref.shape[0]):
            high, low = split(take(w ^ me_ref[0], even_ref, odd_ref, slice(0, nb)))
            here = slice(w * per, (w + 1) * per)
            right_ref[:nb, here] = high
            right_ref[nb : 2 * nb, here] = high
            right_ref[2 * nb :, here] = low

    high, low = split(r_ref[...])
    left = jnp.concatenate([high, low, high], axis=1)
    out_ref[...] = v_ref[...] - mul(left, right_ref[...])


def update(me, vectors, reflectors, c, after):
    rows, columns = vectors.shape
    nb = reflectors.shape[1]
    count = next(x for x in range(4, rows) if rows % (16 * x) == 0)
    rows_of = pl.BlockSpec((rows // count, columns), lambda j, *_: (j, 0))
    return pl.pallas_call(
        update_kernel,
        grid_spec=pltpu.PrefetchScalarGridSpec(
            num_scalar_prefetch=1,
            grid=(count,),
            in_specs=[rows_of, pl.BlockSpec((rows // count, nb), lambda j, *_: (j, 0))]
            + [whole(x.shape) for x in c]
            + [ANY],
            out_specs=[rows_of, whole((8, 128))],
            scratch_shapes=[pltpu.VMEM((3 * nb, columns), BF16)],
        ),
        out_shape=[
            jax.ShapeDtypeStruct(vectors.shape, F32),
            jax.ShapeDtypeStruct((8, 128), F32),
        ],
        compiler_params=params(),
        cost_estimate=SHORT,
        name="update",
    )(me, vectors, reflectors, *c, after)


def late_kernel(per, counts, at_ref, u_ref, after_ref, *refs):
    *refs, even_out, odd_out, both_ref, block_ref, sem_ref = refs
    j = pl.program_id(0)
    m = both_ref.shape[0] // 2
    each = block_ref.shape[2]

    @pl.when(j == 0)
    def _():
        first = 0
        for s, count in enumerate(counts):
            for k, ref in enumerate(refs[first : first + count]):

                @pl.when(at_ref[1 + s] == k)
                def _(ref=ref, s=s):
                    pltpu.make_async_copy(ref, block_ref.at[s], sem_ref.at[s]).start()

            first += count
        for s in range(len(counts)):
            pltpu.make_async_copy(block_ref.at[s], block_ref.at[s], sem_ref.at[s]).wait()
            high, low = split(block_ref[s].T)
            both_ref[s * each : (s + 1) * each] = high
            both_ref[m + s * each : m + (s + 1) * each] = low

    value = stacked(both_ref[...], both_ref[:m], split(u_ref[...]))
    count = u_ref.shape[1] // per
    for g in range(count):
        index = (j * count + g) ^ at_ref[0]
        place(value[:, g * per : (g + 1) * per], index, even_out, odd_out, 0)


def late(me, updated, slots, after, wide):
    rows, columns = updated.shape
    per = columns // wide
    step = width(columns, wide)
    flat = [x for choices, _ in slots for x in choices]
    counts = [len(choices) for choices, _ in slots]
    each = flat[0].shape[1]
    m = each * len(slots)
    at = jnp.stack([me[0]] + [which.astype(jnp.int32) for _, which in slots])
    half = jax.ShapeDtypeStruct((wide // 2, m, per), F32)
    return pl.pallas_call(
        functools.partial(late_kernel, per, counts),
        grid_spec=pltpu.PrefetchScalarGridSpec(
            num_scalar_prefetch=1,
            grid=(columns // step,),
            in_specs=[pl.BlockSpec((rows, step), lambda j, *_: (0, j))] + [ANY] * (1 + len(flat)),
            out_specs=[whole(half.shape)] * 2,
            scratch_shapes=[
                pltpu.VMEM((2 * m, rows), BF16),
                pltpu.VMEM((len(slots), rows, each), F32),
                pltpu.SemaphoreType.DMA((len(slots),)),
            ],
        ),
        out_shape=[half, half],
        compiler_params=params(),
        cost_estimate=SHORT,
        name="late",
    )(at, updated, after, *flat)


def own_kernel(me_ref, even_ref, odd_ref, after_ref, out_ref):
    each, nb = out_ref.shape
    per = even_ref.shape[2]
    block = take((OFF // per) ^ me_ref[0], even_ref, odd_ref, slice(0, nb))
    out_ref[...] = block[:, OFF % per : OFF % per + each].T


def own_columns(me, c, after, nb, each):
    return pl.pallas_call(
        own_kernel,
        grid_spec=pltpu.PrefetchScalarGridSpec(
            num_scalar_prefetch=1,
            grid=(1,),
            in_specs=[whole(x.shape) for x in c] + [ANY],
            out_specs=whole((each, nb)),
        ),
        out_shape=jax.ShapeDtypeStruct((each, nb), F32),
        compiler_params=params(),
        cost_estimate=SHORT,
        name="own_columns",
    )(me, *c, after)


def base_kernel(n, each, ride, at_ref, ready_ref, c_ref, *refs):
    *refs, out_ref, coef_ref, small_ref = refs
    me, z = at_ref[0], at_ref[1]
    nb = c_ref.shape[0]
    k = small_ref.shape[0]
    for s in range(n):
        first = pl.multiple_of((z + n - s) % n * each, each)
        coef_ref[pl.ds(first, each), :] = refs[s][...]
    if ride:
        wide = 2 * refs[n].shape[0]
        for w in range(wide):
            small_ref[w * (k // wide) : (w + 1) * (k // wide)] = take(
                w ^ me, *refs[n:], slice(nb, nb + k // wide)
            )
    else:
        small_ref[...] = refs[n][...]
    corrected = ready_ref[...] - three(split(small_ref[...]), split(c_ref[...]))
    out_ref[...] = -three(split(coef_ref[...]), split(corrected[:nb]))
    out_ref[pl.ds(pl.multiple_of(z * each, each), each), :] += corrected[nb:]


def base(at, ready, c, coef, small, n, each, ride):
    operands = [ready, c, *coef, *small]
    k, per = ready.shape
    nb = c.shape[0]
    return pl.pallas_call(
        functools.partial(base_kernel, n, each, ride),
        grid_spec=pltpu.PrefetchScalarGridSpec(
            num_scalar_prefetch=1,
            grid=(1,),
            in_specs=[whole(x.shape) for x in operands],
            out_specs=whole((FB, per)),
            scratch_shapes=[pltpu.VMEM((FB, nb), F32), pltpu.VMEM((k, nb), F32)],
        ),
        out_shape=jax.ShapeDtypeStruct((FB, per), F32),
        compiler_params=params(),
        cost_estimate=LONG,
        name="base",
    )(at, *operands)


def last_kernel(each, at_ref, base_ref, *refs):
    *refs, out_ref, total_ref = refs
    total_ref[...] = base_ref[...]
    total = functools.reduce(jnp.add, [ref[...] for ref in refs])
    for slot in range(total.shape[0] // each):
        first = pl.multiple_of(at_ref[2 + slot] * each, each)
        total_ref[pl.ds(first, each), :] += total[slot * each : (slot + 1) * each]
    out_ref[...] = total_ref[...].T


def last(at, held, terms, each):
    per = held.shape[1]
    operands = [held, *terms]
    return pl.pallas_call(
        functools.partial(last_kernel, each),
        grid_spec=pltpu.PrefetchScalarGridSpec(
            num_scalar_prefetch=1,
            grid=(1,),
            in_specs=[whole(x.shape) for x in operands],
            out_specs=whole((per, FB)),
            scratch_shapes=[pltpu.VMEM((FB, per), F32)],
        ),
        out_shape=jax.ShapeDtypeStruct((per, FB), F32),
        compiler_params=params(),
        cost_estimate=SHORT,
        name="last",
    )(at, *operands)


def arrivals(n):
    order = []
    for z in range(n):
        found = [(hops, 0) for hops in range(1, n) if z + hops < n]
        found += [(hops, 1) for hops in range(1, n) if z - hops >= 0]
        order.append(sorted(found))
    return [[order[z][slot] for z in range(n)] for slot in range(n - 1)]


def travel(came, held, n, hops, after):
    if hops > 1:
        held = gate(held, *after, cost=LONG)
        came[(hops - 1, 0)], came[(hops - 1, 1)] = held
    pairs = [
        [(p, p - 1) for p in range(1, n - hops + 1)],
        [(p, p + 1) for p in range(hops - 1, n - 1)],
    ]
    held = [lax.ppermute(held[d], "narrow", pairs[d]) for d in (0, 1)]
    came[(hops, 0)], came[(hops, 1)] = held
    return held


def options(came, places, z):
    choices = sorted(set(places))
    which = jnp.int32(0)
    for p, place in enumerate(places):
        which = jnp.where(z == p, choices.index(place), which)
    return [came[choice] for choice in choices], which


def source(places, z):
    value = jnp.int32(0)
    for p, (hops, direction) in enumerate(places):
        value = jnp.where(z == p, p - hops if direction else p + hops, value)
    return value


def swap(x, wide, distance):
    return lax.ppermute(x, "wide", [(i, i ^ distance) for i in range(wide)])


def scatter_terms(even, odd, wide, after=None):
    other = swap(odd, wide, 1)
    if after is not None:
        (other,) = gate([other], after)
    sums = [even[h] + other[h] for h in range(wide // 2)]
    return [sums[0]] + [swap(sums[h], wide, 2 * h) for h in range(1, wide // 2)]


def collect(x, wide, after=()):
    pieces = [swap(x, wide, 2 * h) for h in range(1, wide // 2)]
    if after:
        (x,) = gate([x], *after)
    even = jnp.stack([x, *pieces])
    return even, swap(even, wide, 1)


def on_device(vectors, reflectors, triangle, energies):
    n = lax.axis_size("narrow")
    wide = lax.axis_size("wide")
    z = lax.axis_index("narrow").astype(jnp.int32)
    me = lax.axis_index("wide").astype(jnp.int32).reshape(1)
    each = FB // n
    rows, columns = vectors.shape
    nb = reflectors.shape[1]
    k = nb + each
    per = columns // wide
    blocks = columns // width(columns, wide)
    half = blocks // 2
    e_row = energies.reshape(1, rows)

    own = energies[:, None] * vectors[:, OFF : OFF + each]
    came = {}
    held = travel(came, [own, own], n, 1, [])
    table = arrivals(n)
    at = jnp.stack([me[0], z] + [source(places, z) for places in table])

    ride = k // wide if per == nb and k % (8 * wide) == 0 else 0
    even, odd, left, small = project(me, vectors, reflectors, e_row, own, wide, ride)
    terms = scatter_terms(even, odd, wide)
    highest = lax.Precision.HIGHEST
    if n > 2:
        held = travel(came, held, n, 2, [left, terms[0]])
    sums, token = early(vectors, left, 0, half, came[(1, 0)], [], wide)
    terms[0] = gate(terms[:1], token)[0]
    projected = functools.reduce(jnp.add, terms)
    coefficients = jnp.dot(triangle, projected[:nb], precision=highest)
    payload = coefficients
    if ride:
        payload = jnp.concatenate([coefficients, projected[nb:]], axis=0)
    sums, token = early(vectors, left, half, blocks - half, payload, [sums], wide)
    ready = lax.psum_scatter(sums, "wide", scatter_dimension=0)
    c = collect(payload, wide, [token])
    for hops in range(3, n):
        held = travel(came, held, n, hops, [token, c[0]])
    after = came[(min(2, n - 1), 0)]
    updated, token = update(me, vectors, reflectors, c, after)

    mine = own_columns(me, c, token, nb, each)
    coef = [mine] + [
        lax.ppermute(mine, "narrow", [(p, (p + s) % n) for p in range(n)]) for s in range(1, n)
    ]
    slots = [options(came, places, z) for places in table]
    even, odd = late(me, updated, slots, token, wide)
    (odd,) = gate([odd], ready, *coef[1:])
    tail = scatter_terms(even, odd, wide)
    (ready,) = gate([ready], tail[0])
    small = c if ride else [lax.psum(small, "wide")]
    base_block = base(at, ready, coefficients, coef, small, n, each, ride)
    return (updated, last(at, base_block, tail, each))


def solution(mesh):
    return jax.shard_map(
        on_device,
        mesh=mesh,
        in_specs=(P("wide", "narrow"), P("wide", None), P(), P("wide")),
        out_specs=(P("wide", "narrow"), P(("narrow", "wide"), None)),
        check_vma=False,
    )
```

```python
import functools

import jax
import jax.numpy as jnp
from jax import lax
from jax.experimental import pallas as pl
from jax.experimental.pallas import tpu as pltpu
from jax.sharding import PartitionSpec as P

FB = 512
OFF = 256
VMEM = 60 * 1024 * 1024

F32 = jnp.float32
BF16 = jnp.bfloat16
LONG = pl.CostEstimate(flops=10**11, bytes_accessed=1024, transcendentals=0)
SHORT = pl.CostEstimate(flops=1024, bytes_accessed=1024, transcendentals=0)


def split(x):
    high = x.astype(BF16)
    return high, (x - high.astype(F32)).astype(BF16)


def mul(left, right):
    return jnp.dot(left, right, preferred_element_type=F32)


def three(left, right):
    (lh, ll), (rh, rl) = left, right
    return mul(lh, rh) + mul(ll, rh) + mul(lh, rl)


def stacked(both, high, right):
    rh, rl = right
    m = high.shape[0]
    top = mul(both, rh)
    return top[:m] + top[m:] + mul(high, rl)


def params():
    return pltpu.CompilerParams(
        dimension_semantics=("arbitrary",), vmem_limit_bytes=VMEM
    )


def width(columns, wide):
    return 256 if columns % 256 == 0 and 256 % (columns // wide) == 0 else columns // wide


def whole(shape):
    return pl.BlockSpec(shape, lambda j, *_: (0,) * len(shape), pipeline_mode=pl.Buffered(1))


ANY = pl.BlockSpec(memory_space=pl.ANY)


def gate_kernel(*refs):
    del refs


def gate(held, *others, cost=SHORT):
    count = len(held)
    return pl.pallas_call(
        gate_kernel,
        in_specs=[ANY] * (count + len(others)),
        out_specs=[ANY] * count,
        out_shape=[jax.ShapeDtypeStruct(x.shape, x.dtype) for x in held],
        input_output_aliases={k: k for k in range(count)},
        cost_estimate=cost,
        name="gate",
    )(*held, *others)


def place(value, index, even_ref, odd_ref, first):
    half = index // 2
    rows = value.shape[0]

    @pl.when(index % 2 == 0)
    def _():
        even_ref[half, first : first + rows] = value

    @pl.when(index % 2 == 1)
    def _():
        odd_ref[half, first : first + rows] = value


def take(index, even_ref, odd_ref, rows):
    half = index // 2
    return jnp.where(index % 2 == 0, even_ref[half, rows], odd_ref[half, rows])


def project_kernel(per, wide, me_ref, v_ref, r_ref, e_ref, x_ref, even_ref, odd_ref, sums_ref, small_ref, both_ref):
    j = pl.program_id(0)
    nb = r_ref.shape[1]
    m = both_ref.shape[0] // 2
    k = m - nb
    ride = even_ref.shape[1] - nb

    @pl.when(j == 0)
    def _():
        turned = r_ref[...].T
        first = 0
        for part in (turned, turned * e_ref[...], x_ref[...].T):
            end = first + part.shape[0]
            both_ref[first:end], both_ref[m + first : m + end] = split(part)
            first = end
        small = three((both_ref[nb:m], both_ref[m + nb :]), split(r_ref[...]))
        small_ref[...] = small
        if ride:
            for w in range(wide):
                share = small[w * ride : (w + 1) * ride]
                place(share, w ^ me_ref[0], even_ref, odd_ref, nb)

    value = stacked(both_ref[...], both_ref[:m], split(v_ref[...]))
    count = v_ref.shape[1] // per
    for g in range(count):
        part = value[:, g * per : (g + 1) * per]
        place(part[:nb], (j * count + g) ^ me_ref[0], even_ref, odd_ref, 0)
        sums_ref[g] = part[nb:]


def project(me, vectors, reflectors, e_row, block, wide, ride):
    rows, columns = vectors.shape
    nb = reflectors.shape[1]
    k = nb + block.shape[1]
    per = columns // wide
    step = width(columns, wide)
    shapes = [(wide // 2, nb + ride, per)] * 2 + [(wide, k, per), (k, nb)]
    specs = [whole(x) for x in shapes]
    specs[2] = pl.BlockSpec((step // per, k, per), lambda j, *_: (j, 0, 0))
    return pl.pallas_call(
        functools.partial(project_kernel, per, wide),
        grid_spec=pltpu.PrefetchScalarGridSpec(
            num_scalar_prefetch=1,
            grid=(columns // step,),
            in_specs=[pl.BlockSpec((rows, step), lambda j, *_: (0, j))]
            + [whole(x) for x in ((rows, nb), (1, rows), block.shape)],
            out_specs=specs,
            scratch_shapes=[pltpu.VMEM((2 * (nb + k), rows), BF16)],
        ),
        out_shape=[jax.ShapeDtypeStruct(x, F32) for x in shapes],
        compiler_params=params(),
        cost_estimate=SHORT,
        name="project",
    )(me, vectors, reflectors, e_row, block)


def update_kernel(me_ref, v_ref, r_ref, even_ref, odd_ref, *refs):
    out_ref, token_ref, right_ref = refs[-3:]
    nb = r_ref.shape[1]
    per = even_ref.shape[2]

    @pl.when(pl.program_id(0) == 0)
    def _():
        token_ref[...] = jnp.zeros_like(token_ref)
        for w in range(2 * even_ref.shape[0]):
            high, low = split(take(w ^ me_ref[0], even_ref, odd_ref, slice(0, nb)))
            here = slice(w * per, (w + 1) * per)
            right_ref[:nb, here] = high
            right_ref[nb : 2 * nb, here] = high
            right_ref[2 * nb :, here] = low

    high, low = split(r_ref[...])
    left = jnp.concatenate([high, low, high], axis=1)
    out_ref[...] = v_ref[...] - mul(left, right_ref[...])


def update(me, vectors, reflectors, c, first, count, of, others, before):
    rows, columns = vectors.shape
    nb = reflectors.shape[1]
    operands = [me, vectors, reflectors, *c, *others, *before]
    return pl.pallas_call(
        update_kernel,
        grid_spec=pltpu.PrefetchScalarGridSpec(
            num_scalar_prefetch=1,
            grid=(count,),
            in_specs=[
                pl.BlockSpec((rows // of, columns), lambda j, *_: (j + first, 0)),
                pl.BlockSpec((rows // of, nb), lambda j, *_: (j + first, 0)),
            ]
            + [whole(x.shape) for x in c]
            + [ANY] * (len(operands) - 5),
            out_specs=[
                pl.BlockSpec((rows // of, columns), lambda j, *_: (j + first, 0)),
                whole((8, 128)),
            ],
            scratch_shapes=[pltpu.VMEM((3 * nb, columns), BF16)],
        ),
        out_shape=[
            jax.ShapeDtypeStruct(vectors.shape, F32),
            jax.ShapeDtypeStruct((8, 128), F32),
        ],
        input_output_aliases={len(operands) - 1: 0} if before else {},
        compiler_params=params(),
        cost_estimate=SHORT,
        name="update",
    )(*operands)


def late_kernel(per, counts, at_ref, u_ref, after_ref, *refs):
    *refs, even_out, odd_out, both_ref, block_ref, sem_ref = refs
    j = pl.program_id(0)
    m = both_ref.shape[0] // 2
    each = block_ref.shape[2]

    @pl.when(j == 0)
    def _():
        first = 0
        for s, count in enumerate(counts):
            for k, ref in enumerate(refs[first : first + count]):

                @pl.when(at_ref[1 + s] == k)
                def _(ref=ref, s=s):
                    pltpu.make_async_copy(ref, block_ref.at[s], sem_ref.at[s]).start()

            first += count
        for s in range(len(counts)):
            pltpu.make_async_copy(block_ref.at[s], block_ref.at[s], sem_ref.at[s]).wait()
            high, low = split(block_ref[s].T)
            both_ref[s * each : (s + 1) * each] = high
            both_ref[m + s * each : m + (s + 1) * each] = low

    value = stacked(both_ref[...], both_ref[:m], split(u_ref[...]))
    count = u_ref.shape[1] // per
    for g in range(count):
        index = (j * count + g) ^ at_ref[0]
        place(value[:, g * per : (g + 1) * per], index, even_out, odd_out, 0)


def late(me, updated, slots, after, wide):
    rows, columns = updated.shape
    per = columns // wide
    step = width(columns, wide)
    flat = [x for choices, _ in slots for x in choices]
    counts = [len(choices) for choices, _ in slots]
    each = flat[0].shape[1]
    m = each * len(slots)
    at = jnp.stack([me[0]] + [which.astype(jnp.int32) for _, which in slots])
    half = jax.ShapeDtypeStruct((wide // 2, m, per), F32)
    return pl.pallas_call(
        functools.partial(late_kernel, per, counts),
        grid_spec=pltpu.PrefetchScalarGridSpec(
            num_scalar_prefetch=1,
            grid=(columns // step,),
            in_specs=[pl.BlockSpec((rows, step), lambda j, *_: (0, j))] + [ANY] * (1 + len(flat)),
            out_specs=[whole(half.shape)] * 2,
            scratch_shapes=[
                pltpu.VMEM((2 * m, rows), BF16),
                pltpu.VMEM((len(slots), rows, each), F32),
                pltpu.SemaphoreType.DMA((len(slots),)),
            ],
        ),
        out_shape=[half, half],
        compiler_params=params(),
        cost_estimate=SHORT,
        name="late",
    )(at, updated, after, *flat)


def own_kernel(me_ref, even_ref, odd_ref, after_ref, out_ref):
    each, nb = out_ref.shape
    per = even_ref.shape[2]
    block = jnp.where(
        ((OFF // per) ^ me_ref[0]) % 2 == 0, even_ref[0, :nb], odd_ref[0, :nb]
    )
    out_ref[...] = block[:, OFF % per : OFF % per + each].T


def own_columns(me, c, after, nb, each):
    per = c[0].shape[2]
    block = pl.BlockSpec(
        (1, *c[0].shape[1:]), lambda j, me_ref: (((OFF // per) ^ me_ref[0]) // 2, 0, 0)
    )
    return pl.pallas_call(
        own_kernel,
        grid_spec=pltpu.PrefetchScalarGridSpec(
            num_scalar_prefetch=1,
            grid=(1,),
            in_specs=[block, block, ANY],
            out_specs=whole((each, nb)),
        ),
        out_shape=jax.ShapeDtypeStruct((each, nb), F32),
        compiler_params=params(),
        cost_estimate=SHORT,
        name="own_columns",
    )(me, *c, after)


def total_kernel(*refs):
    refs[-1][...] = functools.reduce(jnp.add, [ref[...] for ref in refs[:-1]])


def total(terms):
    shape = terms[0].shape
    return pl.pallas_call(
        total_kernel,
        grid=(1,),
        in_specs=[pl.BlockSpec(shape, lambda j: (0, 0))] * len(terms),
        out_specs=pl.BlockSpec(shape, lambda j: (0, 0)),
        out_shape=jax.ShapeDtypeStruct(shape, F32),
        compiler_params=params(),
        cost_estimate=LONG,
        name="total",
    )(*terms)


def base_kernel(n, each, ride, at_ref, ready_ref, c_ref, middle_ref, *refs):
    *refs, out_ref, coef_ref, small_ref = refs
    me, z = at_ref[0], at_ref[1]
    nb = c_ref.shape[0]
    k = small_ref.shape[0]
    for s in range(n):
        first = pl.multiple_of((z + n - s) % n * each, each)
        coef_ref[pl.ds(first, each), :] = refs[s][...]
    if ride:
        wide = 2 * refs[n].shape[0]
        for w in range(wide):
            small_ref[w * (k // wide) : (w + 1) * (k // wide)] = take(
                w ^ me, *refs[n:], slice(nb, nb + k // wide)
            )
    else:
        small_ref[...] = refs[n][...]
    corrected = ready_ref[...] - three(split(small_ref[...]), split(c_ref[...]))
    out_ref[...] = -three(split(coef_ref[...]), split(corrected[:nb]))
    middle = middle_ref[...]
    pieces = [corrected[nb:]] + [
        middle[first : first + each] for first in range(0, middle.shape[0], each)
    ]
    for slot, piece in enumerate(pieces):
        first = pl.multiple_of(at_ref[1 + slot] * each, each)
        out_ref[pl.ds(first, each), :] += piece


def base(at, ready, c, middle, coef, small, n, each, ride):
    operands = [ready, c, middle, *coef, *small]
    k, per = ready.shape
    nb = c.shape[0]
    return pl.pallas_call(
        functools.partial(base_kernel, n, each, ride),
        grid_spec=pltpu.PrefetchScalarGridSpec(
            num_scalar_prefetch=1,
            grid=(1,),
            in_specs=[whole(x.shape) for x in operands],
            out_specs=whole((FB, per)),
            scratch_shapes=[pltpu.VMEM((FB, nb), F32), pltpu.VMEM((k, nb), F32)],
        ),
        out_shape=jax.ShapeDtypeStruct((FB, per), F32),
        compiler_params=params(),
        cost_estimate=LONG,
        name="base",
    )(at, *operands)


def last_kernel(each, at_ref, base_ref, *refs):
    *refs, out_ref, total_ref = refs
    total_ref[...] = base_ref[...]
    total = functools.reduce(jnp.add, [ref[...] for ref in refs])
    first = pl.multiple_of(at_ref[at_ref.shape[0] - 1] * each, each)
    total_ref[pl.ds(first, each), :] += total
    out_ref[...] = total_ref[...].T


def last(at, held, terms, each):
    per = held.shape[1]
    operands = [held, *terms]
    return pl.pallas_call(
        functools.partial(last_kernel, each),
        grid_spec=pltpu.PrefetchScalarGridSpec(
            num_scalar_prefetch=1,
            grid=(1,),
            in_specs=[whole(x.shape) for x in operands],
            out_specs=whole((per, FB)),
            scratch_shapes=[pltpu.VMEM((FB, per), F32)],
        ),
        out_shape=jax.ShapeDtypeStruct((per, FB), F32),
        compiler_params=params(),
        cost_estimate=SHORT,
        name="last",
    )(at, *operands)


def arrivals(n):
    order = []
    for z in range(n):
        found = [(hops, 0) for hops in range(1, n) if z + hops < n]
        found += [(hops, 1) for hops in range(1, n) if z - hops >= 0]
        order.append(sorted(found))
    return [[order[z][slot] for z in range(n)] for slot in range(n - 1)]


def travel(came, held, n, hops, after):
    if hops > 1:
        held = gate(held, *after, cost=LONG)
        came[(hops - 1, 0)], came[(hops - 1, 1)] = held
    pairs = [
        [(p, p - 1) for p in range(1, n - hops + 1)],
        [(p, p + 1) for p in range(hops - 1, n - 1)],
    ]
    held = [lax.ppermute(held[d], "narrow", pairs[d]) for d in (0, 1)]
    came[(hops, 0)], came[(hops, 1)] = held
    return held


def options(came, places, z):
    choices = sorted(set(places))
    which = jnp.int32(0)
    for p, place in enumerate(places):
        which = jnp.where(z == p, choices.index(place), which)
    return [came[choice] for choice in choices], which


def source(places, z):
    value = jnp.int32(0)
    for p, (hops, direction) in enumerate(places):
        value = jnp.where(z == p, p - hops if direction else p + hops, value)
    return value


def swap(x, wide, distance):
    return lax.ppermute(x, "wide", [(i, i ^ distance) for i in range(wide)])


def scatter_terms(even, odd, wide, after=None):
    other = swap(odd, wide, 1)
    if after is not None:
        (other,) = gate([other], after)
    sums = [even[h] + other[h] for h in range(wide // 2)]
    return [sums[0]] + [swap(sums[h], wide, 2 * h) for h in range(1, wide // 2)]


def collect(x, wide, after=()):
    pieces = [swap(x, wide, 2 * h) for h in range(1, wide // 2)]
    if after:
        (x,) = gate([x], *after)
    even = jnp.stack([x, *pieces])
    return even, swap(even, wide, 1)


def on_device(vectors, reflectors, triangle, energies):
    n = lax.axis_size("narrow")
    wide = lax.axis_size("wide")
    z = lax.axis_index("narrow").astype(jnp.int32)
    me = lax.axis_index("wide").astype(jnp.int32).reshape(1)
    each = FB // n
    rows, columns = vectors.shape
    nb = reflectors.shape[1]
    k = nb + each
    per = columns // wide
    e_row = energies.reshape(1, rows)

    own = energies[:, None] * vectors[:, OFF : OFF + each]
    came = {}
    held = travel(came, [own, own], n, 1, [])
    table = arrivals(n)
    at = jnp.stack([me[0], z] + [source(places, z) for places in table])

    ride = k // wide if per == nb and k % (8 * wide) == 0 else 0
    even, odd, sums, small = project(me, vectors, reflectors, e_row, own, wide, ride)
    if n > 2:
        held = travel(came, held, n, 2, [small])
    ready = lax.psum_scatter(sums, "wide", scatter_dimension=0)

    projected = functools.reduce(jnp.add, scatter_terms(even, odd, wide, came[(1, 0)]))
    highest = lax.Precision.HIGHEST
    coefficients = jnp.dot(triangle, projected[:nb], precision=highest)
    payload = coefficients
    if ride:
        payload = jnp.concatenate([coefficients, projected[nb:]], axis=0)
    c = collect(payload, wide)

    of = next(x for x in range(4, rows) if rows % (16 * x) == 0)
    updated, token = update(me, vectors, reflectors, c, 0, of // 2, of, [], [])
    for hops in range(3, n):
        held = travel(came, held, n, hops, [token])
    updated, token = update(
        me, vectors, reflectors, c, of // 2, of - of // 2, of, [came[(n - 2, 0)]], [updated]
    )

    slots = [options(came, places, z) for places in table]
    even, odd = late(me, updated, slots[:-1], token, wide)
    mine = own_columns(me, c, even, nb, each)
    coef = [mine] + [
        lax.ppermute(mine, "narrow", [(p, (p + s) % n) for p in range(n)]) for s in range(1, n)
    ]
    middle = scatter_terms(even, odd, wide)
    (ready,) = gate([ready], middle[0], mine)
    even, odd = late(me, updated, slots[-1:], ready, wide)
    middle = total(middle)
    (odd,) = gate([odd], *coef[1:])
    tail = scatter_terms(even, odd, wide, middle)
    (ready,) = gate([ready], tail[0])
    small = c if ride else [lax.psum(small, "wide")]
    base_block = base(at, ready, coefficients, middle, coef, small, n, each, ride)
    return (updated, last(at, base_block, tail, each))


def solution(mesh):
    return jax.shard_map(
        on_device,
        mesh=mesh,
        in_specs=(P("wide", "narrow"), P("wide", None), P(), P("wide")),
        out_specs=(P("wide", "narrow"), P(("narrow", "wide"), None)),
        check_vma=False,
    )
```

```python
import functools

import jax
import jax.numpy as jnp
from jax import lax
from jax.experimental import pallas as pl
from jax.experimental.pallas import tpu as pltpu
from jax.sharding import PartitionSpec as P

FB = 512
OFF = 256
VMEM = 60 * 1024 * 1024

F32 = jnp.float32
BF16 = jnp.bfloat16
LONG = pl.CostEstimate(flops=10**11, bytes_accessed=1024, transcendentals=0)
SHORT = pl.CostEstimate(flops=1024, bytes_accessed=1024, transcendentals=0)


def split(x):
    high = x.astype(BF16)
    return high, (x - high.astype(F32)).astype(BF16)


def mul(left, right):
    return jnp.dot(left, right, preferred_element_type=F32)


def three(left, right):
    (lh, ll), (rh, rl) = left, right
    return mul(lh, rh) + mul(ll, rh) + mul(lh, rl)


def stacked(both, high, right):
    rh, rl = right
    m = high.shape[0]
    top = mul(both, rh)
    return top[:m] + top[m:] + mul(high, rl)


def params():
    return pltpu.CompilerParams(
        dimension_semantics=("arbitrary",), vmem_limit_bytes=VMEM
    )


def width(columns, wide):
    return 256 if columns % 256 == 0 and 256 % (columns // wide) == 0 else columns // wide


def whole(shape):
    return pl.BlockSpec(shape, lambda j, *_: (0,) * len(shape), pipeline_mode=pl.Buffered(1))


ANY = pl.BlockSpec(memory_space=pl.ANY)


def gate_kernel(*refs):
    del refs


def gate(held, *others, cost=SHORT):
    count = len(held)
    return pl.pallas_call(
        gate_kernel,
        in_specs=[ANY] * (count + len(others)),
        out_specs=[ANY] * count,
        out_shape=[jax.ShapeDtypeStruct(x.shape, x.dtype) for x in held],
        input_output_aliases={k: k for k in range(count)},
        cost_estimate=cost,
        name="gate",
    )(*held, *others)


def place(value, index, even_ref, odd_ref, first):
    half = index // 2
    rows = value.shape[0]

    @pl.when(index % 2 == 0)
    def _():
        even_ref[half, first : first + rows] = value

    @pl.when(index % 2 == 1)
    def _():
        odd_ref[half, first : first + rows] = value


def take(index, even_ref, odd_ref, rows):
    half = index // 2
    return jnp.where(index % 2 == 0, even_ref[half, rows], odd_ref[half, rows])


def project_kernel(per, wide, me_ref, v_ref, r_ref, e_ref, x_ref, even_ref, odd_ref, sums_ref, small_ref, both_ref):
    j = pl.program_id(0)
    nb = r_ref.shape[1]
    m = both_ref.shape[0] // 2
    k = m - nb
    ride = even_ref.shape[1] - nb

    @pl.when(j == 0)
    def _():
        turned = r_ref[...].T
        first = 0
        for part in (turned, turned * e_ref[...], x_ref[...].T):
            end = first + part.shape[0]
            both_ref[first:end], both_ref[m + first : m + end] = split(part)
            first = end
        small = three((both_ref[nb:m], both_ref[m + nb :]), split(r_ref[...]))
        small_ref[...] = small
        if ride:
            for w in range(wide):
                share = small[w * ride : (w + 1) * ride]
                place(share, w ^ me_ref[0], even_ref, odd_ref, nb)

    value = stacked(both_ref[...], both_ref[:m], split(v_ref[...]))
    count = v_ref.shape[1] // per
    for g in range(count):
        part = value[:, g * per : (g + 1) * per]
        place(part[:nb], (j * count + g) ^ me_ref[0], even_ref, odd_ref, 0)
        sums_ref[g] = part[nb:]


def project(me, vectors, reflectors, e_row, block, wide, ride):
    rows, columns = vectors.shape
    nb = reflectors.shape[1]
    k = nb + block.shape[1]
    per = columns // wide
    step = width(columns, wide)
    shapes = [(wide // 2, nb + ride, per)] * 2 + [(wide, k, per), (k, nb)]
    specs = [whole(x) for x in shapes]
    specs[2] = pl.BlockSpec((step // per, k, per), lambda j, *_: (j, 0, 0))
    return pl.pallas_call(
        functools.partial(project_kernel, per, wide),
        grid_spec=pltpu.PrefetchScalarGridSpec(
            num_scalar_prefetch=1,
            grid=(columns // step,),
            in_specs=[pl.BlockSpec((rows, step), lambda j, *_: (0, j))]
            + [whole(x) for x in ((rows, nb), (1, rows), block.shape)],
            out_specs=specs,
            scratch_shapes=[pltpu.VMEM((2 * (nb + k), rows), BF16)],
        ),
        out_shape=[jax.ShapeDtypeStruct(x, F32) for x in shapes],
        compiler_params=params(),
        cost_estimate=SHORT,
        name="project",
    )(me, vectors, reflectors, e_row, block)


def update_kernel(me_ref, v_ref, r_ref, even_ref, odd_ref, *refs):
    out_ref, token_ref, right_ref = refs[-3:]
    nb = r_ref.shape[1]
    per = even_ref.shape[2]

    @pl.when(pl.program_id(0) == 0)
    def _():
        token_ref[...] = jnp.zeros_like(token_ref)
        for w in range(2 * even_ref.shape[0]):
            high, low = split(take(w ^ me_ref[0], even_ref, odd_ref, slice(0, nb)))
            here = slice(w * per, (w + 1) * per)
            right_ref[:nb, here] = high
            right_ref[nb : 2 * nb, here] = high
            right_ref[2 * nb :, here] = low

    high, low = split(r_ref[...])
    left = jnp.concatenate([high, low, high], axis=1)
    out_ref[...] = v_ref[...] - mul(left, right_ref[...])


def update(me, vectors, reflectors, c, first, count, of, others, before):
    rows, columns = vectors.shape
    nb = reflectors.shape[1]
    operands = [me, vectors, reflectors, *c, *others, *before]
    return pl.pallas_call(
        update_kernel,
        grid_spec=pltpu.PrefetchScalarGridSpec(
            num_scalar_prefetch=1,
            grid=(count,),
            in_specs=[
                pl.BlockSpec((rows // of, columns), lambda j, *_: (j + first, 0)),
                pl.BlockSpec((rows // of, nb), lambda j, *_: (j + first, 0)),
            ]
            + [whole(x.shape) for x in c]
            + [ANY] * (len(operands) - 5),
            out_specs=[
                pl.BlockSpec((rows // of, columns), lambda j, *_: (j + first, 0)),
                whole((8, 128)),
            ],
            scratch_shapes=[pltpu.VMEM((3 * nb, columns), BF16)],
        ),
        out_shape=[
            jax.ShapeDtypeStruct(vectors.shape, F32),
            jax.ShapeDtypeStruct((8, 128), F32),
        ],
        input_output_aliases={len(operands) - 1: 0} if before else {},
        compiler_params=params(),
        cost_estimate=SHORT,
        name="update",
    )(*operands)


def late_kernel(per, counts, at_ref, u_ref, after_ref, *refs):
    *refs, even_out, odd_out, both_ref, block_ref, sem_ref = refs
    j = pl.program_id(0)
    m = both_ref.shape[0] // 2
    each = block_ref.shape[2]

    @pl.when(j == 0)
    def _():
        first = 0
        for s, count in enumerate(counts):
            for k, ref in enumerate(refs[first : first + count]):

                @pl.when(at_ref[1 + s] == k)
                def _(ref=ref, s=s):
                    pltpu.make_async_copy(ref, block_ref.at[s], sem_ref.at[s]).start()

            first += count
        for s in range(len(counts)):
            pltpu.make_async_copy(block_ref.at[s], block_ref.at[s], sem_ref.at[s]).wait()
            high, low = split(block_ref[s].T)
            both_ref[s * each : (s + 1) * each] = high
            both_ref[m + s * each : m + (s + 1) * each] = low

    value = stacked(both_ref[...], both_ref[:m], split(u_ref[...]))
    count = u_ref.shape[1] // per
    for g in range(count):
        index = (j * count + g) ^ at_ref[0]
        place(value[:, g * per : (g + 1) * per], index, even_out, odd_out, 0)


def late(me, updated, slots, after, wide):
    rows, columns = updated.shape
    per = columns // wide
    step = width(columns, wide)
    flat = [x for choices, _ in slots for x in choices]
    counts = [len(choices) for choices, _ in slots]
    each = flat[0].shape[1]
    m = each * len(slots)
    at = jnp.stack([me[0]] + [which.astype(jnp.int32) for _, which in slots])
    half = jax.ShapeDtypeStruct((wide // 2, m, per), F32)
    return pl.pallas_call(
        functools.partial(late_kernel, per, counts),
        grid_spec=pltpu.PrefetchScalarGridSpec(
            num_scalar_prefetch=1,
            grid=(columns // step,),
            in_specs=[pl.BlockSpec((rows, step), lambda j, *_: (0, j))] + [ANY] * (1 + len(flat)),
            out_specs=[whole(half.shape)] * 2,
            scratch_shapes=[
                pltpu.VMEM((2 * m, rows), BF16),
                pltpu.VMEM((len(slots), rows, each), F32),
                pltpu.SemaphoreType.DMA((len(slots),)),
            ],
        ),
        out_shape=[half, half],
        compiler_params=params(),
        cost_estimate=SHORT,
        name="late",
    )(at, updated, after, *flat)


def own_kernel(me_ref, even_ref, odd_ref, after_ref, out_ref):
    each, nb = out_ref.shape
    per = even_ref.shape[2]
    block = jnp.where(
        ((OFF // per) ^ me_ref[0]) % 2 == 0, even_ref[0, :nb], odd_ref[0, :nb]
    )
    out_ref[...] = block[:, OFF % per : OFF % per + each].T


def own_columns(me, c, after, nb, each):
    per = c[0].shape[2]
    block = pl.BlockSpec(
        (1, *c[0].shape[1:]), lambda j, me_ref: (((OFF // per) ^ me_ref[0]) // 2, 0, 0)
    )
    return pl.pallas_call(
        own_kernel,
        grid_spec=pltpu.PrefetchScalarGridSpec(
            num_scalar_prefetch=1,
            grid=(1,),
            in_specs=[block, block, ANY],
            out_specs=whole((each, nb)),
        ),
        out_shape=jax.ShapeDtypeStruct((each, nb), F32),
        compiler_params=params(),
        cost_estimate=SHORT,
        name="own_columns",
    )(me, *c, after)


def base_kernel(n, each, ride, at_ref, ready_ref, c_ref, *refs):
    *refs, out_ref, coef_ref, small_ref = refs
    me, z = at_ref[0], at_ref[1]
    nb = c_ref.shape[0]
    k = small_ref.shape[0]
    for s in range(n):
        first = pl.multiple_of((z + n - s) % n * each, each)
        coef_ref[pl.ds(first, each), :] = refs[s][...]
    if ride:
        wide = 2 * refs[n].shape[0]
        for w in range(wide):
            small_ref[w * (k // wide) : (w + 1) * (k // wide)] = take(
                w ^ me, *refs[n:], slice(nb, nb + k // wide)
            )
    else:
        small_ref[...] = refs[n][...]
    corrected = ready_ref[...] - three(split(small_ref[...]), split(c_ref[...]))
    out_ref[...] = -three(split(coef_ref[...]), split(corrected[:nb]))
    out_ref[pl.ds(pl.multiple_of(z * each, each), each), :] += corrected[nb:]


def base(at, ready, c, coef, small, n, each, ride):
    operands = [ready, c, *coef, *small]
    k, per = ready.shape
    nb = c.shape[0]
    return pl.pallas_call(
        functools.partial(base_kernel, n, each, ride),
        grid_spec=pltpu.PrefetchScalarGridSpec(
            num_scalar_prefetch=1,
            grid=(1,),
            in_specs=[whole(x.shape) for x in operands],
            out_specs=whole((FB, per)),
            scratch_shapes=[pltpu.VMEM((FB, nb), F32), pltpu.VMEM((k, nb), F32)],
        ),
        out_shape=jax.ShapeDtypeStruct((FB, per), F32),
        compiler_params=params(),
        cost_estimate=LONG,
        name="base",
    )(at, *operands)


def last_kernel(each, at_ref, base_ref, *refs):
    *refs, out_ref, total_ref = refs
    total_ref[...] = base_ref[...]
    total = functools.reduce(jnp.add, [ref[...] for ref in refs])
    for slot in range(total.shape[0] // each):
        first = pl.multiple_of(at_ref[2 + slot] * each, each)
        total_ref[pl.ds(first, each), :] += total[slot * each : (slot + 1) * each]
    out_ref[...] = total_ref[...].T


def last(at, held, terms, each):
    per = held.shape[1]
    operands = [held, *terms]
    return pl.pallas_call(
        functools.partial(last_kernel, each),
        grid_spec=pltpu.PrefetchScalarGridSpec(
            num_scalar_prefetch=1,
            grid=(1,),
            in_specs=[whole(x.shape) for x in operands],
            out_specs=whole((per, FB)),
            scratch_shapes=[pltpu.VMEM((FB, per), F32)],
        ),
        out_shape=jax.ShapeDtypeStruct((per, FB), F32),
        compiler_params=params(),
        cost_estimate=SHORT,
        name="last",
    )(at, *operands)


def arrivals(n):
    order = []
    for z in range(n):
        found = [(hops, 0) for hops in range(1, n) if z + hops < n]
        found += [(hops, 1) for hops in range(1, n) if z - hops >= 0]
        order.append(sorted(found))
    return [[order[z][slot] for z in range(n)] for slot in range(n - 1)]


def travel(came, held, n, hops, after):
    if hops > 1:
        held = gate(held, *after, cost=LONG)
        came[(hops - 1, 0)], came[(hops - 1, 1)] = held
    pairs = [
        [(p, p - 1) for p in range(1, n - hops + 1)],
        [(p, p + 1) for p in range(hops - 1, n - 1)],
    ]
    held = [lax.ppermute(held[d], "narrow", pairs[d]) for d in (0, 1)]
    came[(hops, 0)], came[(hops, 1)] = held
    return held


def options(came, places, z):
    choices = sorted(set(places))
    which = jnp.int32(0)
    for p, place in enumerate(places):
        which = jnp.where(z == p, choices.index(place), which)
    return [came[choice] for choice in choices], which


def source(places, z):
    value = jnp.int32(0)
    for p, (hops, direction) in enumerate(places):
        value = jnp.where(z == p, p - hops if direction else p + hops, value)
    return value


def swap(x, wide, distance):
    return lax.ppermute(x, "wide", [(i, i ^ distance) for i in range(wide)])


def scatter_terms(halves, wide, after):
    others = [swap(odd, wide, 1) for _, odd in halves]
    others[-1:] = gate(others[-1:], after)
    sums = [
        [even[h] + other[h] for (even, _), other in zip(halves, others)] for h in range(wide // 2)
    ]
    sums = [x[0] if len(x) == 1 else jnp.concatenate(x, axis=0) for x in sums]
    return [sums[0]] + [swap(sums[h], wide, 2 * h) for h in range(1, wide // 2)]


def collect(x, wide, after=()):
    pieces = [swap(x, wide, 2 * h) for h in range(1, wide // 2)]
    if after:
        (x,) = gate([x], *after)
    even = jnp.stack([x, *pieces])
    return even, swap(even, wide, 1)


def on_device(vectors, reflectors, triangle, energies):
    n = lax.axis_size("narrow")
    wide = lax.axis_size("wide")
    z = lax.axis_index("narrow").astype(jnp.int32)
    me = lax.axis_index("wide").astype(jnp.int32).reshape(1)
    each = FB // n
    rows, columns = vectors.shape
    nb = reflectors.shape[1]
    k = nb + each
    per = columns // wide
    e_row = energies.reshape(1, rows)

    own = energies[:, None] * vectors[:, OFF : OFF + each]
    came = {}
    held = travel(came, [own, own], n, 1, [])
    table = arrivals(n)
    at = jnp.stack([me[0], z] + [source(places, z) for places in table])

    ride = k // wide if per == nb and k % (8 * wide) == 0 else 0
    even, odd, sums, small = project(me, vectors, reflectors, e_row, own, wide, ride)
    if n > 2:
        held = travel(came, held, n, 2, [small])
    ready = lax.psum_scatter(sums, "wide", scatter_dimension=0)

    projected = functools.reduce(jnp.add, scatter_terms([(even, odd)], wide, came[(1, 0)]))
    highest = lax.Precision.HIGHEST
    coefficients = jnp.dot(triangle, projected[:nb], precision=highest)
    payload = coefficients
    if ride:
        payload = jnp.concatenate([coefficients, projected[nb:]], axis=0)
    c = collect(payload, wide)

    of = next(x for x in range(4, rows) if rows % (16 * x) == 0)
    updated, token = update(me, vectors, reflectors, c, 0, of // 2, of, [], [])
    for hops in range(3, n):
        held = travel(came, held, n, hops, [token])
    updated, token = update(
        me, vectors, reflectors, c, of // 2, of - of // 2, of, [came[(n - 2, 0)]], [updated]
    )

    slots = [options(came, places, z) for places in table]
    halves = [late(me, updated, slots[:-1], token, wide)]
    (ready,) = gate([ready], halves[0][0])
    halves.append(late(me, updated, slots[-1:], ready, wide))
    mine = own_columns(me, c, halves[1][0], nb, each)
    coef = [mine] + [
        lax.ppermute(mine, "narrow", [(p, (p + s) % n) for p in range(n)]) for s in range(1, n)
    ]
    tail = scatter_terms(halves, wide, mine)
    (ready,) = gate([ready], tail[0])
    small = c if ride else [lax.psum(small, "wide")]
    base_block = base(at, ready, coefficients, coef, small, n, each, ride)
    return (updated, last(at, base_block, tail, each))


def solution(mesh):
    return jax.shard_map(
        on_device,
        mesh=mesh,
        in_specs=(P("wide", "narrow"), P("wide", None), P(), P("wide")),
        out_specs=(P("wide", "narrow"), P(("narrow", "wide"), None)),
        check_vma=False,
    )
```

```python
import functools

import jax
import jax.numpy as jnp
from jax import lax
from jax.experimental import pallas as pl
from jax.experimental.pallas import tpu as pltpu
from jax.sharding import PartitionSpec as P

FB = 512
OFF = 256
VMEM = 60 * 1024 * 1024

F32 = jnp.float32
BF16 = jnp.bfloat16
LONG = pl.CostEstimate(flops=10**11, bytes_accessed=1024, transcendentals=0)
SHORT = pl.CostEstimate(flops=1024, bytes_accessed=1024, transcendentals=0)


def split(x):
    high = x.astype(BF16)
    return high, (x - high.astype(F32)).astype(BF16)


def mul(left, right):
    return jnp.dot(left, right, preferred_element_type=F32)


def three(left, right):
    (lh, ll), (rh, rl) = left, right
    return mul(lh, rh) + mul(ll, rh) + mul(lh, rl)


def stacked(both, high, right):
    rh, rl = right
    m = high.shape[0]
    top = mul(both, rh)
    return top[:m] + top[m:] + mul(high, rl)


def params():
    return pltpu.CompilerParams(
        dimension_semantics=("arbitrary",), vmem_limit_bytes=VMEM
    )


def width(columns, wide):
    return 256 if columns % 256 == 0 and 256 % (columns // wide) == 0 else columns // wide


def whole(shape):
    return pl.BlockSpec(shape, lambda j, *_: (0,) * len(shape), pipeline_mode=pl.Buffered(1))


ANY = pl.BlockSpec(memory_space=pl.ANY)


def gate_kernel(*refs):
    del refs


def gate(held, *others, cost=SHORT):
    count = len(held)
    return pl.pallas_call(
        gate_kernel,
        in_specs=[ANY] * (count + len(others)),
        out_specs=[ANY] * count,
        out_shape=[jax.ShapeDtypeStruct(x.shape, x.dtype) for x in held],
        input_output_aliases={k: k for k in range(count)},
        cost_estimate=cost,
        name="gate",
    )(*held, *others)


def place(value, index, even_ref, odd_ref, first):
    half = index // 2
    rows = value.shape[0]

    @pl.when(index % 2 == 0)
    def _():
        even_ref[half, first : first + rows] = value

    @pl.when(index % 2 == 1)
    def _():
        odd_ref[half, first : first + rows] = value


def take(index, even_ref, odd_ref, rows):
    half = index // 2
    return jnp.where(index % 2 == 0, even_ref[half, rows], odd_ref[half, rows])


def project_kernel(per, wide, me_ref, v_ref, r_ref, e_ref, x_ref, even_ref, odd_ref, sums_ref, small_ref, both_ref):
    j = pl.program_id(0)
    nb = r_ref.shape[1]
    m = both_ref.shape[0] // 2
    k = m - nb
    ride = even_ref.shape[1] - nb

    @pl.when(j == 0)
    def _():
        turned = r_ref[...].T
        first = 0
        for part in (turned, turned * e_ref[...], x_ref[...].T):
            end = first + part.shape[0]
            both_ref[first:end], both_ref[m + first : m + end] = split(part)
            first = end
        small = three((both_ref[nb:m], both_ref[m + nb :]), split(r_ref[...]))
        small_ref[...] = small
        if ride:
            for w in range(wide):
                share = small[w * ride : (w + 1) * ride]
                place(share, w ^ me_ref[0], even_ref, odd_ref, nb)

    value = stacked(both_ref[...], both_ref[:m], split(v_ref[...]))
    count = v_ref.shape[1] // per
    for g in range(count):
        part = value[:, g * per : (g + 1) * per]
        place(part[:nb], (j * count + g) ^ me_ref[0], even_ref, odd_ref, 0)
        sums_ref[g] = part[nb:]


def project(me, vectors, reflectors, e_row, block, wide, ride):
    rows, columns = vectors.shape
    nb = reflectors.shape[1]
    k = nb + block.shape[1]
    per = columns // wide
    step = width(columns, wide)
    shapes = [(wide // 2, nb + ride, per)] * 2 + [(wide, k, per), (k, nb)]
    specs = [whole(x) for x in shapes]
    specs[2] = pl.BlockSpec((step // per, k, per), lambda j, *_: (j, 0, 0))
    return pl.pallas_call(
        functools.partial(project_kernel, per, wide),
        grid_spec=pltpu.PrefetchScalarGridSpec(
            num_scalar_prefetch=1,
            grid=(columns // step,),
            in_specs=[pl.BlockSpec((rows, step), lambda j, *_: (0, j))]
            + [whole(x) for x in ((rows, nb), (1, rows), block.shape)],
            out_specs=specs,
            scratch_shapes=[pltpu.VMEM((2 * (nb + k), rows), BF16)],
        ),
        out_shape=[jax.ShapeDtypeStruct(x, F32) for x in shapes],
        compiler_params=params(),
        cost_estimate=SHORT,
        name="project",
    )(me, vectors, reflectors, e_row, block)


def update_kernel(me_ref, v_ref, r_ref, even_ref, odd_ref, *refs):
    out_ref, token_ref, right_ref = refs[-3:]
    nb = r_ref.shape[1]
    per = even_ref.shape[2]

    @pl.when(pl.program_id(0) == 0)
    def _():
        token_ref[...] = jnp.zeros_like(token_ref)
        for w in range(2 * even_ref.shape[0]):
            high, low = split(take(w ^ me_ref[0], even_ref, odd_ref, slice(0, nb)))
            here = slice(w * per, (w + 1) * per)
            right_ref[:nb, here] = high
            right_ref[nb : 2 * nb, here] = high
            right_ref[2 * nb :, here] = low

    high, low = split(r_ref[...])
    left = jnp.concatenate([high, low, high], axis=1)
    out_ref[...] = v_ref[...] - mul(left, right_ref[...])


def update(me, vectors, reflectors, c, first, count, of, others, before):
    rows, columns = vectors.shape
    nb = reflectors.shape[1]
    operands = [me, vectors, reflectors, *c, *others, *before]
    return pl.pallas_call(
        update_kernel,
        grid_spec=pltpu.PrefetchScalarGridSpec(
            num_scalar_prefetch=1,
            grid=(count,),
            in_specs=[
                pl.BlockSpec((rows // of, columns), lambda j, *_: (j + first, 0)),
                pl.BlockSpec((rows // of, nb), lambda j, *_: (j + first, 0)),
            ]
            + [whole(x.shape) for x in c]
            + [ANY] * (len(operands) - 5),
            out_specs=[
                pl.BlockSpec((rows // of, columns), lambda j, *_: (j + first, 0)),
                whole((8, 128)),
            ],
            scratch_shapes=[pltpu.VMEM((3 * nb, columns), BF16)],
        ),
        out_shape=[
            jax.ShapeDtypeStruct(vectors.shape, F32),
            jax.ShapeDtypeStruct((8, 128), F32),
        ],
        input_output_aliases={len(operands) - 1: 0} if before else {},
        compiler_params=params(),
        cost_estimate=SHORT,
        name="update",
    )(*operands)


def late_kernel(per, counts, at_ref, u_ref, after_ref, *refs):
    *refs, both_ref, block_ref, sem_ref = refs
    outs = refs[sum(counts) :]
    j = pl.program_id(0)
    m = both_ref.shape[0] // 2
    each = block_ref.shape[2]

    @pl.when(j == 0)
    def _():
        first = 0
        for s, count in enumerate(counts):
            for k, ref in enumerate(refs[first : first + count]):

                @pl.when(at_ref[1 + s] == k)
                def _(ref=ref, s=s):
                    pltpu.make_async_copy(ref, block_ref.at[s], sem_ref.at[s]).start()

            first += count
        for s in range(len(counts)):
            pltpu.make_async_copy(block_ref.at[s], block_ref.at[s], sem_ref.at[s]).wait()
            high, low = split(block_ref[s].T)
            both_ref[s * each : (s + 1) * each] = high
            both_ref[m + s * each : m + (s + 1) * each] = low

    value = stacked(both_ref[...], both_ref[:m], split(u_ref[...]))
    count = u_ref.shape[1] // per
    for g in range(count):
        part = value[:, g * per : (g + 1) * per]
        if len(outs) == 2:
            place(part, (j * count + g) ^ at_ref[0], *outs, 0)
        else:
            outs[0][g] = part


def late(me, updated, slots, after, wide, ordered):
    rows, columns = updated.shape
    per = columns // wide
    step = width(columns, wide)
    flat = [x for choices, _ in slots for x in choices]
    counts = [len(choices) for choices, _ in slots]
    each = flat[0].shape[1]
    m = each * len(slots)
    at = jnp.stack([me[0]] + [which.astype(jnp.int32) for _, which in slots])
    if ordered:
        shapes = [(wide, m, per)]
        specs = [pl.BlockSpec((step // per, m, per), lambda j, *_: (j, 0, 0))]
    else:
        shapes = [(wide // 2, m, per)] * 2
        specs = [whole(x) for x in shapes]
    return pl.pallas_call(
        functools.partial(late_kernel, per, counts),
        grid_spec=pltpu.PrefetchScalarGridSpec(
            num_scalar_prefetch=1,
            grid=(columns // step,),
            in_specs=[pl.BlockSpec((rows, step), lambda j, *_: (0, j))] + [ANY] * (1 + len(flat)),
            out_specs=specs,
            scratch_shapes=[
                pltpu.VMEM((2 * m, rows), BF16),
                pltpu.VMEM((len(slots), rows, each), F32),
                pltpu.SemaphoreType.DMA((len(slots),)),
            ],
        ),
        out_shape=[jax.ShapeDtypeStruct(x, F32) for x in shapes],
        compiler_params=params(),
        cost_estimate=SHORT,
        name="late",
    )(at, updated, after, *flat)


def own_kernel(me_ref, even_ref, odd_ref, after_ref, out_ref):
    each, nb = out_ref.shape
    per = even_ref.shape[2]
    block = jnp.where(
        ((OFF // per) ^ me_ref[0]) % 2 == 0, even_ref[0, :nb], odd_ref[0, :nb]
    )
    out_ref[...] = block[:, OFF % per : OFF % per + each].T


def own_columns(me, c, after, nb, each):
    per = c[0].shape[2]
    block = pl.BlockSpec(
        (1, *c[0].shape[1:]), lambda j, me_ref: (((OFF // per) ^ me_ref[0]) // 2, 0, 0)
    )
    return pl.pallas_call(
        own_kernel,
        grid_spec=pltpu.PrefetchScalarGridSpec(
            num_scalar_prefetch=1,
            grid=(1,),
            in_specs=[block, block, ANY],
            out_specs=whole((each, nb)),
        ),
        out_shape=jax.ShapeDtypeStruct((each, nb), F32),
        compiler_params=params(),
        cost_estimate=SHORT,
        name="own_columns",
    )(me, *c, after)


def base_kernel(n, each, ride, at_ref, ready_ref, c_ref, *refs):
    *refs, out_ref, coef_ref, small_ref = refs
    me, z = at_ref[0], at_ref[1]
    nb = c_ref.shape[0]
    k = small_ref.shape[0]
    for s in range(n):
        first = pl.multiple_of((z + n - s) % n * each, each)
        coef_ref[pl.ds(first, each), :] = refs[s][...]
    if ride:
        wide = 2 * refs[n].shape[0]
        for w in range(wide):
            small_ref[w * (k // wide) : (w + 1) * (k // wide)] = take(
                w ^ me, *refs[n:], slice(nb, nb + k // wide)
            )
    else:
        small_ref[...] = refs[n][...]
    corrected = ready_ref[...] - three(split(small_ref[...]), split(c_ref[...]))
    out_ref[...] = -three(split(coef_ref[...]), split(corrected[:nb]))
    out_ref[pl.ds(pl.multiple_of(z * each, each), each), :] += corrected[nb:]


def base(at, ready, c, coef, small, n, each, ride):
    operands = [ready, c, *coef, *small]
    k, per = ready.shape
    nb = c.shape[0]
    return pl.pallas_call(
        functools.partial(base_kernel, n, each, ride),
        grid_spec=pltpu.PrefetchScalarGridSpec(
            num_scalar_prefetch=1,
            grid=(1,),
            in_specs=[whole(x.shape) for x in operands],
            out_specs=whole((FB, per)),
            scratch_shapes=[pltpu.VMEM((FB, nb), F32), pltpu.VMEM((k, nb), F32)],
        ),
        out_shape=jax.ShapeDtypeStruct((FB, per), F32),
        compiler_params=params(),
        cost_estimate=SHORT,
        name="base",
    )(at, *operands)


def last_kernel(each, at_ref, base_ref, middle_ref, *refs):
    *refs, out_ref, total_ref = refs
    total_ref[...] = base_ref[...]
    total = functools.reduce(jnp.add, [ref[...] for ref in refs])
    middle = middle_ref[...]
    pieces = [middle[k : k + each] for k in range(0, middle.shape[0], each)] + [total]
    for slot, piece in enumerate(pieces):
        first = pl.multiple_of(at_ref[2 + slot] * each, each)
        total_ref[pl.ds(first, each), :] += piece
    out_ref[...] = total_ref[...].T


def last(at, held, middle, terms, each):
    per = held.shape[1]
    operands = [held, middle, *terms]
    return pl.pallas_call(
        functools.partial(last_kernel, each),
        grid_spec=pltpu.PrefetchScalarGridSpec(
            num_scalar_prefetch=1,
            grid=(1,),
            in_specs=[whole(x.shape) for x in operands],
            out_specs=whole((per, FB)),
            scratch_shapes=[pltpu.VMEM((FB, per), F32)],
        ),
        out_shape=jax.ShapeDtypeStruct((per, FB), F32),
        compiler_params=params(),
        cost_estimate=SHORT,
        name="last",
    )(at, *operands)


def arrivals(n):
    order = []
    for z in range(n):
        found = [(hops, 0) for hops in range(1, n) if z + hops < n]
        found += [(hops, 1) for hops in range(1, n) if z - hops >= 0]
        order.append(sorted(found))
    return [[order[z][slot] for z in range(n)] for slot in range(n - 1)]


def travel(came, held, n, hops, after):
    if hops > 1:
        held = gate(held, *after, cost=LONG)
        came[(hops - 1, 0)], came[(hops - 1, 1)] = held
    pairs = [
        [(p, p - 1) for p in range(1, n - hops + 1)],
        [(p, p + 1) for p in range(hops - 1, n - 1)],
    ]
    held = [lax.ppermute(held[d], "narrow", pairs[d]) for d in (0, 1)]
    came[(hops, 0)], came[(hops, 1)] = held
    return held


def options(came, places, z):
    choices = sorted(set(places))
    which = jnp.int32(0)
    for p, place in enumerate(places):
        which = jnp.where(z == p, choices.index(place), which)
    return [came[choice] for choice in choices], which


def source(places, z):
    value = jnp.int32(0)
    for p, (hops, direction) in enumerate(places):
        value = jnp.where(z == p, p - hops if direction else p + hops, value)
    return value


def swap(x, wide, distance):
    return lax.ppermute(x, "wide", [(i, i ^ distance) for i in range(wide)])


def scatter_terms(even, odd, wide, after):
    (other,) = gate([swap(odd, wide, 1)], after)
    sums = [even[h] + other[h] for h in range(wide // 2)]
    return [sums[0]] + [swap(sums[h], wide, 2 * h) for h in range(1, wide // 2)]


def collect(x, wide, after=()):
    pieces = [swap(x, wide, 2 * h) for h in range(1, wide // 2)]
    if after:
        (x,) = gate([x], *after)
    even = jnp.stack([x, *pieces])
    return even, swap(even, wide, 1)


def on_device(vectors, reflectors, triangle, energies):
    n = lax.axis_size("narrow")
    wide = lax.axis_size("wide")
    z = lax.axis_index("narrow").astype(jnp.int32)
    me = lax.axis_index("wide").astype(jnp.int32).reshape(1)
    each = FB // n
    rows, columns = vectors.shape
    nb = reflectors.shape[1]
    k = nb + each
    per = columns // wide
    e_row = energies.reshape(1, rows)

    own = energies[:, None] * vectors[:, OFF : OFF + each]
    came = {}
    held = travel(came, [own, own], n, 1, [])
    table = arrivals(n)
    at = jnp.stack([me[0], z] + [source(places, z) for places in table])

    ride = k // wide if per == nb and k % (8 * wide) == 0 else 0
    even, odd, sums, small = project(me, vectors, reflectors, e_row, own, wide, ride)
    if n > 2:
        held = travel(came, held, n, 2, [small])
    ready = lax.psum_scatter(sums, "wide", scatter_dimension=0)

    projected = functools.reduce(jnp.add, scatter_terms(even, odd, wide, came[(1, 0)]))
    highest = lax.Precision.HIGHEST
    coefficients = jnp.dot(triangle, projected[:nb], precision=highest)
    payload = coefficients
    if ride:
        payload = jnp.concatenate([coefficients, projected[nb:]], axis=0)
    c = collect(payload, wide)

    of = next(x for x in range(4, rows) if rows % (16 * x) == 0)
    updated, token = update(me, vectors, reflectors, c, 0, of // 2, of, [], [])
    for hops in range(3, n):
        held = travel(came, held, n, hops, [token])
    updated, token = update(
        me, vectors, reflectors, c, of // 2, of - of // 2, of, [came[(n - 2, 0)]], [updated]
    )

    slots = [options(came, places, z) for places in table]
    (middle,) = late(me, updated, slots[:-1], token, wide, True)
    middle_sum = lax.psum_scatter(middle, "wide", scatter_dimension=0)
    (ready,) = gate([ready], middle)
    even, odd = late(me, updated, slots[-1:], ready, wide, False)
    mine = own_columns(me, c, odd, nb, each)
    coef = [mine] + [
        lax.ppermute(mine, "narrow", [(p, (p + s) % n) for p in range(n)]) for s in range(1, n)
    ]
    tail = scatter_terms(even, odd, wide, mine)
    (ready,) = gate([ready], tail[0])
    small = c if ride else [lax.psum(small, "wide")]
    base_block = base(at, ready, coefficients, coef, small, n, each, ride)
    return (updated, last(at, base_block, middle_sum, tail, each))


def solution(mesh):
    return jax.shard_map(
        on_device,
        mesh=mesh,
        in_specs=(P("wide", "narrow"), P("wide", None), P(), P("wide")),
        out_specs=(P("wide", "narrow"), P(("narrow", "wide"), None)),
        check_vma=False,
    )
```

```python
import functools

import jax
import jax.numpy as jnp
from jax import lax
from jax.experimental import pallas as pl
from jax.experimental.pallas import tpu as pltpu
from jax.sharding import PartitionSpec as P

FB = 512
OFF = 256
VMEM = 60 * 1024 * 1024

F32 = jnp.float32
BF16 = jnp.bfloat16
LONG = pl.CostEstimate(flops=10**11, bytes_accessed=1024, transcendentals=0)
SHORT = pl.CostEstimate(flops=1024, bytes_accessed=1024, transcendentals=0)


def split(x):
    high = x.astype(BF16)
    return high, (x - high.astype(F32)).astype(BF16)


def mul(left, right):
    return jnp.dot(left, right, preferred_element_type=F32)


def three(left, right):
    (lh, ll), (rh, rl) = left, right
    return mul(lh, rh) + mul(ll, rh) + mul(lh, rl)


def stacked(both, high, right):
    rh, rl = right
    m = high.shape[0]
    top = mul(both, rh)
    return top[:m] + top[m:] + mul(high, rl)


def params():
    return pltpu.CompilerParams(
        dimension_semantics=("arbitrary",), vmem_limit_bytes=VMEM
    )


def width(columns, wide):
    return 256 if columns % 256 == 0 and 256 % (columns // wide) == 0 else columns // wide


def whole(shape):
    return pl.BlockSpec(shape, lambda j, *_: (0,) * len(shape), pipeline_mode=pl.Buffered(1))


ANY = pl.BlockSpec(memory_space=pl.ANY)


def gate_kernel(*refs):
    del refs


def gate(held, *others, cost=SHORT):
    count = len(held)
    return pl.pallas_call(
        gate_kernel,
        in_specs=[ANY] * (count + len(others)),
        out_specs=[ANY] * count,
        out_shape=[jax.ShapeDtypeStruct(x.shape, x.dtype) for x in held],
        input_output_aliases={k: k for k in range(count)},
        cost_estimate=cost,
        name="gate",
    )(*held, *others)


def place(value, index, even_ref, odd_ref, first):
    half = index // 2
    rows = value.shape[0]

    @pl.when(index % 2 == 0)
    def _():
        even_ref[half, first : first + rows] = value

    @pl.when(index % 2 == 1)
    def _():
        odd_ref[half, first : first + rows] = value


def take(index, even_ref, odd_ref, rows):
    half = index // 2
    return jnp.where(index % 2 == 0, even_ref[half, rows], odd_ref[half, rows])


def project_kernel(per, wide, me_ref, v_ref, r_ref, e_ref, x_ref, even_ref, odd_ref, sums_ref, small_ref, both_ref):
    j = pl.program_id(0)
    nb = r_ref.shape[1]
    m = both_ref.shape[0] // 2
    k = m - nb
    ride = even_ref.shape[1] - nb

    @pl.when(j == 0)
    def _():
        turned = r_ref[...].T
        first = 0
        for part in (turned, turned * e_ref[...], x_ref[...].T):
            end = first + part.shape[0]
            both_ref[first:end], both_ref[m + first : m + end] = split(part)
            first = end
        small = three((both_ref[nb:m], both_ref[m + nb :]), split(r_ref[...]))
        small_ref[...] = small
        if ride:
            for w in range(wide):
                share = small[w * ride : (w + 1) * ride]
                place(share, w ^ me_ref[0], even_ref, odd_ref, nb)

    value = stacked(both_ref[...], both_ref[:m], split(v_ref[...]))
    count = v_ref.shape[1] // per
    for g in range(count):
        part = value[:, g * per : (g + 1) * per]
        place(part[:nb], (j * count + g) ^ me_ref[0], even_ref, odd_ref, 0)
        sums_ref[g] = part[nb:]


def project(me, vectors, reflectors, e_row, block, wide, ride):
    rows, columns = vectors.shape
    nb = reflectors.shape[1]
    k = nb + block.shape[1]
    per = columns // wide
    step = width(columns, wide)
    shapes = [(wide // 2, nb + ride, per)] * 2 + [(wide, k, per), (k, nb)]
    specs = [whole(x) for x in shapes]
    specs[2] = pl.BlockSpec((step // per, k, per), lambda j, *_: (j, 0, 0))
    return pl.pallas_call(
        functools.partial(project_kernel, per, wide),
        grid_spec=pltpu.PrefetchScalarGridSpec(
            num_scalar_prefetch=1,
            grid=(columns // step,),
            in_specs=[pl.BlockSpec((rows, step), lambda j, *_: (0, j))]
            + [whole(x) for x in ((rows, nb), (1, rows), block.shape)],
            out_specs=specs,
            scratch_shapes=[pltpu.VMEM((2 * (nb + k), rows), BF16)],
        ),
        out_shape=[jax.ShapeDtypeStruct(x, F32) for x in shapes],
        compiler_params=params(),
        cost_estimate=SHORT,
        name="project",
    )(me, vectors, reflectors, e_row, block)


def update_kernel(me_ref, v_ref, r_ref, even_ref, odd_ref, *refs):
    out_ref, token_ref, right_ref = refs[-3:]
    nb = r_ref.shape[1]
    per = even_ref.shape[2]

    @pl.when(pl.program_id(0) == 0)
    def _():
        token_ref[...] = jnp.zeros_like(token_ref)
        for w in range(2 * even_ref.shape[0]):
            high, low = split(take(w ^ me_ref[0], even_ref, odd_ref, slice(0, nb)))
            here = slice(w * per, (w + 1) * per)
            right_ref[:nb, here] = high
            right_ref[nb : 2 * nb, here] = high
            right_ref[2 * nb :, here] = low

    high, low = split(r_ref[...])
    left = jnp.concatenate([high, low, high], axis=1)
    out_ref[...] = v_ref[...] - mul(left, right_ref[...])


def update(me, vectors, reflectors, c, first, count, of, others, before):
    rows, columns = vectors.shape
    nb = reflectors.shape[1]
    operands = [me, vectors, reflectors, *c, *others, *before]
    return pl.pallas_call(
        update_kernel,
        grid_spec=pltpu.PrefetchScalarGridSpec(
            num_scalar_prefetch=1,
            grid=(count,),
            in_specs=[
                pl.BlockSpec((rows // of, columns), lambda j, *_: (j + first, 0)),
                pl.BlockSpec((rows // of, nb), lambda j, *_: (j + first, 0)),
            ]
            + [whole(x.shape) for x in c]
            + [ANY] * (len(operands) - 5),
            out_specs=[
                pl.BlockSpec((rows // of, columns), lambda j, *_: (j + first, 0)),
                whole((8, 128)),
            ],
            scratch_shapes=[pltpu.VMEM((3 * nb, columns), BF16)],
        ),
        out_shape=[
            jax.ShapeDtypeStruct(vectors.shape, F32),
            jax.ShapeDtypeStruct((8, 128), F32),
        ],
        input_output_aliases={len(operands) - 1: 0} if before else {},
        compiler_params=params(),
        cost_estimate=SHORT,
        name="update",
    )(*operands)


def late_kernel(per, counts, at_ref, u_ref, after_ref, *refs):
    *refs, both_ref, block_ref, sem_ref = refs
    outs = refs[sum(counts) :]
    j = pl.program_id(0)
    m = both_ref.shape[0] // 2
    each = block_ref.shape[2]

    @pl.when(j == 0)
    def _():
        first = 0
        for s, count in enumerate(counts):
            for k, ref in enumerate(refs[first : first + count]):

                @pl.when(at_ref[1 + s] == k)
                def _(ref=ref, s=s):
                    pltpu.make_async_copy(ref, block_ref.at[s], sem_ref.at[s]).start()

            first += count
        for s in range(len(counts)):
            pltpu.make_async_copy(block_ref.at[s], block_ref.at[s], sem_ref.at[s]).wait()
            high, low = split(block_ref[s].T)
            both_ref[s * each : (s + 1) * each] = high
            both_ref[m + s * each : m + (s + 1) * each] = low

    value = stacked(both_ref[...], both_ref[:m], split(u_ref[...]))
    count = u_ref.shape[1] // per
    for g in range(count):
        part = value[:, g * per : (g + 1) * per]
        if len(outs) == 2:
            place(part, (j * count + g) ^ at_ref[0], *outs, 0)
        else:
            outs[0][g] = part


def late(me, updated, slots, after, wide, ordered):
    rows, columns = updated.shape
    per = columns // wide
    step = width(columns, wide)
    flat = [x for choices, _ in slots for x in choices]
    counts = [len(choices) for choices, _ in slots]
    each = flat[0].shape[1]
    m = each * len(slots)
    at = jnp.stack([me[0]] + [which.astype(jnp.int32) for _, which in slots])
    if ordered:
        shapes = [(wide, m, per)]
        specs = [pl.BlockSpec((step // per, m, per), lambda j, *_: (j, 0, 0))]
    else:
        shapes = [(wide // 2, m, per)] * 2
        specs = [whole(x) for x in shapes]
    return pl.pallas_call(
        functools.partial(late_kernel, per, counts),
        grid_spec=pltpu.PrefetchScalarGridSpec(
            num_scalar_prefetch=1,
            grid=(columns // step,),
            in_specs=[pl.BlockSpec((rows, step), lambda j, *_: (0, j))] + [ANY] * (1 + len(flat)),
            out_specs=specs,
            scratch_shapes=[
                pltpu.VMEM((2 * m, rows), BF16),
                pltpu.VMEM((len(slots), rows, each), F32),
                pltpu.SemaphoreType.DMA((len(slots),)),
            ],
        ),
        out_shape=[jax.ShapeDtypeStruct(x, F32) for x in shapes],
        compiler_params=params(),
        cost_estimate=SHORT if ordered else LONG,
        name="late",
    )(at, updated, after, *flat)


def own_kernel(me_ref, even_ref, odd_ref, after_ref, out_ref):
    each, nb = out_ref.shape
    per = even_ref.shape[2]
    block = jnp.where(
        ((OFF // per) ^ me_ref[0]) % 2 == 0, even_ref[0, :nb], odd_ref[0, :nb]
    )
    out_ref[...] = block[:, OFF % per : OFF % per + each].T


def own_columns(me, c, after, nb, each):
    per = c[0].shape[2]
    block = pl.BlockSpec(
        (1, *c[0].shape[1:]), lambda j, me_ref: (((OFF // per) ^ me_ref[0]) // 2, 0, 0)
    )
    return pl.pallas_call(
        own_kernel,
        grid_spec=pltpu.PrefetchScalarGridSpec(
            num_scalar_prefetch=1,
            grid=(1,),
            in_specs=[block, block, ANY],
            out_specs=whole((each, nb)),
        ),
        out_shape=jax.ShapeDtypeStruct((each, nb), F32),
        compiler_params=params(),
        cost_estimate=SHORT,
        name="own_columns",
    )(me, *c, after)


def base_kernel(n, each, ride, at_ref, ready_ref, c_ref, *refs):
    *refs, out_ref, coef_ref, small_ref = refs
    me, z = at_ref[0], at_ref[1]
    nb = c_ref.shape[0]
    k = small_ref.shape[0]
    for s in range(n):
        first = pl.multiple_of((z + n - s) % n * each, each)
        coef_ref[pl.ds(first, each), :] = refs[s][...]
    if ride:
        wide = 2 * refs[n].shape[0]
        for w in range(wide):
            small_ref[w * (k // wide) : (w + 1) * (k // wide)] = take(
                w ^ me, *refs[n:], slice(nb, nb + k // wide)
            )
    else:
        small_ref[...] = refs[n][...]
    corrected = ready_ref[...] - three(split(small_ref[...]), split(c_ref[...]))
    out_ref[...] = -three(split(coef_ref[...]), split(corrected[:nb]))
    out_ref[pl.ds(pl.multiple_of(z * each, each), each), :] += corrected[nb:]


def base(at, ready, c, coef, small, n, each, ride):
    operands = [ready, c, *coef, *small]
    k, per = ready.shape
    nb = c.shape[0]
    return pl.pallas_call(
        functools.partial(base_kernel, n, each, ride),
        grid_spec=pltpu.PrefetchScalarGridSpec(
            num_scalar_prefetch=1,
            grid=(1,),
            in_specs=[whole(x.shape) for x in operands],
            out_specs=whole((FB, per)),
            scratch_shapes=[pltpu.VMEM((FB, nb), F32), pltpu.VMEM((k, nb), F32)],
        ),
        out_shape=jax.ShapeDtypeStruct((FB, per), F32),
        compiler_params=params(),
        cost_estimate=SHORT,
        name="base",
    )(at, *operands)


def last_kernel(each, at_ref, base_ref, middle_ref, *refs):
    *refs, out_ref, total_ref = refs
    total_ref[...] = base_ref[...]
    total = functools.reduce(jnp.add, [ref[...] for ref in refs])
    middle = middle_ref[...]
    pieces = [middle[k : k + each] for k in range(0, middle.shape[0], each)] + [total]
    for slot, piece in enumerate(pieces):
        first = pl.multiple_of(at_ref[2 + slot] * each, each)
        total_ref[pl.ds(first, each), :] += piece
    out_ref[...] = total_ref[...].T


def last(at, held, middle, terms, each):
    per = held.shape[1]
    operands = [held, middle, *terms]
    return pl.pallas_call(
        functools.partial(last_kernel, each),
        grid_spec=pltpu.PrefetchScalarGridSpec(
            num_scalar_prefetch=1,
            grid=(1,),
            in_specs=[whole(x.shape) for x in operands],
            out_specs=whole((per, FB)),
            scratch_shapes=[pltpu.VMEM((FB, per), F32)],
        ),
        out_shape=jax.ShapeDtypeStruct((per, FB), F32),
        compiler_params=params(),
        cost_estimate=SHORT,
        name="last",
    )(at, *operands)


def arrivals(n):
    order = []
    for z in range(n):
        found = [(hops, 0) for hops in range(1, n) if z + hops < n]
        found += [(hops, 1) for hops in range(1, n) if z - hops >= 0]
        order.append(sorted(found))
    return [[order[z][slot] for z in range(n)] for slot in range(n - 1)]


def travel(came, held, n, hops, after):
    if hops > 1:
        held = gate(held, *after, cost=LONG)
        came[(hops - 1, 0)], came[(hops - 1, 1)] = held
    pairs = [
        [(p, p - 1) for p in range(1, n - hops + 1)],
        [(p, p + 1) for p in range(hops - 1, n - 1)],
    ]
    held = [lax.ppermute(held[d], "narrow", pairs[d]) for d in (0, 1)]
    came[(hops, 0)], came[(hops, 1)] = held
    return held


def options(came, places, z):
    choices = sorted(set(places))
    which = jnp.int32(0)
    for p, place in enumerate(places):
        which = jnp.where(z == p, choices.index(place), which)
    return [came[choice] for choice in choices], which


def source(places, z):
    value = jnp.int32(0)
    for p, (hops, direction) in enumerate(places):
        value = jnp.where(z == p, p - hops if direction else p + hops, value)
    return value


def swap(x, wide, distance):
    return lax.ppermute(x, "wide", [(i, i ^ distance) for i in range(wide)])


def scatter_terms(even, odd, wide, after):
    (other,) = gate([swap(odd, wide, 1)], after)
    sums = [even[h] + other[h] for h in range(wide // 2)]
    return [sums[0]] + [swap(sums[h], wide, 2 * h) for h in range(1, wide // 2)]


def collect(x, wide, after=()):
    pieces = [swap(x, wide, 2 * h) for h in range(1, wide // 2)]
    if after:
        (x,) = gate([x], *after)
    even = jnp.stack([x, *pieces])
    return even, swap(even, wide, 1)


def on_device(vectors, reflectors, triangle, energies):
    n = lax.axis_size("narrow")
    wide = lax.axis_size("wide")
    z = lax.axis_index("narrow").astype(jnp.int32)
    me = lax.axis_index("wide").astype(jnp.int32).reshape(1)
    each = FB // n
    rows, columns = vectors.shape
    nb = reflectors.shape[1]
    k = nb + each
    per = columns // wide
    e_row = energies.reshape(1, rows)

    own = energies[:, None] * vectors[:, OFF : OFF + each]
    came = {}
    held = travel(came, [own, own], n, 1, [])
    table = arrivals(n)
    at = jnp.stack([me[0], z] + [source(places, z) for places in table])

    ride = k // wide if per == nb and k % (8 * wide) == 0 else 0
    even, odd, sums, small = project(me, vectors, reflectors, e_row, own, wide, ride)
    if n > 2:
        held = travel(came, held, n, 2, [small])
    ready = lax.psum_scatter(sums, "wide", scatter_dimension=0)

    projected = functools.reduce(jnp.add, scatter_terms(even, odd, wide, came[(1, 0)]))
    highest = lax.Precision.HIGHEST
    coefficients = jnp.dot(triangle, projected[:nb], precision=highest)
    payload = coefficients
    if ride:
        payload = jnp.concatenate([coefficients, projected[nb:]], axis=0)
    c = collect(payload, wide)

    of = next(x for x in range(4, rows) if rows % (16 * x) == 0)
    updated, token = update(me, vectors, reflectors, c, 0, of // 2, of, [], [])
    for hops in range(3, n):
        held = travel(came, held, n, hops, [token])
    updated, token = update(
        me, vectors, reflectors, c, of // 2, of - of // 2, of, [came[(n - 2, 0)]], [updated]
    )

    slots = [options(came, places, z) for places in table]
    (middle,) = late(me, updated, slots[:-1], token, wide, True)
    middle_sum = lax.psum_scatter(middle, "wide", scatter_dimension=0)
    (ready,) = gate([ready], middle)
    even, odd = late(me, updated, slots[-1:], ready, wide, False)
    mine = own_columns(me, c, odd, nb, each)
    coef = [mine] + [
        lax.ppermute(mine, "narrow", [(p, (p + s) % n) for p in range(n)]) for s in range(1, n)
    ]
    tail = scatter_terms(even, odd, wide, mine)
    (ready,) = gate([ready], tail[0])
    small = c if ride else [lax.psum(small, "wide")]
    base_block = base(at, ready, coefficients, coef, small, n, each, ride)
    return (updated, last(at, base_block, middle_sum, tail, each))


def solution(mesh):
    return jax.shard_map(
        on_device,
        mesh=mesh,
        in_specs=(P("wide", "narrow"), P("wide", None), P(), P("wide")),
        out_specs=(P("wide", "narrow"), P(("narrow", "wide"), None)),
        check_vma=False,
    )
```

```python
import functools

import jax
import jax.numpy as jnp
from jax import lax
from jax.experimental import pallas as pl
from jax.experimental.pallas import tpu as pltpu
from jax.sharding import PartitionSpec as P

FB = 512
OFF = 256
VMEM = 60 * 1024 * 1024

F32 = jnp.float32
BF16 = jnp.bfloat16
LONG = pl.CostEstimate(flops=10**11, bytes_accessed=1024, transcendentals=0)
SHORT = pl.CostEstimate(flops=1024, bytes_accessed=1024, transcendentals=0)


def split(x):
    high = x.astype(BF16)
    return high, (x - high.astype(F32)).astype(BF16)


def mul(left, right):
    return jnp.dot(left, right, preferred_element_type=F32)


def three(left, right):
    (lh, ll), (rh, rl) = left, right
    return mul(lh, rh) + mul(ll, rh) + mul(lh, rl)


def stacked(both, high, right):
    rh, rl = right
    m = high.shape[0]
    top = mul(both, rh)
    return top[:m] + top[m:] + mul(high, rl)


def params():
    return pltpu.CompilerParams(
        dimension_semantics=("arbitrary",), vmem_limit_bytes=VMEM
    )


def width(columns, wide):
    fits = (x for x in (512, 256) if columns % x == 0 and x % (columns // wide) == 0)
    return next(fits, columns // wide)


def whole(shape):
    return pl.BlockSpec(shape, lambda j, *_: (0,) * len(shape), pipeline_mode=pl.Buffered(1))


ANY = pl.BlockSpec(memory_space=pl.ANY)


def gate_kernel(*refs):
    del refs


def gate(held, *others, cost=SHORT):
    count = len(held)
    return pl.pallas_call(
        gate_kernel,
        in_specs=[ANY] * (count + len(others)),
        out_specs=[ANY] * count,
        out_shape=[jax.ShapeDtypeStruct(x.shape, x.dtype) for x in held],
        input_output_aliases={k: k for k in range(count)},
        cost_estimate=cost,
        name="gate",
    )(*held, *others)


def place(value, index, even_ref, odd_ref, first):
    half = index // 2
    rows = value.shape[0]

    @pl.when(index % 2 == 0)
    def _():
        even_ref[half, first : first + rows] = value

    @pl.when(index % 2 == 1)
    def _():
        odd_ref[half, first : first + rows] = value


def take(index, even_ref, odd_ref, rows):
    half = index // 2
    return jnp.where(index % 2 == 0, even_ref[half, rows], odd_ref[half, rows])


def project_kernel(per, wide, me_ref, v_ref, r_ref, e_ref, x_ref, even_ref, odd_ref, sums_ref, small_ref, both_ref):
    j = pl.program_id(0)
    nb = r_ref.shape[1]
    m = both_ref.shape[0] // 2
    k = m - nb
    ride = even_ref.shape[1] - nb

    @pl.when(j == 0)
    def _():
        turned = r_ref[...].T
        first = 0
        for part in (turned, turned * e_ref[...], x_ref[...].T):
            end = first + part.shape[0]
            both_ref[first:end], both_ref[m + first : m + end] = split(part)
            first = end
        small = three((both_ref[nb:m], both_ref[m + nb :]), split(r_ref[...]))
        small_ref[...] = small
        if ride:
            for w in range(wide):
                share = small[w * ride : (w + 1) * ride]
                place(share, w ^ me_ref[0], even_ref, odd_ref, nb)

    value = stacked(both_ref[...], both_ref[:m], split(v_ref[...]))
    count = v_ref.shape[1] // per
    for g in range(count):
        part = value[:, g * per : (g + 1) * per]
        place(part[:nb], (j * count + g) ^ me_ref[0], even_ref, odd_ref, 0)
        sums_ref[g] = part[nb:]


def project(me, vectors, reflectors, e_row, block, wide, ride):
    rows, columns = vectors.shape
    nb = reflectors.shape[1]
    k = nb + block.shape[1]
    per = columns // wide
    step = width(columns, wide)
    shapes = [(wide // 2, nb + ride, per)] * 2 + [(wide, k, per), (k, nb)]
    specs = [whole(x) for x in shapes]
    specs[2] = pl.BlockSpec((step // per, k, per), lambda j, *_: (j, 0, 0))
    return pl.pallas_call(
        functools.partial(project_kernel, per, wide),
        grid_spec=pltpu.PrefetchScalarGridSpec(
            num_scalar_prefetch=1,
            grid=(columns // step,),
            in_specs=[pl.BlockSpec((rows, step), lambda j, *_: (0, j))]
            + [whole(x) for x in ((rows, nb), (1, rows), block.shape)],
            out_specs=specs,
            scratch_shapes=[pltpu.VMEM((2 * (nb + k), rows), BF16)],
        ),
        out_shape=[jax.ShapeDtypeStruct(x, F32) for x in shapes],
        compiler_params=params(),
        cost_estimate=SHORT,
        name="project",
    )(me, vectors, reflectors, e_row, block)


def update_kernel(me_ref, v_ref, r_ref, even_ref, odd_ref, *refs):
    out_ref, token_ref, right_ref = refs[-3:]
    nb = r_ref.shape[1]
    per = even_ref.shape[2]

    @pl.when(pl.program_id(0) == 0)
    def _():
        token_ref[...] = jnp.zeros_like(token_ref)
        for w in range(2 * even_ref.shape[0]):
            high, low = split(take(w ^ me_ref[0], even_ref, odd_ref, slice(0, nb)))
            here = slice(w * per, (w + 1) * per)
            right_ref[:nb, here] = high
            right_ref[nb : 2 * nb, here] = high
            right_ref[2 * nb :, here] = low

    high, low = split(r_ref[...])
    left = jnp.concatenate([high, low, high], axis=1)
    out_ref[...] = v_ref[...] - mul(left, right_ref[...])


def update(me, vectors, reflectors, c, first, count, of, others, before):
    rows, columns = vectors.shape
    nb = reflectors.shape[1]
    operands = [me, vectors, reflectors, *c, *others, *before]
    return pl.pallas_call(
        update_kernel,
        grid_spec=pltpu.PrefetchScalarGridSpec(
            num_scalar_prefetch=1,
            grid=(count,),
            in_specs=[
                pl.BlockSpec((rows // of, columns), lambda j, *_: (j + first, 0)),
                pl.BlockSpec((rows // of, nb), lambda j, *_: (j + first, 0)),
            ]
            + [whole(x.shape) for x in c]
            + [ANY] * (len(operands) - 5),
            out_specs=[
                pl.BlockSpec((rows // of, columns), lambda j, *_: (j + first, 0)),
                whole((8, 128)),
            ],
            scratch_shapes=[pltpu.VMEM((3 * nb, columns), BF16)],
        ),
        out_shape=[
            jax.ShapeDtypeStruct(vectors.shape, F32),
            jax.ShapeDtypeStruct((8, 128), F32),
        ],
        input_output_aliases={len(operands) - 1: 0} if before else {},
        compiler_params=params(),
        cost_estimate=SHORT,
        name="update",
    )(*operands)


def late_kernel(per, counts, at_ref, u_ref, after_ref, *refs):
    *refs, both_ref, block_ref, sem_ref = refs
    outs = refs[sum(counts) :]
    j = pl.program_id(0)
    m = both_ref.shape[0] // 2
    each = block_ref.shape[2]

    @pl.when(j == 0)
    def _():
        first = 0
        for s, count in enumerate(counts):
            for k, ref in enumerate(refs[first : first + count]):

                @pl.when(at_ref[1 + s] == k)
                def _(ref=ref, s=s):
                    pltpu.make_async_copy(ref, block_ref.at[s], sem_ref.at[s]).start()

            first += count
        for s in range(len(counts)):
            pltpu.make_async_copy(block_ref.at[s], block_ref.at[s], sem_ref.at[s]).wait()
            high, low = split(block_ref[s].T)
            both_ref[s * each : (s + 1) * each] = high
            both_ref[m + s * each : m + (s + 1) * each] = low

    value = stacked(both_ref[...], both_ref[:m], split(u_ref[...]))
    count = u_ref.shape[1] // per
    for g in range(count):
        part = value[:, g * per : (g + 1) * per]
        if len(outs) == 2:
            place(part, (j * count + g) ^ at_ref[0], *outs, 0)
        else:
            outs[0][g] = part


def late(me, updated, slots, after, wide, ordered):
    rows, columns = updated.shape
    per = columns // wide
    step = width(columns, wide)
    flat = [x for choices, _ in slots for x in choices]
    counts = [len(choices) for choices, _ in slots]
    each = flat[0].shape[1]
    m = each * len(slots)
    at = jnp.stack([me[0]] + [which.astype(jnp.int32) for _, which in slots])
    if ordered:
        shapes = [(wide, m, per)]
        specs = [pl.BlockSpec((step // per, m, per), lambda j, *_: (j, 0, 0))]
    else:
        shapes = [(wide // 2, m, per)] * 2
        specs = [whole(x) for x in shapes]
    return pl.pallas_call(
        functools.partial(late_kernel, per, counts),
        grid_spec=pltpu.PrefetchScalarGridSpec(
            num_scalar_prefetch=1,
            grid=(columns // step,),
            in_specs=[pl.BlockSpec((rows, step), lambda j, *_: (0, j))] + [ANY] * (1 + len(flat)),
            out_specs=specs,
            scratch_shapes=[
                pltpu.VMEM((2 * m, rows), BF16),
                pltpu.VMEM((len(slots), rows, each), F32),
                pltpu.SemaphoreType.DMA((len(slots),)),
            ],
        ),
        out_shape=[jax.ShapeDtypeStruct(x, F32) for x in shapes],
        compiler_params=params(),
        cost_estimate=SHORT if ordered else LONG,
        name="late",
    )(at, updated, after, *flat)


def own_kernel(me_ref, even_ref, odd_ref, after_ref, out_ref):
    each, nb = out_ref.shape
    per = even_ref.shape[2]
    block = jnp.where(
        ((OFF // per) ^ me_ref[0]) % 2 == 0, even_ref[0, :nb], odd_ref[0, :nb]
    )
    out_ref[...] = block[:, OFF % per : OFF % per + each].T


def own_columns(me, c, after, nb, each):
    per = c[0].shape[2]
    block = pl.BlockSpec(
        (1, *c[0].shape[1:]), lambda j, me_ref: (((OFF // per) ^ me_ref[0]) // 2, 0, 0)
    )
    return pl.pallas_call(
        own_kernel,
        grid_spec=pltpu.PrefetchScalarGridSpec(
            num_scalar_prefetch=1,
            grid=(1,),
            in_specs=[block, block, ANY],
            out_specs=whole((each, nb)),
        ),
        out_shape=jax.ShapeDtypeStruct((each, nb), F32),
        compiler_params=params(),
        cost_estimate=SHORT,
        name="own_columns",
    )(me, *c, after)


def base_kernel(n, each, ride, at_ref, ready_ref, c_ref, *refs):
    *refs, out_ref, coef_ref, small_ref = refs
    me, z = at_ref[0], at_ref[1]
    nb = c_ref.shape[0]
    k = small_ref.shape[0]
    for s in range(n):
        first = pl.multiple_of((z + n - s) % n * each, each)
        coef_ref[pl.ds(first, each), :] = refs[s][...]
    if ride:
        wide = 2 * refs[n].shape[0]
        for w in range(wide):
            small_ref[w * (k // wide) : (w + 1) * (k // wide)] = take(
                w ^ me, *refs[n:], slice(nb, nb + k // wide)
            )
    else:
        small_ref[...] = refs[n][...]
    corrected = ready_ref[...] - three(split(small_ref[...]), split(c_ref[...]))
    out_ref[...] = -three(split(coef_ref[...]), split(corrected[:nb]))
    out_ref[pl.ds(pl.multiple_of(z * each, each), each), :] += corrected[nb:]


def base(at, ready, c, coef, small, n, each, ride):
    operands = [ready, c, *coef, *small]
    k, per = ready.shape
    nb = c.shape[0]
    return pl.pallas_call(
        functools.partial(base_kernel, n, each, ride),
        grid_spec=pltpu.PrefetchScalarGridSpec(
            num_scalar_prefetch=1,
            grid=(1,),
            in_specs=[whole(x.shape) for x in operands],
            out_specs=whole((FB, per)),
            scratch_shapes=[pltpu.VMEM((FB, nb), F32), pltpu.VMEM((k, nb), F32)],
        ),
        out_shape=jax.ShapeDtypeStruct((FB, per), F32),
        compiler_params=params(),
        cost_estimate=SHORT,
        name="base",
    )(at, *operands)


def last_kernel(each, at_ref, base_ref, middle_ref, *refs):
    *refs, out_ref, total_ref = refs
    total_ref[...] = base_ref[...]
    total = functools.reduce(jnp.add, [ref[...] for ref in refs])
    middle = middle_ref[...]
    pieces = [middle[k : k + each] for k in range(0, middle.shape[0], each)] + [total]
    for slot, piece in enumerate(pieces):
        first = pl.multiple_of(at_ref[2 + slot] * each, each)
        total_ref[pl.ds(first, each), :] += piece
    out_ref[...] = total_ref[...].T


def last(at, held, middle, terms, each):
    per = held.shape[1]
    operands = [held, middle, *terms]
    return pl.pallas_call(
        functools.partial(last_kernel, each),
        grid_spec=pltpu.PrefetchScalarGridSpec(
            num_scalar_prefetch=1,
            grid=(1,),
            in_specs=[whole(x.shape) for x in operands],
            out_specs=whole((per, FB)),
            scratch_shapes=[pltpu.VMEM((FB, per), F32)],
        ),
        out_shape=jax.ShapeDtypeStruct((per, FB), F32),
        compiler_params=params(),
        cost_estimate=SHORT,
        name="last",
    )(at, *operands)


def arrivals(n):
    order = []
    for z in range(n):
        found = [(hops, 0) for hops in range(1, n) if z + hops < n]
        found += [(hops, 1) for hops in range(1, n) if z - hops >= 0]
        order.append(sorted(found))
    return [[order[z][slot] for z in range(n)] for slot in range(n - 1)]


def travel(came, held, n, hops, after):
    if hops > 1:
        held = gate(held, *after, cost=LONG)
        came[(hops - 1, 0)], came[(hops - 1, 1)] = held
    pairs = [
        [(p, p - 1) for p in range(1, n - hops + 1)],
        [(p, p + 1) for p in range(hops - 1, n - 1)],
    ]
    held = [lax.ppermute(held[d], "narrow", pairs[d]) for d in (0, 1)]
    came[(hops, 0)], came[(hops, 1)] = held
    return held


def options(came, places, z):
    choices = sorted(set(places))
    which = jnp.int32(0)
    for p, place in enumerate(places):
        which = jnp.where(z == p, choices.index(place), which)
    return [came[choice] for choice in choices], which


def source(places, z):
    value = jnp.int32(0)
    for p, (hops, direction) in enumerate(places):
        value = jnp.where(z == p, p - hops if direction else p + hops, value)
    return value


def swap(x, wide, distance):
    return lax.ppermute(x, "wide", [(i, i ^ distance) for i in range(wide)])


def add_kernel(even_ref, other_ref, after_ref, *outs):
    for h, out_ref in enumerate(outs):
        out_ref[...] = even_ref[h] + other_ref[h]


def scatter_terms(even, odd, wide, after):
    count, *shape = even.shape
    sums = pl.pallas_call(
        add_kernel,
        in_specs=[pl.BlockSpec(memory_space=pltpu.VMEM)] * 2 + [ANY],
        out_specs=[pl.BlockSpec(memory_space=pltpu.VMEM)] * count,
        out_shape=[jax.ShapeDtypeStruct(shape, F32)] * count,
        compiler_params=pltpu.CompilerParams(vmem_limit_bytes=VMEM),
        cost_estimate=SHORT,
        name="add",
    )(even, swap(odd, wide, 1), after)
    return [sums[0]] + [swap(sums[h], wide, 2 * h) for h in range(1, count)]


def collect(x, wide, after=()):
    pieces = [swap(x, wide, 2 * h) for h in range(1, wide // 2)]
    if after:
        (x,) = gate([x], *after)
    even = jnp.stack([x, *pieces])
    return even, swap(even, wide, 1)


def on_device(vectors, reflectors, triangle, energies):
    n = lax.axis_size("narrow")
    wide = lax.axis_size("wide")
    z = lax.axis_index("narrow").astype(jnp.int32)
    me = lax.axis_index("wide").astype(jnp.int32).reshape(1)
    each = FB // n
    rows, columns = vectors.shape
    nb = reflectors.shape[1]
    k = nb + each
    per = columns // wide
    e_row = energies.reshape(1, rows)

    own = energies[:, None] * vectors[:, OFF : OFF + each]
    came = {}
    held = travel(came, [own, own], n, 1, [])
    table = arrivals(n)
    at = jnp.stack([me[0], z] + [source(places, z) for places in table])

    ride = k // wide if per == nb and k % (8 * wide) == 0 else 0
    even, odd, sums, small = project(me, vectors, reflectors, e_row, own, wide, ride)
    if n > 2:
        held = travel(came, held, n, 2, [small])
    ready = lax.psum_scatter(sums, "wide", scatter_dimension=0)

    projected = functools.reduce(jnp.add, scatter_terms(even, odd, wide, came[(1, 0)]))
    highest = lax.Precision.HIGHEST
    coefficients = jnp.dot(triangle, projected[:nb], precision=highest)
    payload = coefficients
    if ride:
        payload = jnp.concatenate([coefficients, projected[nb:]], axis=0)
    c = collect(payload, wide)

    of = next(x for x in range(4, rows) if rows % (16 * x) == 0)
    updated, token = update(me, vectors, reflectors, c, 0, of // 2, of, [], [])
    for hops in range(3, n):
        held = travel(came, held, n, hops, [token])
    updated, token = update(
        me, vectors, reflectors, c, of // 2, of - of // 2, of, [came[(n - 2, 0)]], [updated]
    )

    slots = [options(came, places, z) for places in table]
    (middle,) = late(me, updated, slots[:-1], token, wide, True)
    middle_sum = lax.psum_scatter(middle, "wide", scatter_dimension=0)
    (ready,) = gate([ready], middle)
    even, odd = late(me, updated, slots[-1:], ready, wide, False)
    mine = own_columns(me, c, odd, nb, each)
    coef = [mine] + [
        lax.ppermute(mine, "narrow", [(p, (p + s) % n) for p in range(n)]) for s in range(1, n)
    ]
    tail = scatter_terms(even, odd, wide, mine)
    (ready,) = gate([ready], tail[0])
    small = c if ride else [lax.psum(small, "wide")]
    base_block = base(at, ready, coefficients, coef, small, n, each, ride)
    return (updated, last(at, base_block, middle_sum, tail, each))


def solution(mesh):
    return jax.shard_map(
        on_device,
        mesh=mesh,
        in_specs=(P("wide", "narrow"), P("wide", None), P(), P("wide")),
        out_specs=(P("wide", "narrow"), P(("narrow", "wide"), None)),
        check_vma=False,
    )
```

```python
import functools

import jax
import jax.numpy as jnp
from jax import lax
from jax.experimental import pallas as pl
from jax.experimental.pallas import tpu as pltpu
from jax.sharding import PartitionSpec as P

FB = 512
OFF = 256
VMEM = 60 * 1024 * 1024
LESS = 29 * 1024 * 1024

F32 = jnp.float32
BF16 = jnp.bfloat16
LONG = pl.CostEstimate(flops=10**11, bytes_accessed=1024, transcendentals=0)
SHORT = pl.CostEstimate(flops=1024, bytes_accessed=1024, transcendentals=0)


def split(x):
    high = x.astype(BF16)
    return high, (x - high.astype(F32)).astype(BF16)


def mul(left, right):
    return jnp.dot(left, right, preferred_element_type=F32)


def three(left, right):
    (lh, ll), (rh, rl) = left, right
    return mul(lh, rh) + mul(ll, rh) + mul(lh, rl)


def stacked(both, high, right):
    rh, rl = right
    m = high.shape[0]
    top = mul(both, rh)
    return top[:m] + top[m:] + mul(high, rl)


def params(limit=VMEM):
    return pltpu.CompilerParams(
        dimension_semantics=("arbitrary",), vmem_limit_bytes=limit
    )


def width(columns, wide):
    return 256 if columns % 256 == 0 and 256 % (columns // wide) == 0 else columns // wide


def whole(shape):
    return pl.BlockSpec(shape, lambda j, *_: (0,) * len(shape), pipeline_mode=pl.Buffered(1))


ANY = pl.BlockSpec(memory_space=pl.ANY)


def gate_kernel(*refs):
    del refs


def gate(held, *others, cost=SHORT):
    count = len(held)
    return pl.pallas_call(
        gate_kernel,
        in_specs=[ANY] * (count + len(others)),
        out_specs=[ANY] * count,
        out_shape=[jax.ShapeDtypeStruct(x.shape, x.dtype) for x in held],
        input_output_aliases={k: k for k in range(count)},
        compiler_params=pltpu.CompilerParams(vmem_limit_bytes=2**20),
        cost_estimate=cost,
        name="gate",
    )(*held, *others)


def place(value, index, even_ref, odd_ref, first):
    half = index // 2
    rows = value.shape[0]

    @pl.when(index % 2 == 0)
    def _():
        even_ref[half, first : first + rows] = value

    @pl.when(index % 2 == 1)
    def _():
        odd_ref[half, first : first + rows] = value


def take(index, even_ref, odd_ref, rows):
    half = index // 2
    return jnp.where(index % 2 == 0, even_ref[half, rows], odd_ref[half, rows])


def project_kernel(per, wide, me_ref, v_ref, r_ref, e_ref, x_ref, even_ref, odd_ref, sums_ref, small_ref, both_ref):
    j = pl.program_id(0)
    nb = r_ref.shape[1]
    m = both_ref.shape[0] // 2
    k = m - nb
    ride = even_ref.shape[1] - nb

    @pl.when(j == 0)
    def _():
        turned = r_ref[...].T
        first = 0
        for part in (turned, turned * e_ref[...], x_ref[...].T):
            end = first + part.shape[0]
            both_ref[first:end], both_ref[m + first : m + end] = split(part)
            first = end
        small = three((both_ref[nb:m], both_ref[m + nb :]), split(r_ref[...]))
        small_ref[...] = small
        if ride:
            for w in range(wide):
                share = small[w * ride : (w + 1) * ride]
                place(share, w ^ me_ref[0], even_ref, odd_ref, nb)

    value = stacked(both_ref[...], both_ref[:m], split(v_ref[...]))
    count = v_ref.shape[1] // per
    for g in range(count):
        part = value[:, g * per : (g + 1) * per]
        place(part[:nb], (j * count + g) ^ me_ref[0], even_ref, odd_ref, 0)
        sums_ref[g] = part[nb:]


def project(me, vectors, reflectors, e_row, block, wide, ride):
    rows, columns = vectors.shape
    nb = reflectors.shape[1]
    k = nb + block.shape[1]
    per = columns // wide
    step = width(columns, wide)
    shapes = [(wide // 2, nb + ride, per)] * 2 + [(wide, k, per), (k, nb)]
    specs = [whole(x) for x in shapes]
    specs[2] = pl.BlockSpec((step // per, k, per), lambda j, *_: (j, 0, 0))
    return pl.pallas_call(
        functools.partial(project_kernel, per, wide),
        grid_spec=pltpu.PrefetchScalarGridSpec(
            num_scalar_prefetch=1,
            grid=(columns // step,),
            in_specs=[pl.BlockSpec((rows, step), lambda j, *_: (0, j))]
            + [whole(x) for x in ((rows, nb), (1, rows), block.shape)],
            out_specs=specs,
            scratch_shapes=[pltpu.VMEM((2 * (nb + k), rows), BF16)],
        ),
        out_shape=[jax.ShapeDtypeStruct(x, F32) for x in shapes],
        compiler_params=params(),
        cost_estimate=SHORT,
        name="project",
    )(me, vectors, reflectors, e_row, block)


def update_kernel(me_ref, v_ref, r_ref, even_ref, odd_ref, *refs):
    out_ref, token_ref, right_ref = refs[-3:]
    nb = r_ref.shape[1]
    per = even_ref.shape[2]

    @pl.when(pl.program_id(0) == 0)
    def _():
        token_ref[...] = jnp.zeros_like(token_ref)
        for w in range(2 * even_ref.shape[0]):
            high, low = split(take(w ^ me_ref[0], even_ref, odd_ref, slice(0, nb)))
            here = slice(w * per, (w + 1) * per)
            right_ref[:nb, here] = high
            right_ref[nb : 2 * nb, here] = high
            right_ref[2 * nb :, here] = low

    high, low = split(r_ref[...])
    left = jnp.concatenate([high, low, high], axis=1)
    out_ref[...] = v_ref[...] - mul(left, right_ref[...])


def update(me, vectors, reflectors, c, first, count, of, others, before):
    rows, columns = vectors.shape
    nb = reflectors.shape[1]
    operands = [me, vectors, reflectors, *c, *others, *before]
    return pl.pallas_call(
        update_kernel,
        grid_spec=pltpu.PrefetchScalarGridSpec(
            num_scalar_prefetch=1,
            grid=(count,),
            in_specs=[
                pl.BlockSpec((rows // of, columns), lambda j, *_: (j + first, 0)),
                pl.BlockSpec((rows // of, nb), lambda j, *_: (j + first, 0)),
            ]
            + [whole(x.shape) for x in c]
            + [ANY] * (len(operands) - 5),
            out_specs=[
                pl.BlockSpec((rows // of, columns), lambda j, *_: (j + first, 0)),
                whole((8, 128)),
            ],
            scratch_shapes=[pltpu.VMEM((3 * nb, columns), BF16)],
        ),
        out_shape=[
            jax.ShapeDtypeStruct(vectors.shape, F32),
            jax.ShapeDtypeStruct((8, 128), F32),
        ],
        input_output_aliases={len(operands) - 1: 0} if before else {},
        compiler_params=params(LESS),
        cost_estimate=SHORT,
        name="update",
    )(*operands)


def late_kernel(per, counts, at_ref, u_ref, after_ref, *refs):
    *refs, both_ref, block_ref, sem_ref = refs
    outs = refs[sum(counts) :]
    j = pl.program_id(0)
    m = both_ref.shape[0] // 2
    each = block_ref.shape[2]

    @pl.when(j == 0)
    def _():
        first = 0
        for s, count in enumerate(counts):
            for k, ref in enumerate(refs[first : first + count]):

                @pl.when(at_ref[1 + s] == k)
                def _(ref=ref, s=s):
                    pltpu.make_async_copy(ref, block_ref.at[s], sem_ref.at[s]).start()

            first += count
        for s in range(len(counts)):
            pltpu.make_async_copy(block_ref.at[s], block_ref.at[s], sem_ref.at[s]).wait()
            high, low = split(block_ref[s].T)
            both_ref[s * each : (s + 1) * each] = high
            both_ref[m + s * each : m + (s + 1) * each] = low

    value = stacked(both_ref[...], both_ref[:m], split(u_ref[...]))
    count = u_ref.shape[1] // per
    for g in range(count):
        part = value[:, g * per : (g + 1) * per]
        if len(outs) == 2:
            place(part, (j * count + g) ^ at_ref[0], *outs, 0)
        else:
            outs[0][g] = part


def late(me, updated, slots, after, wide, ordered):
    rows, columns = updated.shape
    per = columns // wide
    step = width(columns, wide)
    flat = [x for choices, _ in slots for x in choices]
    counts = [len(choices) for choices, _ in slots]
    each = flat[0].shape[1]
    m = each * len(slots)
    at = jnp.stack([me[0]] + [which.astype(jnp.int32) for _, which in slots])
    if ordered:
        shapes = [(wide, m, per)]
        specs = [pl.BlockSpec((step // per, m, per), lambda j, *_: (j, 0, 0))]
    else:
        shapes = [(wide // 2, m, per)] * 2
        specs = [whole(x) for x in shapes]
    return pl.pallas_call(
        functools.partial(late_kernel, per, counts),
        grid_spec=pltpu.PrefetchScalarGridSpec(
            num_scalar_prefetch=1,
            grid=(columns // step,),
            in_specs=[pl.BlockSpec((rows, step), lambda j, *_: (0, j))] + [ANY] * (1 + len(flat)),
            out_specs=specs,
            scratch_shapes=[
                pltpu.VMEM((2 * m, rows), BF16),
                pltpu.VMEM((len(slots), rows, each), F32),
                pltpu.SemaphoreType.DMA((len(slots),)),
            ],
        ),
        out_shape=[jax.ShapeDtypeStruct(x, F32) for x in shapes],
        compiler_params=params(LESS),
        cost_estimate=SHORT if ordered else LONG,
        name="late",
    )(at, updated, after, *flat)


def own_kernel(me_ref, even_ref, odd_ref, after_ref, out_ref):
    each, nb = out_ref.shape
    per = even_ref.shape[2]
    block = jnp.where(
        ((OFF // per) ^ me_ref[0]) % 2 == 0, even_ref[0, :nb], odd_ref[0, :nb]
    )
    out_ref[...] = block[:, OFF % per : OFF % per + each].T


def own_columns(me, c, after, nb, each):
    per = c[0].shape[2]
    block = pl.BlockSpec(
        (1, *c[0].shape[1:]), lambda j, me_ref: (((OFF // per) ^ me_ref[0]) // 2, 0, 0)
    )
    return pl.pallas_call(
        own_kernel,
        grid_spec=pltpu.PrefetchScalarGridSpec(
            num_scalar_prefetch=1,
            grid=(1,),
            in_specs=[block, block, ANY],
            out_specs=whole((each, nb)),
        ),
        out_shape=jax.ShapeDtypeStruct((each, nb), F32),
        compiler_params=params(),
        cost_estimate=SHORT,
        name="own_columns",
    )(me, *c, after)


def base_kernel(n, each, ride, at_ref, ready_ref, c_ref, *refs):
    *refs, out_ref, coef_ref, small_ref = refs
    me, z = at_ref[0], at_ref[1]
    nb = c_ref.shape[0]
    k = small_ref.shape[0]
    for s in range(n):
        first = pl.multiple_of((z + n - s) % n * each, each)
        coef_ref[pl.ds(first, each), :] = refs[s][...]
    if ride:
        wide = 2 * refs[n].shape[0]
        for w in range(wide):
            small_ref[w * (k // wide) : (w + 1) * (k // wide)] = take(
                w ^ me, *refs[n:], slice(nb, nb + k // wide)
            )
    else:
        small_ref[...] = refs[n][...]
    corrected = ready_ref[...] - three(split(small_ref[...]), split(c_ref[...]))
    out_ref[...] = -three(split(coef_ref[...]), split(corrected[:nb]))
    out_ref[pl.ds(pl.multiple_of(z * each, each), each), :] += corrected[nb:]


def base(at, ready, c, coef, small, n, each, ride):
    operands = [ready, c, *coef, *small]
    k, per = ready.shape
    nb = c.shape[0]
    return pl.pallas_call(
        functools.partial(base_kernel, n, each, ride),
        grid_spec=pltpu.PrefetchScalarGridSpec(
            num_scalar_prefetch=1,
            grid=(1,),
            in_specs=[whole(x.shape) for x in operands],
            out_specs=whole((FB, per)),
            scratch_shapes=[pltpu.VMEM((FB, nb), F32), pltpu.VMEM((k, nb), F32)],
        ),
        out_shape=jax.ShapeDtypeStruct((FB, per), F32),
        compiler_params=params(),
        cost_estimate=SHORT,
        name="base",
    )(at, *operands)


def last_kernel(each, at_ref, base_ref, middle_ref, *refs):
    *refs, out_ref, total_ref = refs
    total_ref[...] = base_ref[...]
    total = functools.reduce(jnp.add, [ref[...] for ref in refs])
    middle = middle_ref[...]
    pieces = [middle[k : k + each] for k in range(0, middle.shape[0], each)] + [total]
    for slot, piece in enumerate(pieces):
        first = pl.multiple_of(at_ref[2 + slot] * each, each)
        total_ref[pl.ds(first, each), :] += piece
    out_ref[...] = total_ref[...].T


def last(at, held, middle, terms, each):
    per = held.shape[1]
    operands = [held, middle, *terms]
    return pl.pallas_call(
        functools.partial(last_kernel, each),
        grid_spec=pltpu.PrefetchScalarGridSpec(
            num_scalar_prefetch=1,
            grid=(1,),
            in_specs=[whole(x.shape) for x in operands],
            out_specs=whole((per, FB)),
            scratch_shapes=[pltpu.VMEM((FB, per), F32)],
        ),
        out_shape=jax.ShapeDtypeStruct((per, FB), F32),
        compiler_params=params(),
        cost_estimate=SHORT,
        name="last",
    )(at, *operands)


def arrivals(n):
    order = []
    for z in range(n):
        found = [(hops, 0) for hops in range(1, n) if z + hops < n]
        found += [(hops, 1) for hops in range(1, n) if z - hops >= 0]
        order.append(sorted(found))
    return [[order[z][slot] for z in range(n)] for slot in range(n - 1)]


def travel(came, held, n, hops, after):
    if hops > 1:
        held = gate(held, *after, cost=LONG)
        came[(hops - 1, 0)], came[(hops - 1, 1)] = held
    pairs = [
        [(p, p - 1) for p in range(1, n - hops + 1)],
        [(p, p + 1) for p in range(hops - 1, n - 1)],
    ]
    held = [lax.ppermute(held[d], "narrow", pairs[d]) for d in (0, 1)]
    came[(hops, 0)], came[(hops, 1)] = held
    return held


def options(came, places, z):
    choices = sorted(set(places))
    which = jnp.int32(0)
    for p, place in enumerate(places):
        which = jnp.where(z == p, choices.index(place), which)
    return [came[choice] for choice in choices], which


def source(places, z):
    value = jnp.int32(0)
    for p, (hops, direction) in enumerate(places):
        value = jnp.where(z == p, p - hops if direction else p + hops, value)
    return value


def swap(x, wide, distance):
    return lax.ppermute(x, "wide", [(i, i ^ distance) for i in range(wide)])


def scatter_terms(even, odd, wide, after):
    (other,) = gate([swap(odd, wide, 1)], after)
    sums = [even[h] + other[h] for h in range(wide // 2)]
    return [sums[0]] + [swap(sums[h], wide, 2 * h) for h in range(1, wide // 2)]


def collect(x, wide, after=()):
    pieces = [swap(x, wide, 2 * h) for h in range(1, wide // 2)]
    if after:
        (x,) = gate([x], *after)
    even = jnp.stack([x, *pieces])
    return even, swap(even, wide, 1)


def on_device(vectors, reflectors, triangle, energies):
    n = lax.axis_size("narrow")
    wide = lax.axis_size("wide")
    z = lax.axis_index("narrow").astype(jnp.int32)
    me = lax.axis_index("wide").astype(jnp.int32).reshape(1)
    each = FB // n
    rows, columns = vectors.shape
    nb = reflectors.shape[1]
    k = nb + each
    per = columns // wide
    e_row = energies.reshape(1, rows)

    own = energies[:, None] * vectors[:, OFF : OFF + each]
    came = {}
    held = travel(came, [own, own], n, 1, [])
    table = arrivals(n)
    at = jnp.stack([me[0], z] + [source(places, z) for places in table])

    ride = k // wide if per == nb and k % (8 * wide) == 0 else 0
    even, odd, sums, small = project(me, vectors, reflectors, e_row, own, wide, ride)
    if n > 2:
        held = travel(came, held, n, 2, [small])
    ready = lax.psum_scatter(sums, "wide", scatter_dimension=0)

    projected = functools.reduce(jnp.add, scatter_terms(even, odd, wide, came[(1, 0)]))
    highest = lax.Precision.HIGHEST
    coefficients = jnp.dot(triangle, projected[:nb], precision=highest)
    payload = coefficients
    if ride:
        payload = jnp.concatenate([coefficients, projected[nb:]], axis=0)
    c = collect(payload, wide)

    of = next(x for x in range(10, rows) if rows % (16 * x) == 0)
    updated, token = update(me, vectors, reflectors, c, 0, of * 2 // 5, of, [], [])
    for hops in range(3, n):
        held = travel(came, held, n, hops, [token])
    updated, token = update(
        me, vectors, reflectors, c, of * 2 // 5, of - of * 2 // 5, of, [came[(n - 2, 0)]], [updated]
    )

    slots = [options(came, places, z) for places in table]
    (middle,) = late(me, updated, slots[:-1], token, wide, True)
    middle_sum = lax.psum_scatter(middle, "wide", scatter_dimension=0)
    mine = own_columns(me, c, middle, nb, each)
    (ready,) = gate([ready], middle, mine)
    even, odd = late(me, updated, slots[-1:], ready, wide, False)
    coef = [mine] + [
        lax.ppermute(mine, "narrow", [(p, (p + s) % n) for p in range(n)]) for s in range(1, n)
    ]
    tail = scatter_terms(even, odd, wide, mine)
    (ready,) = gate([ready], tail[0])
    small = c if ride else [lax.psum(small, "wide")]
    base_block = base(at, ready, coefficients, coef, small, n, each, ride)
    return (updated, last(at, base_block, middle_sum, tail, each))


def solution(mesh):
    return jax.shard_map(
        on_device,
        mesh=mesh,
        in_specs=(P("wide", "narrow"), P("wide", None), P(), P("wide")),
        out_specs=(P("wide", "narrow"), P(("narrow", "wide"), None)),
        check_vma=False,
    )
```

```python
import functools

import jax
import jax.numpy as jnp
from jax import lax
from jax.experimental import pallas as pl
from jax.experimental.pallas import tpu as pltpu
from jax.sharding import PartitionSpec as P

FB = 512
OFF = 256
VMEM = 60 * 1024 * 1024
LESS = 29 * 1024 * 1024

F32 = jnp.float32
BF16 = jnp.bfloat16
LONG = pl.CostEstimate(flops=10**11, bytes_accessed=1024, transcendentals=0)
SHORT = pl.CostEstimate(flops=1024, bytes_accessed=1024, transcendentals=0)


def split(x):
    high = x.astype(BF16)
    return high, (x - high.astype(F32)).astype(BF16)


def mul(left, right):
    return jnp.dot(left, right, preferred_element_type=F32)


def three(left, right):
    (lh, ll), (rh, rl) = left, right
    return mul(lh, rh) + mul(ll, rh) + mul(lh, rl)


def stacked(both, high, right):
    rh, rl = right
    m = high.shape[0]
    top = mul(both, rh)
    return top[:m] + top[m:] + mul(high, rl)


def params(limit=VMEM):
    return pltpu.CompilerParams(
        dimension_semantics=("arbitrary",), vmem_limit_bytes=limit
    )


def width(columns, wide):
    return 256 if columns % 256 == 0 and 256 % (columns // wide) == 0 else columns // wide


def whole(shape):
    return pl.BlockSpec(shape, lambda j, *_: (0,) * len(shape), pipeline_mode=pl.Buffered(1))


ANY = pl.BlockSpec(memory_space=pl.ANY)


def gate_kernel(*refs):
    del refs


def gate(held, *others, cost=SHORT):
    count = len(held)
    return pl.pallas_call(
        gate_kernel,
        in_specs=[ANY] * (count + len(others)),
        out_specs=[ANY] * count,
        out_shape=[jax.ShapeDtypeStruct(x.shape, x.dtype) for x in held],
        input_output_aliases={k: k for k in range(count)},
        compiler_params=pltpu.CompilerParams(vmem_limit_bytes=2**20),
        cost_estimate=cost,
        name="gate",
    )(*held, *others)


def place(value, index, even_ref, odd_ref, first):
    half = index // 2
    rows = value.shape[0]

    @pl.when(index % 2 == 0)
    def _():
        even_ref[half, first : first + rows] = value

    @pl.when(index % 2 == 1)
    def _():
        odd_ref[half, first : first + rows] = value


def take(index, even_ref, odd_ref, rows):
    half = index // 2
    return jnp.where(index % 2 == 0, even_ref[half, rows], odd_ref[half, rows])


def project_kernel(per, wide, me_ref, v_ref, r_ref, e_ref, x_ref, even_ref, odd_ref, sums_ref, small_ref, both_ref):
    j = pl.program_id(0)
    nb = r_ref.shape[1]
    m = both_ref.shape[0] // 2
    k = m - nb
    ride = even_ref.shape[1] - nb

    @pl.when(j == 0)
    def _():
        turned = r_ref[...].T
        first = 0
        for part in (turned, turned * e_ref[...], x_ref[...].T):
            end = first + part.shape[0]
            both_ref[first:end], both_ref[m + first : m + end] = split(part)
            first = end
        small = three((both_ref[nb:m], both_ref[m + nb :]), split(r_ref[...]))
        small_ref[...] = small
        if ride:
            for w in range(wide):
                share = small[w * ride : (w + 1) * ride]
                place(share, w ^ me_ref[0], even_ref, odd_ref, nb)

    value = stacked(both_ref[...], both_ref[:m], split(v_ref[...]))
    count = v_ref.shape[1] // per
    for g in range(count):
        part = value[:, g * per : (g + 1) * per]
        place(part[:nb], (j * count + g) ^ me_ref[0], even_ref, odd_ref, 0)
        sums_ref[g] = part[nb:]


def project(me, vectors, reflectors, e_row, block, wide, ride):
    rows, columns = vectors.shape
    nb = reflectors.shape[1]
    k = nb + block.shape[1]
    per = columns // wide
    step = width(columns, wide)
    shapes = [(wide // 2, nb + ride, per)] * 2 + [(wide, k, per), (k, nb)]
    specs = [whole(x) for x in shapes]
    specs[2] = pl.BlockSpec((step // per, k, per), lambda j, *_: (j, 0, 0))
    return pl.pallas_call(
        functools.partial(project_kernel, per, wide),
        grid_spec=pltpu.PrefetchScalarGridSpec(
            num_scalar_prefetch=1,
            grid=(columns // step,),
            in_specs=[pl.BlockSpec((rows, step), lambda j, *_: (0, j))]
            + [whole(x) for x in ((rows, nb), (1, rows), block.shape)],
            out_specs=specs,
            scratch_shapes=[pltpu.VMEM((2 * (nb + k), rows), BF16)],
        ),
        out_shape=[jax.ShapeDtypeStruct(x, F32) for x in shapes],
        compiler_params=params(),
        cost_estimate=SHORT,
        name="project",
    )(me, vectors, reflectors, e_row, block)


def update_kernel(me_ref, v_ref, r_ref, even_ref, odd_ref, *refs):
    out_ref, token_ref, right_ref = refs[-3:]
    nb = r_ref.shape[1]
    per = even_ref.shape[2]

    @pl.when(pl.program_id(0) == 0)
    def _():
        token_ref[...] = jnp.zeros_like(token_ref)
        for w in range(2 * even_ref.shape[0]):
            high, low = split(take(w ^ me_ref[0], even_ref, odd_ref, slice(0, nb)))
            here = slice(w * per, (w + 1) * per)
            right_ref[:nb, here] = high
            right_ref[nb : 2 * nb, here] = high
            right_ref[2 * nb :, here] = low

    high, low = split(r_ref[...])
    left = jnp.concatenate([high, low, high], axis=1)
    out_ref[...] = v_ref[...] - mul(left, right_ref[...])


def update(me, vectors, reflectors, c, first, count, of, others, before):
    rows, columns = vectors.shape
    nb = reflectors.shape[1]
    operands = [me, vectors, reflectors, *c, *others, *before]
    return pl.pallas_call(
        update_kernel,
        grid_spec=pltpu.PrefetchScalarGridSpec(
            num_scalar_prefetch=1,
            grid=(count,),
            in_specs=[
                pl.BlockSpec((rows // of, columns), lambda j, *_: (j + first, 0)),
                pl.BlockSpec((rows // of, nb), lambda j, *_: (j + first, 0)),
            ]
            + [whole(x.shape) for x in c]
            + [ANY] * (len(operands) - 5),
            out_specs=[
                pl.BlockSpec((rows // of, columns), lambda j, *_: (j + first, 0)),
                whole((8, 128)),
            ],
            scratch_shapes=[pltpu.VMEM((3 * nb, columns), BF16)],
        ),
        out_shape=[
            jax.ShapeDtypeStruct(vectors.shape, F32),
            jax.ShapeDtypeStruct((8, 128), F32),
        ],
        input_output_aliases={len(operands) - 1: 0} if before else {},
        compiler_params=params(),
        cost_estimate=SHORT,
        name="update",
    )(*operands)


def late_kernel(per, counts, n_after, at_ref, u_ref, *refs):
    refs = refs[n_after:]
    *refs, both_ref, block_ref, sem_ref = refs
    outs = refs[sum(counts) :]
    j = pl.program_id(0)
    m = both_ref.shape[0] // 2
    each = block_ref.shape[2]

    @pl.when(j == 0)
    def _():
        first = 0
        for s, count in enumerate(counts):
            for k, ref in enumerate(refs[first : first + count]):

                @pl.when(at_ref[1 + s] == k)
                def _(ref=ref, s=s):
                    pltpu.make_async_copy(ref, block_ref.at[s], sem_ref.at[s]).start()

            first += count
        for s in range(len(counts)):
            pltpu.make_async_copy(block_ref.at[s], block_ref.at[s], sem_ref.at[s]).wait()
            high, low = split(block_ref[s].T)
            both_ref[s * each : (s + 1) * each] = high
            both_ref[m + s * each : m + (s + 1) * each] = low

    value = stacked(both_ref[...], both_ref[:m], split(u_ref[...]))
    count = u_ref.shape[1] // per
    for g in range(count):
        part = value[:, g * per : (g + 1) * per]
        if len(outs) == 2:
            place(part, (j * count + g) ^ at_ref[0], *outs, 0)
        else:
            outs[0][g] = part


def late(me, updated, slots, after, wide, ordered):
    rows, columns = updated.shape
    per = columns // wide
    step = width(columns, wide)
    flat = [x for choices, _ in slots for x in choices]
    counts = [len(choices) for choices, _ in slots]
    each = flat[0].shape[1]
    m = each * len(slots)
    at = jnp.stack([me[0]] + [which.astype(jnp.int32) for _, which in slots])
    if ordered:
        shapes = [(wide, m, per)]
        specs = [pl.BlockSpec((step // per, m, per), lambda j, *_: (j, 0, 0))]
    else:
        shapes = [(wide // 2, m, per)] * 2
        specs = [whole(x) for x in shapes]
    return pl.pallas_call(
        functools.partial(late_kernel, per, counts, len(after)),
        grid_spec=pltpu.PrefetchScalarGridSpec(
            num_scalar_prefetch=1,
            grid=(columns // step,),
            in_specs=[pl.BlockSpec((rows, step), lambda j, *_: (0, j))] + [ANY] * (len(after) + len(flat)),
            out_specs=specs,
            scratch_shapes=[
                pltpu.VMEM((2 * m, rows), BF16),
                pltpu.VMEM((len(slots), rows, each), F32),
                pltpu.SemaphoreType.DMA((len(slots),)),
            ],
        ),
        out_shape=[jax.ShapeDtypeStruct(x, F32) for x in shapes],
        compiler_params=params(LESS),
        cost_estimate=SHORT if ordered else LONG,
        name="late",
    )(at, updated, *after, *flat)


def own_kernel(me_ref, even_ref, odd_ref, after_ref, out_ref):
    each, nb = out_ref.shape
    per = even_ref.shape[2]
    block = jnp.where(
        ((OFF // per) ^ me_ref[0]) % 2 == 0, even_ref[0, :nb], odd_ref[0, :nb]
    )
    out_ref[...] = block[:, OFF % per : OFF % per + each].T


def own_columns(me, c, after, nb, each):
    per = c[0].shape[2]
    block = pl.BlockSpec(
        (1, *c[0].shape[1:]), lambda j, me_ref: (((OFF // per) ^ me_ref[0]) // 2, 0, 0)
    )
    return pl.pallas_call(
        own_kernel,
        grid_spec=pltpu.PrefetchScalarGridSpec(
            num_scalar_prefetch=1,
            grid=(1,),
            in_specs=[block, block, ANY],
            out_specs=whole((each, nb)),
        ),
        out_shape=jax.ShapeDtypeStruct((each, nb), F32),
        compiler_params=params(),
        cost_estimate=SHORT,
        name="own_columns",
    )(me, *c, after)


def base_kernel(n, each, ride, at_ref, ready_ref, c_ref, *refs):
    *refs, out_ref, coef_ref, small_ref = refs
    me, z = at_ref[0], at_ref[1]
    nb = c_ref.shape[0]
    k = small_ref.shape[0]
    for s in range(n):
        first = pl.multiple_of((z + n - s) % n * each, each)
        coef_ref[pl.ds(first, each), :] = refs[s][...]
    if ride:
        wide = 2 * refs[n].shape[0]
        for w in range(wide):
            small_ref[w * (k // wide) : (w + 1) * (k // wide)] = take(
                w ^ me, *refs[n:], slice(nb, nb + k // wide)
            )
    else:
        small_ref[...] = refs[n][...]
    corrected = ready_ref[...] - three(split(small_ref[...]), split(c_ref[...]))
    out_ref[...] = -three(split(coef_ref[...]), split(corrected[:nb]))
    out_ref[pl.ds(pl.multiple_of(z * each, each), each), :] += corrected[nb:]


def base(at, ready, c, coef, small, n, each, ride):
    operands = [ready, c, *coef, *small]
    k, per = ready.shape
    nb = c.shape[0]
    return pl.pallas_call(
        functools.partial(base_kernel, n, each, ride),
        grid_spec=pltpu.PrefetchScalarGridSpec(
            num_scalar_prefetch=1,
            grid=(1,),
            in_specs=[whole(x.shape) for x in operands],
            out_specs=whole((FB, per)),
            scratch_shapes=[pltpu.VMEM((FB, nb), F32), pltpu.VMEM((k, nb), F32)],
        ),
        out_shape=jax.ShapeDtypeStruct((FB, per), F32),
        compiler_params=params(),
        cost_estimate=SHORT,
        name="base",
    )(at, *operands)


def last_kernel(each, at_ref, base_ref, middle_ref, *refs):
    *refs, out_ref, total_ref = refs
    total_ref[...] = base_ref[...]
    total = functools.reduce(jnp.add, [ref[...] for ref in refs])
    middle = middle_ref[...]
    pieces = [middle[k : k + each] for k in range(0, middle.shape[0], each)] + [total]
    for slot, piece in enumerate(pieces):
        first = pl.multiple_of(at_ref[2 + slot] * each, each)
        total_ref[pl.ds(first, each), :] += piece
    out_ref[...] = total_ref[...].T


def last(at, held, middle, terms, each):
    per = held.shape[1]
    operands = [held, middle, *terms]
    return pl.pallas_call(
        functools.partial(last_kernel, each),
        grid_spec=pltpu.PrefetchScalarGridSpec(
            num_scalar_prefetch=1,
            grid=(1,),
            in_specs=[whole(x.shape) for x in operands],
            out_specs=whole((per, FB)),
            scratch_shapes=[pltpu.VMEM((FB, per), F32)],
        ),
        out_shape=jax.ShapeDtypeStruct((per, FB), F32),
        compiler_params=params(),
        cost_estimate=SHORT,
        name="last",
    )(at, *operands)


def arrivals(n):
    order = []
    for z in range(n):
        found = [(hops, 0) for hops in range(1, n) if z + hops < n]
        found += [(hops, 1) for hops in range(1, n) if z - hops >= 0]
        order.append(sorted(found))
    return [[order[z][slot] for z in range(n)] for slot in range(n - 1)]


def travel(came, held, n, hops, after):
    if hops > 1:
        held = gate(held, *after, cost=LONG)
        came[(hops - 1, 0)], came[(hops - 1, 1)] = held
    pairs = [
        [(p, p - 1) for p in range(1, n - hops + 1)],
        [(p, p + 1) for p in range(hops - 1, n - 1)],
    ]
    held = [lax.ppermute(held[d], "narrow", pairs[d]) for d in (0, 1)]
    came[(hops, 0)], came[(hops, 1)] = held
    return held


def options(came, places, z):
    choices = sorted(set(places))
    which = jnp.int32(0)
    for p, place in enumerate(places):
        which = jnp.where(z == p, choices.index(place), which)
    return [came[choice] for choice in choices], which


def source(places, z):
    value = jnp.int32(0)
    for p, (hops, direction) in enumerate(places):
        value = jnp.where(z == p, p - hops if direction else p + hops, value)
    return value


def swap(x, wide, distance):
    return lax.ppermute(x, "wide", [(i, i ^ distance) for i in range(wide)])


def scatter_terms(even, odd, wide, after):
    (other,) = gate([swap(odd, wide, 1)], after)
    sums = [even[h] + other[h] for h in range(wide // 2)]
    return [sums[0]] + [swap(sums[h], wide, 2 * h) for h in range(1, wide // 2)]


def collect(x, wide, after=()):
    pieces = [swap(x, wide, 2 * h) for h in range(1, wide // 2)]
    if after:
        (x,) = gate([x], *after)
    even = jnp.stack([x, *pieces])
    return even, swap(even, wide, 1)


def on_device(vectors, reflectors, triangle, energies):
    n = lax.axis_size("narrow")
    wide = lax.axis_size("wide")
    z = lax.axis_index("narrow").astype(jnp.int32)
    me = lax.axis_index("wide").astype(jnp.int32).reshape(1)
    each = FB // n
    rows, columns = vectors.shape
    nb = reflectors.shape[1]
    k = nb + each
    per = columns // wide
    e_row = energies.reshape(1, rows)

    own = energies[:, None] * vectors[:, OFF : OFF + each]
    came = {}
    held = travel(came, [own, own], n, 1, [])
    table = arrivals(n)
    at = jnp.stack([me[0], z] + [source(places, z) for places in table])

    ride = k // wide if per == nb and k % (8 * wide) == 0 else 0
    even, odd, sums, small = project(me, vectors, reflectors, e_row, own, wide, ride)
    if n > 2:
        held = travel(came, held, n, 2, [small])
    ready = lax.psum_scatter(sums, "wide", scatter_dimension=0)

    projected = functools.reduce(jnp.add, scatter_terms(even, odd, wide, came[(1, 0)]))
    highest = lax.Precision.HIGHEST
    coefficients = jnp.dot(triangle, projected[:nb], precision=highest)
    payload = coefficients
    if ride:
        payload = jnp.concatenate([coefficients, projected[nb:]], axis=0)
    c = collect(payload, wide)

    of = next(x for x in range(10, rows) if rows % (16 * x) == 0)
    updated, token = update(me, vectors, reflectors, c, 0, of * 2 // 5, of, [], [])
    for hops in range(3, n):
        held = travel(came, held, n, hops, [token])
    updated, token = update(
        me, vectors, reflectors, c, of * 2 // 5, of - of * 2 // 5, of, [came[(n - 2, 0)]], [updated]
    )

    slots = [options(came, places, z) for places in table]
    (middle,) = late(me, updated, slots[:-1], [token], wide, True)
    middle_sum = lax.psum_scatter(middle, "wide", scatter_dimension=0)
    mine = own_columns(me, c, middle, nb, each)
    even, odd = late(me, updated, slots[-1:], [ready, mine], wide, False)
    coef = [mine] + [
        lax.ppermute(mine, "narrow", [(p, (p + s) % n) for p in range(n)]) for s in range(1, n)
    ]
    tail = scatter_terms(even, odd, wide, mine)
    (ready,) = gate([ready], tail[0])
    small = c if ride else [lax.psum(small, "wide")]
    base_block = base(at, ready, coefficients, coef, small, n, each, ride)
    return (updated, last(at, base_block, middle_sum, tail, each))


def solution(mesh):
    return jax.shard_map(
        on_device,
        mesh=mesh,
        in_specs=(P("wide", "narrow"), P("wide", None), P(), P("wide")),
        out_specs=(P("wide", "narrow"), P(("narrow", "wide"), None)),
        check_vma=False,
    )
```
